256 devices in a mesh: blk: 64 (over z, y, x_hi), rep: 4 (over x_lo, core).
Axes of the slice: x: 4 (x_hi: 2, x_lo: 2; x = x_hi * 2 + x_lo), y: 4, z: 8, core: 2. Of those that a mesh axis runs over, the one named last changes fastest.
Arguments:
- cotangent: bfloat16 [65536, 256], P('blk'), may hold values from -6 to 6
- features: bfloat16 [65536, 768], P('blk', 'rep'), may hold values from -6 to 6
- weight: bfloat16 [768, 256], P('rep'), may hold values from -0.375 to 0.375
- heat_time: float32 [1], replicated, may hold values from 0.5 to 4
- tile_values: bfloat16 [4096, 256, 256], P(('blk', 'rep')), may hold values from -0.09375 to 0.09375
- tile_row: int32 [4096], P(('blk', 'rep')), may hold values from 0 to 255, as said below
- tile_col: int32 [4096], P(('blk', 'rep')), may hold values from 0 to 255, as said below
- section_offsets: int32 [4352], P(('blk', 'rep')), may hold values from 0 to 16, as said below
Outputs:
- grad_weight: float32 [768, 256], P('rep')
- grad_features: bfloat16 [65536, 768], P('blk', 'rep')
The draws below stay inside these ranges and needn't reach their ends.
Inputs may be any that keep to these rules, and one draw needn't show every extreme that they name: `tile_row`: for the device at blk index d and rep index r, the live slots between its offsets m and m + 1 (m = 0 to 15) name row tiles of node block (d - r - 4 * m) mod 64, that is row tiles (4 blocks further back for each m) of that block's 4 tiles; slots past the last offset are unused. `tile_col`: every live slot of the device at blk index d names a column tile of node block d. `section_offsets`: each device's 16 + 1 offsets start at 0 and never fall; the last one is its count of live slots, which differs between devices, and is 16 on at least one device.
All inputs are finite; a program needn't handle non-finite values.
Results may differ from the reference program's by a relative error of at most 0.0053.
Values may be sent and summed in bfloat16 or wider, within the bound.
A program may use at most 64 MiB of HBM per device.

```python
import jax
import jax.numpy as jnp
from jax import lax

FEATS = 768
HID = 256
TILE = 256
ROWB = 4
TPD = 16
BLOCKS = 64
REPS = 4
SPD = 16
NTILES = 256
NODES = 65536


def tile_layout(key):
    groups = BLOCKS * REPS
    key_total, key_full, key_cuts, key_rows, key_cols = jax.random.split(key, 5)
    totals = jax.random.randint(key_total, (groups,), TPD // 3, TPD + 1).astype(jnp.int32)
    fullest = jax.random.randint(key_full, (), 0, groups)
    totals = jnp.where(jnp.arange(groups) == fullest, TPD, totals).astype(jnp.int32)
    cuts = jax.random.randint(key_cuts, (groups, SPD - 1), 0, totals[:, None] + 1).astype(jnp.int32)
    cuts = jnp.sort(cuts, axis=1)
    offsets = jnp.concatenate([jnp.zeros((groups, 1), jnp.int32), cuts, totals[:, None]], axis=1)
    slot_index = jnp.arange(TPD, dtype=jnp.int32)
    section_idx = jnp.sum((slot_index[None, :, None] >= offsets[:, None, 1:SPD]).astype(jnp.int32), axis=2)
    device_blk = jnp.arange(groups, dtype=jnp.int32) // REPS
    device_rep = jnp.arange(groups, dtype=jnp.int32) % REPS
    source = (device_blk[:, None] - device_rep[:, None] - REPS * section_idx) % BLOCKS
    rows_pick = jax.random.randint(key_rows, (groups, TPD), 0, ROWB).astype(jnp.int32)
    cols_pick = jax.random.randint(key_cols, (groups, TPD), 0, ROWB).astype(jnp.int32)
    tile_rows = source * ROWB + rows_pick
    tile_cols = device_blk[:, None] * ROWB + cols_pick
    return (offsets.reshape(-1), tile_rows.reshape(-1).astype(jnp.int32), tile_cols.reshape(-1).astype(jnp.int32))


def draw_section_offsets(key, part):
    return tile_layout(key)[0]


def draw_tile_row(key, part):
    return tile_layout(key)[1]


def draw_tile_col(key, part):
    return tile_layout(key)[2]


def steps_of(stream_key, extent, cuts, low, high):
    level = 1.0
    for position, blocks in cuts:
        heights = jax.random.uniform(jax.random.fold_in(jax.random.fold_in(stream_key, 6), position), (blocks,), jnp.float32, low / len(cuts), high / len(cuts))
        level = level * jnp.repeat(jnp.exp(heights), extent[position] // blocks).reshape((-1,) + (1,) * (len(extent) - 1 - position))
    return level


def normal_values(own_key, dims, deviation, most, cuts=(), held_as=jnp.bfloat16):
    array = jax.random.normal(own_key, dims, jnp.float32) * deviation
    if len(cuts) > 0:
        array = steps_of(own_key, dims, cuts, -0.22, 0.18) * array
    return jnp.clip(array, min=-most, max=most).astype(held_as)


def setup_inputs(seed: int = 0) -> dict:
    key_list = jax.random.split(jax.random.key(seed), 9)
    cotangent = normal_values(key_list[0], (NODES, HID), 1.0, 6.0, ((0, 64),))
    features = normal_values(key_list[1], (NODES, FEATS), 1.0, 6.0, ((0, 64), (1, 4)))
    weight = normal_values(key_list[2], (FEATS, HID), HID ** -0.5, 0.375, ((0, 4),))
    heat_time = jnp.clip(jax.random.uniform(key_list[3], (1,), jnp.float32, 0.5, 4.0), 0.5, 4.0)
    tile_values = normal_values(key_list[4], (BLOCKS * REPS * TPD, TILE, TILE), (TILE * TPD) ** -0.5, 0.09375, ((0, 256),))
    tile_row = draw_tile_row(jax.random.fold_in(key_list[8], 71), 0)
    tile_col = draw_tile_col(jax.random.fold_in(key_list[8], 71), 0)
    section_offsets = draw_section_offsets(jax.random.fold_in(key_list[8], 71), 0)
    return {"cotangent": cotangent, "features": features, "weight": weight, "heat_time": heat_time, "tile_values": tile_values, "tile_row": tile_row, "tile_col": tile_col, "section_offsets": section_offsets}


def taylor_coef(heat_time):
    tvalue = heat_time[0]
    taylor = jnp.stack([jnp.ones((), jnp.float32), tvalue, tvalue * tvalue / 2.0])
    return taylor / jnp.sum(taylor)

def adjoint(field, tile_values, tile_row, tile_col, alive_mask):
    blocks = field.reshape(NTILES, TILE, HID)
    tile_groups = tile_values.reshape(BLOCKS * REPS, TPD, TILE, TILE)
    row_groups = tile_row.reshape(BLOCKS * REPS, TPD)
    col_groups = tile_col.reshape(BLOCKS * REPS, TPD)

    def one_group(totals, pieces):
        group_tiles, group_rows, group_cols, group_alive = pieces
        picked = blocks[group_rows].astype(jnp.float32)
        contrib = jnp.einsum('kab,kac->kbc', group_tiles.astype(jnp.float32), picked)
        contrib = contrib * group_alive[:, None, None]
        return (totals.at[group_cols].add(contrib), None)
    start_totals = jnp.zeros((NTILES, TILE, HID), jnp.float32)
    totals, _ = lax.scan(one_group, start_totals, (tile_groups, row_groups, col_groups, alive_mask))
    return totals.reshape(NODES, HID)

def reference(cotangent, features, weight, heat_time, tile_values, tile_row, tile_col, section_offsets):
    offset_table = section_offsets.reshape(BLOCKS * REPS, SPD + 1)
    slot_index = jnp.arange(TPD, dtype=jnp.int32)
    alive_mask = (slot_index[None, :] < offset_table[:, SPD:SPD + 1]).astype(jnp.float32)
    coef = taylor_coef(heat_time)
    first = adjoint(cotangent, tile_values, tile_row, tile_col, alive_mask).astype(jnp.bfloat16)
    second = adjoint(first, tile_values, tile_row, tile_col, alive_mask)
    combined = coef[0] * cotangent.astype(jnp.float32) + coef[1] * first.astype(jnp.float32) + coef[2] * second
    combined = combined.astype(jnp.bfloat16)
    grad_weight = jnp.dot(features.T, combined, preferred_element_type=jnp.float32) / jnp.sqrt(jnp.float32(NODES))
    grad_features = jnp.dot(combined, weight.T, preferred_element_type=jnp.float32).astype(jnp.bfloat16)
    return (grad_weight, grad_features)
```

```python
import functools
import math

import jax
import jax.numpy as jnp
from jax import lax
from jax.experimental import pallas as pl
from jax.experimental.pallas import tpu as pltpu
from jax.sharding import PartitionSpec as P

MESH = pl.DeviceIdType.MESH
T = 256
WIDE = 192
RELAY = 64


def xor(a, b):
    return a + b - 2 * a * b


def kernel(
    rows_ref, cols_ref, offs_ref, heat_ref, cot_ref, feat_ref, weight_ref, tiles_hbm,
    gw_ref, gf_ref,
    field0, field1, tiles, own, acc, core_in, chip_out, chip_in, qsum, comb, gwp, g1, s1, g2, s2, gfin,
    tile_sem, own_sem, relay_sem, gy_sem, g0_sem, grest_sem, r1_sem, send_sem, self_sem,
    ex_send, ex_recv, cb_send, cb_recv, gw_send, gw_recv,
):
    blk = lax.axis_index("blk")
    rep = lax.axis_index("rep")
    z = blk // 8
    y = (blk // 2) % 4
    xh = blk % 2
    xl = rep // 2
    c = rep % 2
    n = xor(c, xh)
    hx = xor(xl, xh)
    own_tile = hx * 2 + c

    def dev(xh_, xl_, y_, z_, c_):
        return (z_ * 8 + y_ * 2 + xh_, xl_ * 2 + c_)

    def delta2(xh_, xl_):
        return (1 - xh_) * (3 - xl_) + xh_ * xl_

    relay_one = dev(xh, xl, (y + 1 - xl) % 4, z, 0)
    relay_two = dev(1 - xh, xl, (y + delta2(xh, xl)) % 4, z, 1)
    one_is_self = xl * (1 - c)

    yr = ((1 - c) * (y - 1 + xl) + c * (y - delta2(1 - xh, xl)) + 4) % 4
    hr = xor(xl, n)
    src_xh = xor(xh, c)
    ey = 2 * hx - 1
    yc = ((1 - c) * (y - ey - 1 + xl) + c * (y - ey - delta2(1 - xh, xl)) + 8) % 4

    z_up = dev(xh, xl, y, (z + 1) % 8, c)
    z_dn = dev(xh, xl, y, (z + 7) % 8, c)
    y_chain = dev(xh, xl, (y + ey + 4) % 4, z, c)
    y_other = dev(xh, xl, (y - ey + 4) % 4, z, c)
    x_near = dev(xh, 1 - xl, y, z, c)
    x_far = dev(1 - xh, 1 - xl, y, z, 1 - c)
    sibling = dev(xh, xl, y, z, 1 - c)

    barrier = pltpu.get_barrier_semaphore()

    def greet(device):
        pl.semaphore_signal(barrier, inc=1, device_id=device, device_id_type=MESH)

    src_y = yr
    src_first = dev(src_xh, xl, src_y, z, 0)
    src_second = dev(src_xh, xl, src_y, z, 1)

    @pl.when(one_is_self == 0)
    def _():
        greet(src_first)

    greet(src_second)
    for device in (y_chain, y_other, x_near, x_far, sibling):
        greet(device)
    for step in range(1, 8):
        greet(dev(xh, xl, y, (z + step) % 8, c))
    for step in range(1, 8):
        place = (y * 2 + xh + step) % 8
        greet(dev(place % 2, xl, place // 2, z, c))
    pl.semaphore_wait(barrier, 21 - one_is_self)

    pltpu.make_async_copy(tiles_hbm, tiles, tile_sem).start()
    own[0] = cot_ref[pl.ds(pl.multiple_of(own_tile * T, T), T), :]

    def send(src, dst, ssem, rsem, device):
        pltpu.make_async_remote_copy(
            src_ref=src, dst_ref=dst, send_sem=ssem, recv_sem=rsem, device_id=device, device_id_type=MESH
        ).start()

    def drain(ref, sem):
        pltpu.make_async_copy(ref, ref, sem).wait()

    wide = pl.ds(0, WIDE)
    thin = pl.ds(WIDE, T - WIDE)

    def propagate(p, buf):

        def zp(i):
            return (z + (0, 7, 6, 5, 1, 2, 3, 4)[i]) % 8

        def relay(i):
            return buf.at[pl.ds(RELAY + zp(i) * 2, 2)]

        def spot(i, ysrc, half):
            return (zp(i) * 2 + ysrc // 2) * 4 + half * 2

        mine = own.at[p]
        slot = RELAY + z * 2 + c

        @pl.when(one_is_self == 1)
        def _():
            pltpu.make_async_copy(mine, buf.at[slot], relay_sem.at[p, 0]).start()

        @pl.when(one_is_self == 0)
        def _():
            send(mine, buf.at[slot], self_sem.at[p], relay_sem.at[p, 0], relay_one)

        send(mine, buf.at[slot], send_sem.at[p, 0], relay_sem.at[p, 0], relay_two)

        def along_z(i, up, index):
            tiles_of = pl.ds(RELAY + zp(i) * 2, 2)
            if index == 7 and up:
                tiles_of = pl.ds(RELAY + zp(i) * 2, 1)
            elif index == 7:
                tiles_of = pl.ds(RELAY + zp(i) * 2 + 1, 1)
            sem = relay_sem.at[p, 8 if index == 7 and not up else index]
            part = buf.at[tiles_of, wide]
            send(part, part, send_sem.at[p, 1], sem, z_up if up else z_dn)

        def over_plane(i):
            rows = pl.ds(0, T) if i == 0 else wide
            ssem = send_sem.at[p, 2 if i == 0 else 3]
            rest = g0_sem.at[p] if i == 0 else grest_sem.at[p]
            src = buf.at[pl.ds(RELAY + zp(i) * 2, 2), rows]
            dst = buf.at[pl.ds(spot(i, yr, hr), 2), rows]
            send(src, dst, ssem, gy_sem.at[p, i], y_chain)
            send(src, dst, ssem, rest, y_other)
            send(src, dst, ssem, rest, x_near)

        def far(i):
            rows = pl.ds(0, T) if i == 0 else wide
            ssem = send_sem.at[p, 2 if i == 0 else 3]
            rest = g0_sem.at[p] if i == 0 else grest_sem.at[p]
            drain(buf.at[pl.ds(0, 2), rows], gy_sem.at[p, i])
            chained = spot(i, yc, hr)
            src = (1 - n) * (RELAY + zp(i) * 2) + n * chained
            dst = (1 - n) * spot(i, yr, hr) + n * chained
            send(buf.at[pl.ds(src, 2), rows], buf.at[pl.ds(dst, 2), rows], ssem, rest, x_far)

        def thin_z(i, up, index):
            first, count = zp(i) * 8, 8
            if index == 7:
                count = 4
                if not up:
                    first = first + 4
            part = buf.at[pl.ds(first, count), thin]
            sem = r1_sem.at[p, 8 if index == 7 and not up else index]
            send(part, part, send_sem.at[p, 4], sem, z_up if up else z_dn)

        drain(buf.at[pl.ds(0, 2)], relay_sem.at[p, 0])
        along_z(0, True, 1)
        along_z(0, False, 4)
        over_plane(0)
        after_up = {1: 2, 2: 3, 3: 7}
        after_dn = {4: 5, 5: 6, 6: 7}

        def relay_step(s):
            for i, up, follow in ((s, True, after_up[s]), (s + 3, False, after_dn[s + 3])):
                drain(buf.at[pl.ds(0, 2), wide], relay_sem.at[p, i])
                along_z(i, up, follow)
                over_plane(i)

        def thin_step(s):
            for i, up, follow in ((s, True, after_up[s]), (s + 3, False, after_dn[s + 3])):
                drain(buf.at[pl.ds(0, 8), thin], r1_sem.at[p, i])
                thin_z(i, up, follow)

        relay_step(1)
        far(0)
        drain(buf.at[pl.ds(0, 6)], g0_sem.at[p])
        thin_z(0, True, 1)
        thin_z(0, False, 4)
        relay_step(2)
        far(1)
        far(4)
        thin_step(1)
        relay_step(3)
        far(2)
        far(5)
        thin_step(2)
        drain(buf.at[pl.ds(0, 1), wide], relay_sem.at[p, 7])
        drain(buf.at[pl.ds(0, 1), wide], relay_sem.at[p, 8])
        over_plane(7)
        far(3)
        far(6)
        thin_step(3)
        far(7)

        if p == 0:
            drain(tiles, tile_sem)

        acc[...] = jnp.zeros_like(acc)

        drain(buf.at[pl.ds(0, 42), wide], grest_sem.at[p])
        drain(buf.at[pl.ds(0, 4), thin], r1_sem.at[p, 7])
        drain(buf.at[pl.ds(0, 4), thin], r1_sem.at[p, 8])

        live = offs_ref[16]

        def slot_step(k, carry_):
            row = rows_ref[k]
            col = cols_ref[k] % 4
            tile = buf[((row // 16) % 16) * 4 + row % 4]
            term = lax.dot_general(
                tiles[k], tile, (((0,), (0,)), ((), ())), preferred_element_type=jnp.float32
            )
            for t in range(4):
                hit = jnp.logical_and(col == t, k < live)
                acc[t] += jnp.where(hit, term, 0.0)
            return carry_

        lax.fori_loop(0, 16, slot_step, 0)

        for g in range(2):
            send(acc.at[g * 2 + 1 - c], core_in.at[p, g], ex_send.at[p, 0], ex_recv.at[p, 0], sibling)
        drain(core_in.at[p], ex_recv.at[p, 0])
        give = (1 - hx) * 2 + c
        chip_out[p] = (acc[give] + core_in[p, 1 - hx]).astype(jnp.bfloat16)
        send(chip_out.at[p], chip_in.at[p], ex_send.at[p, 1], ex_recv.at[p, 1], x_near)
        drain(chip_in.at[p], ex_recv.at[p, 1])
        qsum[...] = acc[own_tile] + core_in[p, hx] + chip_in[p].astype(jnp.float32)
        own[p + 1] = qsum[...].astype(jnp.bfloat16)

        @pl.when(one_is_self == 0)
        def _():
            drain(mine, self_sem.at[p])

        drain(mine, send_sem.at[p, 0])
        drain(buf.at[pl.ds(0, 14), wide], send_sem.at[p, 1])
        drain(buf.at[pl.ds(0, 8)], send_sem.at[p, 2])
        drain(buf.at[pl.ds(0, 56), wide], send_sem.at[p, 3])
        drain(buf.at[pl.ds(0, 56), thin], send_sem.at[p, 4])
        drain(core_in.at[p], ex_send.at[p, 0])
        drain(chip_in.at[p], ex_send.at[p, 1])

    propagate(0, field0)
    propagate(1, field1)

    tv = jnp.full((1, T), heat_ref[0], jnp.float32)
    total = 1.0 + tv + tv * tv / 2.0
    combined = (
        (1.0 / total) * own[0].astype(jnp.float32)
        + (tv / total) * own[1].astype(jnp.float32)
        + ((tv * tv / 2.0) / total) * qsum[...]
    ).astype(jnp.bfloat16)
    comb[own_tile] = combined
    other_tile = (1 - hx) * 2 + c
    send(comb.at[own_tile], comb.at[own_tile], cb_send.at[0], cb_recv.at[0], x_near)
    send(comb.at[own_tile], comb.at[own_tile], cb_send.at[1], cb_recv.at[1], sibling)
    drain(comb.at[0], cb_recv.at[0])
    send(comb.at[other_tile], comb.at[other_tile], cb_send.at[2], cb_recv.at[2], sibling)
    drain(comb.at[0], cb_recv.at[1])
    drain(comb.at[0], cb_recv.at[2])

    partial = jnp.zeros((192, T), jnp.float32)
    for t in range(4):
        partial += lax.dot_general(
            feat_ref[pl.ds(t * T, T), :], comb[t], (((0,), (0,)), ((), ())), preferred_element_type=jnp.float32
        )
    gwp[...] = partial * (1.0 / 256.0)

    piece = 24
    my_rows = pl.ds(pl.multiple_of(z * piece, 8), piece)
    for step in range(1, 8):
        zt = (z + step) % 8
        send(
            gwp.at[pl.ds(pl.multiple_of(zt * piece, 8), piece)], g1.at[z],
            gw_send.at[0], gw_recv.at[0], dev(xh, xl, y, zt, c),
        )
    g1[z] = gwp[my_rows, :]

    for t in range(4):
        gf_ref[pl.ds(t * T, T), :] = lax.dot_general(
            comb[t], weight_ref[...], (((1,), (1,)), ((), ())), preferred_element_type=jnp.float32
        ).astype(jnp.bfloat16)

    drain(g1.at[pl.ds(0, 7)], gw_recv.at[0])
    s1[...] = functools.reduce(lambda a, b: a + b, [g1[i] for i in range(8)])
    here = y * 2 + xh
    for step in range(1, 8):
        place = (here + step) % 8
        send(s1, g2.at[here], gw_send.at[1], gw_recv.at[1], dev(place % 2, xl, place // 2, z, c))
    g2[here] = s1[...]
    drain(g2.at[pl.ds(0, 7)], gw_recv.at[1])
    s2[...] = functools.reduce(lambda a, b: a + b, [g2[i] for i in range(8)])
    for step in range(1, 8):
        send(s2, gfin.at[z], gw_send.at[2], gw_recv.at[2], dev(xh, xl, y, (z + step) % 8, c))
    gfin[z] = s2[...]
    drain(gfin.at[pl.ds(0, 7)], gw_recv.at[2])
    for i in range(8):
        gw_ref[pl.ds(i * piece, piece), :] = gfin[i]

    for i in range(3):
        drain(comb.at[0], cb_send.at[i])
        drain(g1.at[pl.ds(0, 7)], gw_send.at[i])


def local(cotangent, features, weight, heat_time, tile_values, tile_row, tile_col, section_offsets):
    vmem = pl.BlockSpec(memory_space=pltpu.VMEM)
    smem = pl.BlockSpec(memory_space=pltpu.SMEM)
    f32, bf16 = jnp.float32, jnp.bfloat16
    dma = pltpu.SemaphoreType.DMA
    return pl.pallas_call(
        kernel,
        out_shape=(
            jax.ShapeDtypeStruct((192, T), f32),
            jax.ShapeDtypeStruct((1024, 192), bf16),
        ),
        in_specs=[smem, smem, smem, smem, vmem, vmem, vmem, pl.BlockSpec(memory_space=pl.ANY)],
        out_specs=(vmem, vmem),
        scratch_shapes=[
            pltpu.VMEM((RELAY + 16, T, T), bf16),
            pltpu.VMEM((RELAY + 16, T, T), bf16),
            pltpu.VMEM((16, T, T), bf16),
            pltpu.VMEM((3, T, T), bf16),
            pltpu.VMEM((4, T, T), f32),
            pltpu.VMEM((2, 2, T, T), f32),
            pltpu.VMEM((2, T, T), bf16),
            pltpu.VMEM((2, T, T), bf16),
            pltpu.VMEM((T, T), f32),
            pltpu.VMEM((4, T, T), bf16),
            pltpu.VMEM((192, T), f32),
            pltpu.VMEM((8, 24, T), f32),
            pltpu.VMEM((24, T), f32),
            pltpu.VMEM((8, 24, T), f32),
            pltpu.VMEM((24, T), f32),
            pltpu.VMEM((8, 24, T), f32),
            dma, dma,
            dma((2, 9)),
            dma((2, 8)),
            dma((2,)),
            dma((2,)),
            dma((2, 9)),
            dma((2, 5)),
            dma((2,)),
            dma((2, 2)), dma((2, 2)),
            dma((3,)), dma((3,)),
            dma((3,)), dma((3,)),
        ],
        compiler_params=pltpu.CompilerParams(
            collective_id=0, has_side_effects=True, vmem_limit_bytes=48 << 20
        ),
        cost_estimate=pl.CostEstimate(flops=1_300_000_000, bytes_accessed=4_000_000, transcendentals=0),
        name="diffuse",
    )(tile_row, tile_col, section_offsets, heat_time, cotangent, features, weight, tile_values)


def solution(mesh):
    in_specs = (
        P("blk", None),
        P("blk", "rep"),
        P("rep", None),
        P(),
        P(("blk", "rep"), None, None),
        P(("blk", "rep")),
        P(("blk", "rep")),
        P(("blk", "rep")),
    )
    out_specs = (P("rep", None), P("blk", "rep"))
    return jax.shard_map(local, mesh=mesh, in_specs=in_specs, out_specs=out_specs, check_vma=False)
```

```python
import functools

import jax
import jax.numpy as jnp
from jax import lax
from jax.experimental import pallas as pl
from jax.experimental.pallas import tpu as pltpu
from jax.sharding import PartitionSpec as P

MESH = pl.DeviceIdType.MESH
T = 256
THIN = 64
CHUNK = 64
RELAY = 64
PIECE = 24


def xor(a, b):
    return a + b - 2 * a * b


def kernel(
    rows_hbm, cols_hbm, offs_hbm, heat_ref, cot_hbm, feat_hbm, weight_hbm, tiles_hbm,
    gw_ref, gf_ref,
    rows_ref, cols_ref, offs_ref, cot, feat, weight, tiles,
    field0, field1, own, acc, core_in, chip_out, chip_in, pair_out, pair_in, comb,
    gwp, g1, s1, g2, s2, gfin,
    load_sem, small_sem, cot_sem,
    rt_sem, relay_sem, gyt_sem, gy_sem, g0_sem, grest_sem, ring_sem, send_sem, self_sem,
    ex_send, ex_recv, chip_send, chip_recv, pair_send, pair_recv, cb_send, cb_recv, gw_send, gw_recv,
):
    blk = lax.axis_index("blk")
    rep = lax.axis_index("rep")
    z = blk // 8
    y = (blk // 2) % 4
    xh = blk % 2
    xl = rep // 2
    c = rep % 2
    n = xor(c, xh)
    hx = xor(xl, xh)
    own_tile = hx * 2 + c
    other_tile = (1 - hx) * 2 + c

    def dev(xh_, xl_, y_, z_, c_):
        return (z_ * 8 + y_ * 2 + xh_, xl_ * 2 + c_)

    def delta2(xh_, xl_):
        return (1 - xh_) * (3 - xl_) + xh_ * xl_

    relay_one = dev(xh, xl, (y + 1 - xl) % 4, z, 0)
    relay_two = dev(1 - xh, xl, (y + delta2(xh, xl)) % 4, z, 1)
    relay_two_near = dev(1 - xh, 1 - xl, (y + delta2(xh, 1 - xl)) % 4, z, 1)
    one_is_self = xl * (1 - c)

    yr = ((1 - c) * (y - 1 + xl) + c * (y - delta2(1 - xh, xl)) + 4) % 4
    hr = xor(xl, n)
    ey = 2 * hx - 1
    yc = ((1 - c) * (y - ey - 1 + xl) + c * (y - ey - delta2(1 - xh, xl)) + 8) % 4

    z_up = dev(xh, xl, y, (z + 1) % 8, c)
    z_dn = dev(xh, xl, y, (z + 7) % 8, c)
    y_chain = dev(xh, xl, (y + ey + 4) % 4, z, c)
    y_other = dev(xh, xl, (y - ey + 4) % 4, z, c)
    x_near = dev(xh, 1 - xl, y, z, c)
    x_far = dev(1 - xh, 1 - xl, y, z, 1 - c)
    sibling = dev(xh, xl, y, z, 1 - c)
    here = y * 2 + xh

    def plane_peer(step):
        place = (here + step) % 8
        return place, dev(place % 2, xl, place // 2, z, c)

    def z_peer(step):
        zt = (z + step) % 8
        return zt, dev(xh, xl, y, zt, c)

    def load(src, dst, sem):
        pltpu.make_async_copy(src, dst, sem).start()

    for i, tile in enumerate((own_tile, other_tile)):
        load(cot_hbm.at[pl.ds(pl.multiple_of(tile * T, T), T)], cot.at[i], cot_sem.at[i])
    load(rows_hbm, rows_ref, small_sem.at[0])
    load(cols_hbm, cols_ref, small_sem.at[1])
    load(offs_hbm, offs_ref, small_sem.at[2])
    load(tiles_hbm, tiles, load_sem.at[0])
    load(feat_hbm, feat, load_sem.at[1])
    load(weight_hbm, weight, load_sem.at[2])

    barrier = pltpu.get_barrier_semaphore()

    def greet(device):
        pl.semaphore_signal(barrier, inc=1, device_id=device, device_id_type=MESH)

    @pl.when(c == 0)
    def _():
        @pl.when(one_is_self == 0)
        def _():
            greet(dev(xh, xl, yr, z, 0))

        greet(dev(xh, xl, yr, z, 1))

    @pl.when(c == 1)
    def _():
        for core in range(2):
            greet(dev(1 - xh, xl, yr, z, core))
            greet(dev(1 - xh, 1 - xl, yr, z, core))

    for device in (y_chain, y_other, x_near, x_far, sibling):
        greet(device)
    for step in range(1, 8):
        greet(z_peer(step)[1])
        greet(plane_peer(step)[1])

    def send(src, dst, ssem, rsem, device):
        pltpu.make_async_remote_copy(
            src_ref=src, dst_ref=dst, send_sem=ssem, recv_sem=rsem, device_id=device, device_id_type=MESH
        ).start()

    def drain(ref, sem):
        pltpu.make_async_copy(ref, ref, sem).wait()

    def turned(ref):
        return ref[...].astype(jnp.float32).T.astype(jnp.bfloat16)

    drain(cot.at[0], cot_sem.at[0])
    own[0] = turned(cot.at[0])
    drain(cot.at[1], cot_sem.at[1])
    own[2] = turned(cot.at[1])

    pl.semaphore_wait(barrier, 22 - one_is_self)

    thin = pl.ds(0, THIN)
    wide = pl.ds(THIN, T - THIN)
    follow_of = {1: 2, 2: 3, 3: 7, 4: 5, 5: 6, 6: 7}

    def zp(i):
        return (z + (0, 7, 6, 5, 1, 2, 3, 4)[i]) % 8

    def spot(i, ysrc):
        return (zp(i) * 2 + ysrc // 2) * 4 + hr * 2

    def hand_out(p, buf, rows, to_two, two):
        mine = own.at[p, rows]
        slot = RELAY + z * 2 + c
        sem = rt_sem.at[p] if rows is thin else relay_sem.at[p, 0, c]

        @pl.when(one_is_self == 1)
        def _():
            load(mine, buf.at[slot, rows], sem)

        @pl.when(one_is_self == 0)
        def _():
            send(mine, buf.at[slot, rows], self_sem.at[p], sem, relay_one)

        send(two.at[rows], buf.at[slot, rows], send_sem.at[p, 0], sem, to_two)

    def gather(p, buf):
        def over_plane(i, tile, count, rows, ssem, chain_sem, rest):
            src = buf.at[pl.ds(RELAY + zp(i) * 2 + tile, count), rows]
            dst = buf.at[pl.ds(spot(i, yr) + tile, count), rows]
            send(src, dst, ssem, chain_sem, y_chain)
            send(src, dst, ssem, rest, y_other)
            send(src, dst, ssem, rest, x_near)

        def far(i, tile, count, rows, ssem, chain_sem, rest):
            drain(buf.at[pl.ds(0, count), rows], chain_sem)
            chained = spot(i, yc) + tile
            src = (1 - n) * (RELAY + zp(i) * 2 + tile) + n * chained
            dst = (1 - n) * (spot(i, yr) + tile) + n * chained
            send(buf.at[pl.ds(src, count), rows], buf.at[pl.ds(dst, count), rows], ssem, rest, x_far)

        def along_z(i, tile, up, follow):
            part = buf.at[RELAY + zp(i) * 2 + tile, wide]
            send(part, part, send_sem.at[p, 1], relay_sem.at[p, follow, tile], z_up if up else z_dn)

        def ring(i, block, up, follow):
            part = buf.at[pl.ds(zp(i) * 8 + block * 4, 4), thin]
            send(part, part, send_sem.at[p, 4], ring_sem.at[p, follow, block], z_up if up else z_dn)

        def wide_plane(i, tile):
            over_plane(i, tile, 1, wide, send_sem.at[p, 3], gy_sem.at[p, i, tile], grest_sem.at[p])

        def wide_far(i):
            for tile in range(2):
                far(i, tile, 1, wide, send_sem.at[p, 3], gy_sem.at[p, i, tile], grest_sem.at[p])

        def wide_wait(i, tile):
            drain(buf.at[0, wide], relay_sem.at[p, i, tile])

        def wide_step(s):
            for tile in range(2):
                for i, up in ((s, True), (s + 3, False)):
                    wide_wait(i, tile)
                    if s < 3 or tile == 1 - up:
                        along_z(i, tile, up, follow_of[i])
                    wide_plane(i, tile)

        def thin_step(s):
            for block in range(2):
                for i, up in ((s, True), (s + 3, False)):
                    drain(buf.at[pl.ds(0, 4), thin], ring_sem.at[p, i, block])
                    if s < 3 or block == 1 - up:
                        ring(i, block, up, follow_of[i])

        drain(buf.at[pl.ds(0, 2), thin], rt_sem.at[p])
        over_plane(0, 0, 2, thin, send_sem.at[p, 2], gyt_sem.at[p], g0_sem.at[p])
        for tile in range(2):
            wide_wait(0, tile)
            along_z(0, tile, True, 1)
            along_z(0, tile, False, 4)
            wide_plane(0, tile)
        far(0, 0, 2, thin, send_sem.at[p, 2], gyt_sem.at[p], g0_sem.at[p])
        drain(buf.at[pl.ds(0, 6), thin], g0_sem.at[p])
        for block in range(2):
            ring(0, block, True, 1)
            ring(0, block, False, 4)
        wide_step(1)
        wide_far(0)
        thin_step(1)
        wide_step(2)
        wide_far(1)
        wide_far(4)
        thin_step(2)
        wide_step(3)
        wide_far(2)
        wide_far(5)
        thin_step(3)
        for tile in range(2):
            wide_wait(7, tile)
            wide_plane(7, tile)
        wide_far(3)
        wide_far(6)
        wide_far(7)
        drain(buf.at[pl.ds(0, 48), wide], grest_sem.at[p])
        for block in range(2):
            drain(buf.at[pl.ds(0, 4), thin], ring_sem.at[p, 7, block])

    def part(j):
        return pl.ds(j * CHUNK, CHUNK)

    parts = T // CHUNK

    def products(buf, j):
        rows = part(j)
        total = jnp.zeros((4 * CHUNK, T), jnp.float32)
        for k in range(16):
            row = rows_ref[k]
            col = cols_ref[k] % 4
            alive = k < offs_ref[16]
            tile = buf[((row // 16) % 16) * 4 + row % 4, rows, :]
            picked = [
                jnp.where(jnp.logical_and(col == t, alive), tile, jnp.zeros_like(tile)) for t in range(4)
            ]
            total = total + jnp.dot(
                jnp.concatenate(picked, axis=0), tiles[k], preferred_element_type=jnp.float32
            )
        for t in range(4):
            acc[t, rows, :] = total[t * CHUNK : (t + 1) * CHUNK]

    def swap_cores(p, j):
        rows = part(j)
        for g in range(2):
            send(
                acc.at[g * 2 + 1 - c, rows], core_in.at[p, g, rows],
                ex_send.at[p, j], ex_recv.at[p, j], sibling,
            )

    def await_cores(p, j):
        drain(core_in.at[p, pl.ds(0, 2), part(j)], ex_recv.at[p, j])

    hand_out(0, field0, thin, relay_two_near, own.at[2])
    hand_out(0, field0, wide, relay_two_near, own.at[2])
    gather(0, field0)
    for i, ref in enumerate((rows_ref, cols_ref, offs_ref)):
        drain(ref, small_sem.at[i])
    drain(tiles, load_sem.at[0])

    def pass_on(j):
        rows = part(j)
        await_cores(0, j)
        chip_out[rows, :] = (acc[other_tile, rows, :] + core_in[0, 1 - hx, rows, :]).astype(jnp.bfloat16)
        send(chip_out.at[rows], chip_in.at[rows], chip_send.at[j], chip_recv.at[j], x_near)

    def close_first(j):
        rows = part(j)
        drain(chip_in.at[rows], chip_recv.at[j])
        own[1, rows, :] = (
            acc[own_tile, rows, :] + core_in[0, hx, rows, :] + chip_in[rows, :].astype(jnp.float32)
        ).astype(jnp.bfloat16)

    for j in range(parts):
        products(field0, j)
        swap_cores(0, j)
        if j >= 1:
            pass_on(j - 1)
        if j >= 2:
            close_first(j - 2)
        if j == 2:
            hand_out(1, field1, thin, relay_two, own.at[1])
    pass_on(parts - 1)
    close_first(parts - 2)
    close_first(parts - 1)

    hand_out(1, field1, wide, relay_two, own.at[1])
    gather(1, field1)
    for j in range(parts):
        drain(core_in.at[0, pl.ds(0, 2), part(j)], ex_send.at[0, j])

    tv = jnp.full((1, T), heat_ref[0], jnp.float32)
    total = 1.0 + tv + tv * tv / 2.0
    coef0 = 1.0 / total
    coef1 = tv / total
    coef2 = (tv * tv / 2.0) / total

    def pair_up(j):
        rows = part(j)
        await_cores(1, j)
        mine = coef2 * (acc[own_tile, rows, :] + core_in[1, hx, rows, :])
        mine += coef0 * own[0, rows, :].astype(jnp.float32) + coef1 * own[1, rows, :].astype(jnp.float32)
        acc[own_tile, rows, :] = mine
        pair_out[0, rows, :] = mine.astype(jnp.bfloat16)
        theirs = coef2 * (acc[other_tile, rows, :] + core_in[1, 1 - hx, rows, :])
        acc[other_tile, rows, :] = theirs
        pair_out[1, rows, :] = theirs.astype(jnp.bfloat16)
        for i in range(2):
            send(pair_out.at[i, rows], pair_in.at[1 - i, rows], pair_send.at[j], pair_recv.at[j], x_near)

    def close_second(j):
        rows = part(j)
        drain(pair_in.at[pl.ds(0, 2), rows], pair_recv.at[j])
        for i, tile in enumerate((own_tile, other_tile)):
            comb[tile, rows, :] = (acc[tile, rows, :] + pair_in[i, rows, :].astype(jnp.float32)).astype(
                jnp.bfloat16
            )
            send(comb.at[tile, rows], comb.at[tile, rows], cb_send, cb_recv, sibling)

    for j in range(parts):
        products(field1, j)
        swap_cores(1, j)
        if j >= 1:
            pair_up(j - 1)
        if j >= 2:
            close_second(j - 2)
    pair_up(parts - 1)
    close_second(parts - 2)
    close_second(parts - 1)
    drain(feat, load_sem.at[1])
    drain(weight, load_sem.at[2])
    drain(comb.at[pl.ds(0, 2)], cb_recv)

    partial = jnp.zeros((192, T), jnp.float32)
    for t in range(4):
        partial += lax.dot_general(
            feat[:, t * T : (t + 1) * T], comb[t], (((1,), (1,)), ((), ())),
            preferred_element_type=jnp.float32,
        )
    gwp[...] = partial * (1.0 / 256.0)

    for step in range(1, 8):
        place, device = plane_peer(step)
        rows = pl.ds(pl.multiple_of(place * PIECE, 8), PIECE)
        send(gwp.at[rows], g1.at[here], gw_send.at[0], gw_recv.at[0], device)
    g1[here] = gwp[pl.ds(pl.multiple_of(here * PIECE, 8), PIECE), :]

    for t in range(4):
        gf_ref[:, t * T : (t + 1) * T] = jnp.dot(
            weight[...], comb[t], preferred_element_type=jnp.float32
        ).astype(jnp.bfloat16)

    drain(g1.at[pl.ds(0, 7)], gw_recv.at[0])
    s1[...] = functools.reduce(lambda a, b: a + b, [g1[i] for i in range(8)])
    for step in range(1, 8):
        send(s1, g2.at[z], gw_send.at[1], gw_recv.at[1], z_peer(step)[1])
    g2[z] = s1[...]
    drain(g2.at[pl.ds(0, 7)], gw_recv.at[1])
    s2[...] = functools.reduce(lambda a, b: a + b, [g2[i] for i in range(8)])
    for step in range(1, 8):
        send(s2, gfin.at[here], gw_send.at[2], gw_recv.at[2], plane_peer(step)[1])
    gfin[here] = s2[...]

    for p, buf in enumerate((field0, field1)):
        @pl.when(one_is_self == 0)
        def _(p=p):
            drain(own.at[p], self_sem.at[p])

        drain(own.at[p], send_sem.at[p, 0])
        drain(buf.at[pl.ds(0, 14), wide], send_sem.at[p, 1])
        drain(buf.at[pl.ds(0, 8), thin], send_sem.at[p, 2])
        drain(buf.at[pl.ds(0, 64), wide], send_sem.at[p, 3])
        drain(buf.at[pl.ds(0, 56), thin], send_sem.at[p, 4])
    for j in range(parts):
        drain(core_in.at[1, pl.ds(0, 2), part(j)], ex_send.at[1, j])
        drain(chip_in.at[part(j)], chip_send.at[j])
        drain(pair_in.at[pl.ds(0, 2), part(j)], pair_send.at[j])
    drain(comb.at[pl.ds(0, 2)], cb_send)

    drain(gfin.at[pl.ds(0, 7)], gw_recv.at[2])
    for i in range(8):
        gw_ref[i * PIECE : (i + 1) * PIECE, :] = gfin[i]
    for i in range(3):
        drain(g1.at[pl.ds(0, 7)], gw_send.at[i])


def local(cotangent, features, weight, heat_time, tile_values, tile_row, tile_col, section_offsets):
    vmem = pl.BlockSpec(memory_space=pltpu.VMEM)
    hbm = pl.BlockSpec(memory_space=pl.ANY)
    f32, bf16, i32 = jnp.float32, jnp.bfloat16, jnp.int32
    dma = pltpu.SemaphoreType.DMA
    parts = T // CHUNK
    grad_weight, grad_features = pl.pallas_call(
        kernel,
        out_shape=(
            jax.ShapeDtypeStruct((192, T), f32),
            jax.ShapeDtypeStruct((192, 1024), bf16),
        ),
        in_specs=[hbm, hbm, hbm, pl.BlockSpec(memory_space=pltpu.SMEM), hbm, hbm, hbm, hbm],
        out_specs=(vmem, vmem),
        scratch_shapes=[
            pltpu.SMEM((16,), i32), pltpu.SMEM((16,), i32), pltpu.SMEM((17,), i32),
            pltpu.VMEM((2, T, T), bf16),
            pltpu.VMEM((192, 1024), bf16),
            pltpu.VMEM((192, T), bf16),
            pltpu.VMEM((16, T, T), bf16),
            pltpu.VMEM((RELAY + 16, T, T), bf16),
            pltpu.VMEM((RELAY + 16, T, T), bf16),
            pltpu.VMEM((3, T, T), bf16),
            pltpu.VMEM((4, T, T), f32),
            pltpu.VMEM((2, 2, T, T), f32),
            pltpu.VMEM((T, T), bf16),
            pltpu.VMEM((T, T), bf16),
            pltpu.VMEM((2, T, T), bf16),
            pltpu.VMEM((2, T, T), bf16),
            pltpu.VMEM((4, T, T), bf16),
            pltpu.VMEM((192, T), f32),
            pltpu.VMEM((8, PIECE, T), f32),
            pltpu.VMEM((PIECE, T), f32),
            pltpu.VMEM((8, PIECE, T), f32),
            pltpu.VMEM((PIECE, T), f32),
            pltpu.VMEM((8, PIECE, T), f32),
            dma((3,)), dma((3,)), dma((2,)),
            dma((2,)),
            dma((2, 8, 2)),
            dma((2,)),
            dma((2, 8, 2)),
            dma((2,)),
            dma((2,)),
            dma((2, 8, 2)),
            dma((2, 5)),
            dma((2,)),
            dma((2, parts)), dma((2, parts)),
            dma((parts,)), dma((parts,)),
            dma((parts,)), dma((parts,)),
            dma, dma,
            dma((3,)), dma((3,)),
        ],
        compiler_params=pltpu.CompilerParams(
            collective_id=0, has_side_effects=True, vmem_limit_bytes=60 << 20
        ),
        cost_estimate=pl.CostEstimate(flops=4_800_000_000, bytes_accessed=4_000_000, transcendentals=0),
        name="diffuse",
    )(tile_row, tile_col, section_offsets, heat_time, cotangent, features.T, weight, tile_values)
    return grad_weight, grad_features.T


def solution(mesh):
    in_specs = (
        P("blk", None),
        P("blk", "rep"),
        P("rep", None),
        P(),
        P(("blk", "rep"), None, None),
        P(("blk", "rep")),
        P(("blk", "rep")),
        P(("blk", "rep")),
    )
    out_specs = (P("rep", None), P("blk", "rep"))
    return jax.shard_map(local, mesh=mesh, in_specs=in_specs, out_specs=out_specs, check_vma=False)
```

```python
import functools

import jax
import jax.numpy as jnp
from jax import lax
from jax.experimental import pallas as pl
from jax.experimental.pallas import tpu as pltpu
from jax.sharding import PartitionSpec as P

MESH = pl.DeviceIdType.MESH
T = 256
THIN = 64
CHUNK = 64
RELAY = 64
PIECE = 24

FIRST_ORDER = " ".join((
    "T00 W00 W01 t00",
    "F00 R00 W10 F01",
    "W41 W40 W11 R11",
    "W20 R10 F40 R40",
    "F11 W50 F41 F10",
    "W21 W51 F20 F51",
    "W30 R41 W60 R21",
    "R20 F50 W31 F21",
    "W61 W70 R50 R51",
    "F30 F60 W71 F31",
    "F61 R31 F71 F70",
    "R61 R60 R30",
))
SECOND_ORDER = " ".join((
    "T00 t00 W00 W01",
    "R00 W10 W40 W11",
    "F01 W41 F10 R40",
    "R11 F41 R41 F40",
    "F00 F11 W20 R10",
    "W21 R50 W50 W51",
    "W30 R51 F20 F21",
    "R20 W31 F51 W60",
    "W61 F30 R21 R61",
    "F31 R30 W70 R60",
    "F50 F61 W71 F70",
    "F71 F60 R31",
))


def xor(a, b):
    return a + b - 2 * a * b


def kernel(
    rows_hbm, cols_hbm, offs_hbm, heat_ref, cot_hbm, feat_hbm, weight_hbm, tiles_hbm,
    gw_ref, gf_ref,
    rows_ref, cols_ref, offs_ref, cot, feat, weight, tiles,
    field0, field1, own, acc, core_in, chip_out, chip_in, pair_out, pair_in, comb,
    gwp, g1, s1, g2, s2, gfin,
    load_sem, small_sem, cot_sem,
    rt_sem, relay_sem, thin_sem, plane_sem, ring_sem, send_sem, self_sem,
    ex_send, ex_recv, chip_send, chip_recv, pair_send, pair_recv, cb_send, cb_recv, gw_send, gw_recv,
):
    blk = lax.axis_index("blk")
    rep = lax.axis_index("rep")
    z = blk // 8
    y = (blk // 2) % 4
    xh = blk % 2
    xl = rep // 2
    c = rep % 2
    n = xor(c, xh)
    hx = xor(xl, xh)
    own_tile = hx * 2 + c
    other_tile = (1 - hx) * 2 + c

    def dev(xh_, xl_, y_, z_, c_):
        return (z_ * 8 + y_ * 2 + xh_, xl_ * 2 + c_)

    def delta2(xh_, xl_):
        return (1 - xh_) * (3 - xl_) + xh_ * xl_

    relay_one = dev(xh, xl, (y + 1 - xl) % 4, z, 0)
    relay_two = dev(1 - xh, xl, (y + delta2(xh, xl)) % 4, z, 1)
    relay_two_near = dev(1 - xh, 1 - xl, (y + delta2(xh, 1 - xl)) % 4, z, 1)
    one_is_self = xl * (1 - c)

    yr = ((1 - c) * (y - 1 + xl) + c * (y - delta2(1 - xh, xl)) + 4) % 4
    hr = xor(xl, n)
    ey = 2 * hx - 1
    yc = ((1 - c) * (y - ey - 1 + xl) + c * (y - ey - delta2(1 - xh, xl)) + 8) % 4

    z_up = dev(xh, xl, y, (z + 1) % 8, c)
    z_dn = dev(xh, xl, y, (z + 7) % 8, c)
    y_chain = dev(xh, xl, (y + ey + 4) % 4, z, c)
    y_other = dev(xh, xl, (y - ey + 4) % 4, z, c)
    x_near = dev(xh, 1 - xl, y, z, c)
    x_far = dev(1 - xh, 1 - xl, y, z, 1 - c)
    sibling = dev(xh, xl, y, z, 1 - c)
    here = y * 2 + xh

    def plane_peer(step):
        place = (here + step) % 8
        return place, dev(place % 2, xl, place // 2, z, c)

    def z_peer(step):
        zt = (z + step) % 8
        return zt, dev(xh, xl, y, zt, c)

    def load(src, dst, sem):
        pltpu.make_async_copy(src, dst, sem).start()

    for i, tile in enumerate((own_tile, other_tile)):
        load(cot_hbm.at[pl.ds(pl.multiple_of(tile * T, T), T)], cot.at[i], cot_sem.at[i])
    load(rows_hbm, rows_ref, small_sem.at[0])
    load(cols_hbm, cols_ref, small_sem.at[1])
    load(offs_hbm, offs_ref, small_sem.at[2])
    load(tiles_hbm, tiles, load_sem.at[0])
    load(feat_hbm, feat, load_sem.at[1])
    load(weight_hbm, weight, load_sem.at[2])

    barrier = pltpu.get_barrier_semaphore()

    def greet(device):
        pl.semaphore_signal(barrier, inc=1, device_id=device, device_id_type=MESH)

    @pl.when(c == 0)
    def _():
        @pl.when(one_is_self == 0)
        def _():
            greet(dev(xh, xl, yr, z, 0))

        greet(dev(xh, xl, yr, z, 1))

    @pl.when(c == 1)
    def _():
        for core in range(2):
            greet(dev(1 - xh, xl, yr, z, core))
            greet(dev(1 - xh, 1 - xl, yr, z, core))

    for device in (y_chain, y_other, x_near, x_far, sibling):
        greet(device)
    greet(z_up)
    greet(z_dn)

    def send(src, dst, ssem, rsem, device):
        pltpu.make_async_remote_copy(
            src_ref=src, dst_ref=dst, send_sem=ssem, recv_sem=rsem, device_id=device, device_id_type=MESH
        ).start()

    def drain(ref, sem):
        pltpu.make_async_copy(ref, ref, sem).wait()

    def turned(ref):
        return ref[...].astype(jnp.float32).T.astype(jnp.bfloat16)

    drain(cot.at[0], cot_sem.at[0])
    own[0] = turned(cot.at[0])
    drain(cot.at[1], cot_sem.at[1])
    own[2] = turned(cot.at[1])

    pl.semaphore_wait(barrier, 10 - one_is_self)

    thin = pl.ds(0, THIN)
    wide = pl.ds(THIN, T - THIN)
    follow_of = {1: 2, 2: 3, 3: 7, 4: 5, 5: 6, 6: 7}

    def zp(i):
        return (z + (0, 7, 6, 5, 1, 2, 3, 4)[i]) % 8

    def spot(i, ysrc):
        return (zp(i) * 2 + ysrc // 2) * 4 + hr * 2

    def hand_out(p, buf, rows, to_two, two):
        mine = own.at[p, rows]
        slot = RELAY + z * 2 + c
        sem = rt_sem.at[p] if rows is thin else relay_sem.at[p, 0, c]

        @pl.when(one_is_self == 1)
        def _():
            load(mine, buf.at[slot, rows], sem)

        @pl.when(one_is_self == 0)
        def _():
            send(mine, buf.at[slot, rows], self_sem.at[p], sem, relay_one)

        send(two.at[rows], buf.at[slot, rows], send_sem.at[p, 0], sem, to_two)

    def gather(p, buf, order):
        def over_plane(i, tile, count, rows, ssem, chain_sem, rest):
            src = buf.at[pl.ds(RELAY + zp(i) * 2 + tile, count), rows]
            dst = buf.at[pl.ds(spot(i, yr) + tile, count), rows]
            send(src, dst, ssem, chain_sem, y_chain)
            send(src, dst, ssem, rest, y_other)
            send(src, dst, ssem, rest, x_near)

            @pl.when(n == 0)
            def _():
                send(src, dst, ssem, rest, x_far)

        def far(i, tile, count, rows, ssem, chain_sem, rest):
            @pl.when(n == 1)
            def _():
                drain(buf.at[pl.ds(0, count), rows], chain_sem)
                part = buf.at[pl.ds(spot(i, yc) + tile, count), rows]
                send(part, part, ssem, rest, x_far)

        def along_z(i, tile, up, follow):
            part = buf.at[RELAY + zp(i) * 2 + tile, wide]
            send(part, part, send_sem.at[p, 1], relay_sem.at[p, follow, tile], z_up if up else z_dn)

        def ring(i, block, up, follow):
            part = buf.at[pl.ds(zp(i) * 8 + block * 4, 4), thin]
            send(part, part, send_sem.at[p, 4], ring_sem.at[p, follow, block], z_up if up else z_dn)

        def thin_task():
            drain(buf.at[pl.ds(0, 2), thin], rt_sem.at[p])
            over_plane(0, 0, 2, thin, send_sem.at[p, 2], thin_sem.at[p, n], thin_sem.at[p, 0])

        def thin_far_task():
            far(0, 0, 2, thin, send_sem.at[p, 2], thin_sem.at[p, 1], thin_sem.at[p, 0])

        def wide_task(i, tile):
            drain(buf.at[0, wide], relay_sem.at[p, i, tile])
            if i == 0:
                along_z(0, tile, True, 1)
                along_z(0, tile, False, 4)
            elif i in (1, 2, 4, 5) or (i, tile) in ((3, 0), (6, 1)):
                along_z(i, tile, i < 4, follow_of[i])
            over_plane(
                i, tile, 1, wide, send_sem.at[p, 3],
                plane_sem.at[p, n * (1 + i * 2 + tile)], plane_sem.at[p, 0],
            )

        def wide_far_task(i, tile):
            far(i, tile, 1, wide, send_sem.at[p, 3], plane_sem.at[p, 1 + i * 2 + tile], plane_sem.at[p, 0])

        def ring_task(i, block):
            if i == 0:
                for cls, count in ((0, 8), (1, 6)):
                    @pl.when(n == cls)
                    def _(count=count):
                        drain(buf.at[pl.ds(0, count), thin], thin_sem.at[p, 0])

                for b in range(2):
                    ring(0, b, True, 1)
                    ring(0, b, False, 4)
                return
            drain(buf.at[pl.ds(0, 4), thin], ring_sem.at[p, i, block])
            if i in (1, 2, 4, 5) or (i, block) in ((3, 0), (6, 1)):
                ring(i, block, i < 4, follow_of[i])

        for name in order.split():
            kind, i, piece = name[0], int(name[1]), int(name[2])
            if kind == "T":
                thin_task()
            elif kind == "t":
                thin_far_task()
            elif kind == "W":
                wide_task(i, piece)
            elif kind == "F":
                wide_far_task(i, piece)
            else:
                ring_task(i, piece)
        for cls, count in ((0, 64), (1, 48)):
            @pl.when(n == cls)
            def _(count=count):
                drain(buf.at[pl.ds(0, count), wide], plane_sem.at[p, 0])

        for block in range(2):
            drain(buf.at[pl.ds(0, 4), thin], ring_sem.at[p, 7, block])

    def part(j):
        return pl.ds(j * CHUNK, CHUNK)

    parts = T // CHUNK

    def products(buf, j):
        rows = part(j)
        total = jnp.zeros((4 * CHUNK, T), jnp.float32)
        for k in range(16):
            row = rows_ref[k]
            col = cols_ref[k] % 4
            alive = k < offs_ref[16]
            tile = buf[((row // 16) % 16) * 4 + row % 4, rows, :]
            picked = [
                jnp.where(jnp.logical_and(col == t, alive), tile, jnp.zeros_like(tile)) for t in range(4)
            ]
            total = total + jnp.dot(
                jnp.concatenate(picked, axis=0), tiles[k], preferred_element_type=jnp.float32
            )
        for t in range(4):
            acc[t, rows, :] = total[t * CHUNK : (t + 1) * CHUNK]

    def swap_cores(p, j):
        rows = part(j)
        for g in range(2):
            send(
                acc.at[g * 2 + 1 - c, rows], core_in.at[p, g, rows],
                ex_send.at[p, j], ex_recv.at[p, j], sibling,
            )

    def await_cores(p, j):
        drain(core_in.at[p, pl.ds(0, 2), part(j)], ex_recv.at[p, j])

    hand_out(0, field0, thin, relay_two_near, own.at[2])
    hand_out(0, field0, wide, relay_two_near, own.at[2])
    gather(0, field0, FIRST_ORDER)
    for i, ref in enumerate((rows_ref, cols_ref, offs_ref)):
        drain(ref, small_sem.at[i])
    drain(tiles, load_sem.at[0])

    def pass_on(j):
        rows = part(j)
        await_cores(0, j)
        chip_out[rows, :] = (acc[other_tile, rows, :] + core_in[0, 1 - hx, rows, :]).astype(jnp.bfloat16)
        send(chip_out.at[rows], chip_in.at[rows], chip_send.at[j], chip_recv.at[j], x_near)

    def close_first(j):
        rows = part(j)
        drain(chip_in.at[rows], chip_recv.at[j])
        own[1, rows, :] = (
            acc[own_tile, rows, :] + core_in[0, hx, rows, :] + chip_in[rows, :].astype(jnp.float32)
        ).astype(jnp.bfloat16)

    for j in range(parts):
        products(field0, j)
        swap_cores(0, j)
        if j >= 1:
            pass_on(j - 1)
        if j >= 2:
            close_first(j - 2)
        if j == 2:
            hand_out(1, field1, thin, relay_two, own.at[1])
    pass_on(parts - 1)
    close_first(parts - 2)
    close_first(parts - 1)

    hand_out(1, field1, wide, relay_two, own.at[1])
    gather(1, field1, SECOND_ORDER)
    for j in range(parts):
        drain(core_in.at[0, pl.ds(0, 2), part(j)], ex_send.at[0, j])

    tv = jnp.full((1, T), heat_ref[0], jnp.float32)
    total = 1.0 + tv + tv * tv / 2.0
    coef0 = 1.0 / total
    coef1 = tv / total
    coef2 = (tv * tv / 2.0) / total

    def pair_up(j):
        rows = part(j)
        await_cores(1, j)
        mine = coef2 * (acc[own_tile, rows, :] + core_in[1, hx, rows, :])
        mine += coef0 * own[0, rows, :].astype(jnp.float32) + coef1 * own[1, rows, :].astype(jnp.float32)
        acc[own_tile, rows, :] = mine
        pair_out[0, rows, :] = mine.astype(jnp.bfloat16)
        theirs = coef2 * (acc[other_tile, rows, :] + core_in[1, 1 - hx, rows, :])
        acc[other_tile, rows, :] = theirs
        pair_out[1, rows, :] = theirs.astype(jnp.bfloat16)
        for i in range(2):
            send(pair_out.at[i, rows], pair_in.at[1 - i, rows], pair_send.at[j], pair_recv.at[j], x_near)

    def close_second(j):
        rows = part(j)
        drain(pair_in.at[pl.ds(0, 2), rows], pair_recv.at[j])
        for i, tile in enumerate((own_tile, other_tile)):
            comb[tile, rows, :] = (acc[tile, rows, :] + pair_in[i, rows, :].astype(jnp.float32)).astype(
                jnp.bfloat16
            )
            send(comb.at[tile, rows], comb.at[tile, rows], cb_send, cb_recv, sibling)

    for j in range(parts):
        products(field1, j)
        swap_cores(1, j)
        if j >= 1:
            pair_up(j - 1)
        if j >= 2:
            close_second(j - 2)
    pair_up(parts - 1)
    close_second(parts - 2)
    close_second(parts - 1)
    drain(feat, load_sem.at[1])
    drain(weight, load_sem.at[2])
    drain(comb.at[pl.ds(0, 2)], cb_recv)

    partial = jnp.zeros((192, T), jnp.float32)
    for t in range(4):
        partial += lax.dot_general(
            feat[:, t * T : (t + 1) * T], comb[t], (((1,), (1,)), ((), ())),
            preferred_element_type=jnp.float32,
        )
    partial = partial * (1.0 / 256.0)
    for i in range(8):
        piece = partial[i * PIECE : (i + 1) * PIECE]
        gwp[i] = jnp.concatenate([piece[:, :128], piece[:, 128:]], axis=0).astype(jnp.bfloat16)

    for step in range(1, 8):
        place, device = plane_peer(step)
        send(gwp.at[place], g1.at[here], gw_send.at[0], gw_recv.at[0], device)
    g1[here] = gwp[here]

    for t in range(4):
        gf_ref[:, t * T : (t + 1) * T] = jnp.dot(
            weight[...], comb[t], preferred_element_type=jnp.float32
        ).astype(jnp.bfloat16)

    drain(g1.at[pl.ds(0, 7)], gw_recv.at[0])
    s1[...] = functools.reduce(lambda a, b: a + b, [g1[i].astype(jnp.float32) for i in range(8)]).astype(
        jnp.bfloat16
    )
    for step in range(1, 8):
        send(s1, g2.at[z], gw_send.at[1], gw_recv.at[1], z_peer(step)[1])
    g2[z] = s1[...]
    drain(g2.at[pl.ds(0, 7)], gw_recv.at[1])
    s2[...] = functools.reduce(lambda a, b: a + b, [g2[i].astype(jnp.float32) for i in range(8)])
    for step in range(1, 8):
        send(s2, gfin.at[here], gw_send.at[2], gw_recv.at[2], plane_peer(step)[1])
    gfin[here] = s2[...]

    for p, buf in enumerate((field0, field1)):
        @pl.when(one_is_self == 0)
        def _(p=p):
            drain(own.at[p], self_sem.at[p])

        drain(own.at[p], send_sem.at[p, 0])
        drain(buf.at[pl.ds(0, 14), wide], send_sem.at[p, 1])
        drain(buf.at[pl.ds(0, 8), thin], send_sem.at[p, 2])
        drain(buf.at[pl.ds(0, 64), wide], send_sem.at[p, 3])
        drain(buf.at[pl.ds(0, 56), thin], send_sem.at[p, 4])
    for j in range(parts):
        drain(core_in.at[1, pl.ds(0, 2), part(j)], ex_send.at[1, j])
        drain(chip_in.at[part(j)], chip_send.at[j])
        drain(pair_in.at[pl.ds(0, 2), part(j)], pair_send.at[j])
    drain(comb.at[pl.ds(0, 2)], cb_send)

    drain(gfin.at[pl.ds(0, 7)], gw_recv.at[2])
    for i in range(8):
        gw_ref[i * PIECE : (i + 1) * PIECE, :128] = gfin[i, :PIECE, :]
        gw_ref[i * PIECE : (i + 1) * PIECE, 128:] = gfin[i, PIECE:, :]
    for i, ref in enumerate((g1, g2, gfin)):
        drain(ref.at[pl.ds(0, 7)], gw_send.at[i])


def hand_back(gw_in, gf_in, gw_out, gf_out, sem):
    copies = [
        pltpu.make_async_copy(src, dst, sem.at[i])
        for i, (src, dst) in enumerate(((gw_in, gw_out), (gf_in, gf_out)))
    ]
    for copy in copies:
        copy.start()
    for copy in copies:
        copy.wait()


def local(cotangent, features, weight, heat_time, tile_values, tile_row, tile_col, section_offsets):
    vmem = pl.BlockSpec(memory_space=pltpu.VMEM)
    hbm = pl.BlockSpec(memory_space=pltpu.HBM)
    f32, bf16, i32 = jnp.float32, jnp.bfloat16, jnp.int32
    dma = pltpu.SemaphoreType.DMA
    parts = T // CHUNK
    grad_weight, grad_features = pl.pallas_call(
        kernel,
        out_shape=(
            jax.ShapeDtypeStruct((192, T), f32),
            jax.ShapeDtypeStruct((192, 1024), bf16),
        ),
        in_specs=[hbm, hbm, hbm, pl.BlockSpec(memory_space=pltpu.SMEM), hbm, hbm, hbm, hbm],
        out_specs=(vmem, vmem),
        scratch_shapes=[
            pltpu.SMEM((16,), i32), pltpu.SMEM((16,), i32), pltpu.SMEM((17,), i32),
            pltpu.VMEM((2, T, T), bf16),
            pltpu.VMEM((192, 1024), bf16),
            pltpu.VMEM((192, T), bf16),
            pltpu.VMEM((16, T, T), bf16),
            pltpu.VMEM((RELAY + 16, T, T), bf16),
            pltpu.VMEM((RELAY + 16, T, T), bf16),
            pltpu.VMEM((3, T, T), bf16),
            pltpu.VMEM((4, T, T), f32),
            pltpu.VMEM((2, 2, T, T), f32),
            pltpu.VMEM((T, T), bf16),
            pltpu.VMEM((T, T), bf16),
            pltpu.VMEM((2, T, T), bf16),
            pltpu.VMEM((2, T, T), bf16),
            pltpu.VMEM((4, T, T), bf16),
            pltpu.VMEM((8, 2 * PIECE, 128), bf16),
            pltpu.VMEM((8, 2 * PIECE, 128), bf16),
            pltpu.VMEM((2 * PIECE, 128), bf16),
            pltpu.VMEM((8, 2 * PIECE, 128), bf16),
            pltpu.VMEM((2 * PIECE, 128), f32),
            pltpu.VMEM((8, 2 * PIECE, 128), f32),
            dma((3,)), dma((3,)), dma((2,)),
            dma((2,)),
            dma((2, 8, 2)),
            dma((2, 2)),
            dma((2, 17)),
            dma((2, 8, 2)),
            dma((2, 5)),
            dma((2,)),
            dma((2, parts)), dma((2, parts)),
            dma((parts,)), dma((parts,)),
            dma((parts,)), dma((parts,)),
            dma, dma,
            dma((3,)), dma((3,)),
        ],
        compiler_params=pltpu.CompilerParams(
            collective_id=0, has_side_effects=True, vmem_limit_bytes=60 << 20
        ),
        cost_estimate=pl.CostEstimate(flops=4_800_000_000, bytes_accessed=4_000_000, transcendentals=0),
        name="diffuse",
    )(tile_row, tile_col, section_offsets, heat_time, cotangent, features.T, weight, tile_values)
    grad_weight, grad_features = pl.pallas_call(
        hand_back,
        out_shape=(
            jax.ShapeDtypeStruct((192, T), f32),
            jax.ShapeDtypeStruct((192, 1024), bf16),
        ),
        in_specs=[pl.BlockSpec(memory_space=pl.ANY)] * 2,
        out_specs=(pl.BlockSpec(memory_space=pl.ANY),) * 2,
        scratch_shapes=[dma((2,))],
        name="hand_back",
    )(grad_weight, grad_features)
    return grad_weight, grad_features.T


def solution(mesh):
    in_specs = (
        P("blk", None),
        P("blk", "rep"),
        P("rep", None),
        P(),
        P(("blk", "rep"), None, None),
        P(("blk", "rep")),
        P(("blk", "rep")),
        P(("blk", "rep")),
    )
    out_specs = (P("rep", None), P("blk", "rep"))
    return jax.shard_map(local, mesh=mesh, in_specs=in_specs, out_specs=out_specs, check_vma=False)
```

```python
import functools

import jax
import jax.numpy as jnp
from jax import lax
from jax.experimental import pallas as pl
from jax.experimental.pallas import tpu as pltpu
from jax.sharding import PartitionSpec as P

MESH = pl.DeviceIdType.MESH
T = 256
THIN = 64
CHUNK = 64
RELAY = 64
PIECE = 24

FIRST_ORDER = " ".join((
    "T00 W00 W01 t00",
    "F00 R00 W10 F01",
    "W41 W40 W11 R11",
    "W20 R10 F40 R40",
    "F11 W50 F41 F10",
    "W21 W51 F20 F51",
    "W30 R41 W60 R21",
    "R20 F50 W31 F21",
    "W61 W70 R50 R51",
    "F30 F60 W71 F31",
    "F61 R31 F71 F70",
    "R61 R60 R30",
))
SECOND_ORDER = " ".join((
    "T00 t00 W00 W01",
    "R00 W10 W40 W11",
    "F01 W41 F10 R40",
    "R11 F41 R41 F40",
    "F00 F11 W20 R10",
    "W21 R50 W50 W51",
    "W30 R51 F20 F21",
    "R20 W31 F51 W60",
    "W61 F30 R21 R61",
    "F31 R30 W70 R60",
    "F50 F61 W71 F70",
    "F71 F60 R31",
))


def xor(a, b):
    return a + b - 2 * a * b


def kernel(
    rows_hbm, cols_hbm, offs_hbm, heat_ref, cot_hbm, feat_hbm, weight_hbm, tiles_hbm,
    gw_ref, gf_ref,
    rows_ref, cols_ref, offs_ref, cot, feat, weight, tiles,
    field0, field1, own, acc, core_in, chip_out, chip_in, pair_out, pair_in, comb,
    gwp, g1, s1, g2, s2, gfin,
    load_sem, small_sem, cot_sem,
    rt_sem, relay_sem, thin_sem, plane_sem, ring_sem, send_sem, self_sem,
    ex_send, ex_recv, chip_send, chip_recv, pair_send, pair_recv, cb_send, cb_recv, gw_send, gw_recv,
):
    blk = lax.axis_index("blk")
    rep = lax.axis_index("rep")
    z = blk // 8
    y = (blk // 2) % 4
    xh = blk % 2
    xl = rep // 2
    c = rep % 2
    n = xor(c, xh)
    hx = xor(xl, xh)
    own_tile = hx * 2 + c
    other_tile = (1 - hx) * 2 + c

    def dev(xh_, xl_, y_, z_, c_):
        return (z_ * 8 + y_ * 2 + xh_, xl_ * 2 + c_)

    def delta2(xh_, xl_):
        return (1 - xh_) * (3 - xl_) + xh_ * xl_

    relay_one = dev(xh, xl, (y + 1 - xl) % 4, z, 0)
    relay_two = dev(1 - xh, xl, (y + delta2(xh, xl)) % 4, z, 1)
    relay_two_near = dev(1 - xh, 1 - xl, (y + delta2(xh, 1 - xl)) % 4, z, 1)
    one_is_self = xl * (1 - c)

    yr = ((1 - c) * (y - 1 + xl) + c * (y - delta2(1 - xh, xl)) + 4) % 4
    hr = xor(xl, n)
    ey = 2 * hx - 1
    yc = ((1 - c) * (y - ey - 1 + xl) + c * (y - ey - delta2(1 - xh, xl)) + 8) % 4

    z_up = dev(xh, xl, y, (z + 1) % 8, c)
    z_dn = dev(xh, xl, y, (z + 7) % 8, c)
    y_chain = dev(xh, xl, (y + ey + 4) % 4, z, c)
    y_other = dev(xh, xl, (y - ey + 4) % 4, z, c)
    x_near = dev(xh, 1 - xl, y, z, c)
    x_far = dev(1 - xh, 1 - xl, y, z, 1 - c)
    sibling = dev(xh, xl, y, z, 1 - c)
    here = y * 2 + xh

    def plane_peer(step):
        place = (here + step) % 8
        return place, dev(place % 2, xl, place // 2, z, c)

    def z_peer(step):
        zt = (z + step) % 8
        return zt, dev(xh, xl, y, zt, c)

    def load(src, dst, sem):
        pltpu.make_async_copy(src, dst, sem).start()

    for i, tile in enumerate((own_tile, other_tile)):
        load(cot_hbm.at[pl.ds(pl.multiple_of(tile * T, T), T)], cot.at[i], cot_sem.at[i])
    load(rows_hbm, rows_ref, small_sem.at[0])
    load(cols_hbm, cols_ref, small_sem.at[1])
    load(offs_hbm, offs_ref, small_sem.at[2])
    load(tiles_hbm, tiles, load_sem.at[0])
    load(feat_hbm, feat, load_sem.at[1])
    load(weight_hbm, weight, load_sem.at[2])

    barrier = pltpu.get_barrier_semaphore()

    def greet(device):
        pl.semaphore_signal(barrier, inc=1, device_id=device, device_id_type=MESH)

    @pl.when(c == 0)
    def _():
        @pl.when(one_is_self == 0)
        def _():
            greet(dev(xh, xl, yr, z, 0))

        greet(dev(xh, xl, yr, z, 1))

    @pl.when(c == 1)
    def _():
        for core in range(2):
            greet(dev(1 - xh, xl, yr, z, core))
            greet(dev(1 - xh, 1 - xl, yr, z, core))

    for device in (y_chain, y_other, x_near, x_far, sibling):
        greet(device)
    greet(z_up)
    greet(z_dn)

    def send(src, dst, ssem, rsem, device):
        pltpu.make_async_remote_copy(
            src_ref=src, dst_ref=dst, send_sem=ssem, recv_sem=rsem, device_id=device, device_id_type=MESH
        ).start()

    def drain(ref, sem):
        pltpu.make_async_copy(ref, ref, sem).wait()

    def turned(ref):
        return ref[...].astype(jnp.float32).T.astype(jnp.bfloat16)

    drain(cot.at[0], cot_sem.at[0])
    own[0] = turned(cot.at[0])
    drain(cot.at[1], cot_sem.at[1])
    own[2] = turned(cot.at[1])

    pl.semaphore_wait(barrier, 10 - one_is_self)

    thin = pl.ds(0, THIN)
    wide = pl.ds(THIN, T - THIN)
    follow_of = {1: 2, 2: 3, 3: 7, 4: 5, 5: 6, 6: 7}

    def zp(i):
        return (z + (0, 7, 6, 5, 1, 2, 3, 4)[i]) % 8

    def spot(i, ysrc):
        return (zp(i) * 2 + ysrc // 2) * 4 + hr * 2

    def hand_out(p, buf, rows, to_two, two):
        mine = own.at[p, rows]
        slot = RELAY + z * 2 + c
        sem = rt_sem.at[p] if rows is thin else relay_sem.at[p, 0, c]

        @pl.when(one_is_self == 1)
        def _():
            load(mine, buf.at[slot, rows], sem)

        @pl.when(one_is_self == 0)
        def _():
            send(mine, buf.at[slot, rows], self_sem.at[p], sem, relay_one)

        send(two.at[rows], buf.at[slot, rows], send_sem.at[p, 0], sem, to_two)

    def gather(p, buf, order):
        def over_plane(i, tile, count, rows, ssem, chain_sem, rest):
            src = buf.at[pl.ds(RELAY + zp(i) * 2 + tile, count), rows]
            dst = buf.at[pl.ds(spot(i, yr) + tile, count), rows]
            send(src, dst, ssem, chain_sem, y_chain)
            send(src, dst, ssem, rest, y_other)
            send(src, dst, ssem, rest, x_near)

            @pl.when(n == 0)
            def _():
                send(src, dst, ssem, rest, x_far)

        def far(i, tile, count, rows, ssem, chain_sem, rest):
            @pl.when(n == 1)
            def _():
                drain(buf.at[pl.ds(0, count), rows], chain_sem)
                part = buf.at[pl.ds(spot(i, yc) + tile, count), rows]
                send(part, part, ssem, rest, x_far)

        def along_z(i, tile, up, follow):
            part = buf.at[RELAY + zp(i) * 2 + tile, wide]
            send(part, part, send_sem.at[p, 1], relay_sem.at[p, follow, tile], z_up if up else z_dn)

        def ring(i, block, up, follow):
            part = buf.at[pl.ds(zp(i) * 8 + block * 4, 4), thin]
            send(part, part, send_sem.at[p, 4], ring_sem.at[p, follow, block], z_up if up else z_dn)

        def thin_task():
            drain(buf.at[pl.ds(0, 2), thin], rt_sem.at[p])
            over_plane(0, 0, 2, thin, send_sem.at[p, 2], thin_sem.at[p, n], thin_sem.at[p, 0])

        def thin_far_task():
            far(0, 0, 2, thin, send_sem.at[p, 2], thin_sem.at[p, 1], thin_sem.at[p, 0])

        def wide_task(i, tile):
            drain(buf.at[0, wide], relay_sem.at[p, i, tile])
            if i == 0:
                along_z(0, tile, True, 1)
                along_z(0, tile, False, 4)
            elif i in (1, 2, 4, 5) or (i, tile) in ((3, 0), (6, 1)):
                along_z(i, tile, i < 4, follow_of[i])
            over_plane(
                i, tile, 1, wide, send_sem.at[p, 3],
                plane_sem.at[p, n * (1 + i * 2 + tile)], plane_sem.at[p, 0],
            )

        def wide_far_task(i, tile):
            far(i, tile, 1, wide, send_sem.at[p, 3], plane_sem.at[p, 1 + i * 2 + tile], plane_sem.at[p, 0])

        def ring_task(i, block):
            if i == 0:
                for cls, count in ((0, 8), (1, 6)):
                    @pl.when(n == cls)
                    def _(count=count):
                        drain(buf.at[pl.ds(0, count), thin], thin_sem.at[p, 0])

                for b in range(2):
                    ring(0, b, True, 1)
                    ring(0, b, False, 4)
                return
            drain(buf.at[pl.ds(0, 4), thin], ring_sem.at[p, i, block])
            if i in (1, 2, 4, 5) or (i, block) in ((3, 0), (6, 1)):
                ring(i, block, i < 4, follow_of[i])

        for name in order.split():
            kind, i, piece = name[0], int(name[1]), int(name[2])
            if kind == "T":
                thin_task()
            elif kind == "t":
                thin_far_task()
            elif kind == "W":
                wide_task(i, piece)
            elif kind == "F":
                wide_far_task(i, piece)
            else:
                ring_task(i, piece)
        for cls, count in ((0, 64), (1, 48)):
            @pl.when(n == cls)
            def _(count=count):
                drain(buf.at[pl.ds(0, count), wide], plane_sem.at[p, 0])

        for block in range(2):
            drain(buf.at[pl.ds(0, 4), thin], ring_sem.at[p, 7, block])

    def part(j):
        return pl.ds(j * CHUNK, CHUNK)

    parts = T // CHUNK

    def products(buf, j):
        rows = part(j)
        total = jnp.zeros((4 * CHUNK, T), jnp.float32)
        for k in range(16):
            row = rows_ref[k]
            col = cols_ref[k] % 4
            alive = k < offs_ref[16]
            tile = buf[((row // 16) % 16) * 4 + row % 4, rows, :]
            picked = [
                jnp.where(jnp.logical_and(col == t, alive), tile, jnp.zeros_like(tile)) for t in range(4)
            ]
            total = total + jnp.dot(
                jnp.concatenate(picked, axis=0), tiles[k], preferred_element_type=jnp.float32
            )
        for t in range(4):
            acc[t, rows, :] = total[t * CHUNK : (t + 1) * CHUNK]

    def swap_cores(p, j):
        rows = part(j)
        for g in range(2):
            send(
                acc.at[g * 2 + 1 - c, rows], core_in.at[p, g, rows],
                ex_send.at[p, j], ex_recv.at[p, j], sibling,
            )

    def await_cores(p, j):
        drain(core_in.at[p, pl.ds(0, 2), part(j)], ex_recv.at[p, j])

    hand_out(0, field0, thin, relay_two_near, own.at[2])
    hand_out(0, field0, wide, relay_two_near, own.at[2])
    gather(0, field0, FIRST_ORDER)
    for i, ref in enumerate((rows_ref, cols_ref, offs_ref)):
        drain(ref, small_sem.at[i])
    drain(tiles, load_sem.at[0])

    def pass_on(j):
        rows = part(j)
        await_cores(0, j)
        chip_out[rows, :] = (acc[other_tile, rows, :] + core_in[0, 1 - hx, rows, :]).astype(jnp.bfloat16)
        send(chip_out.at[rows], chip_in.at[rows], chip_send.at[j], chip_recv.at[j], x_near)

    def close_first(j):
        rows = part(j)
        drain(chip_in.at[rows], chip_recv.at[j])
        own[1, rows, :] = (
            acc[own_tile, rows, :] + core_in[0, hx, rows, :] + chip_in[rows, :].astype(jnp.float32)
        ).astype(jnp.bfloat16)

    for j in range(parts):
        products(field0, j)
        swap_cores(0, j)
        if j >= 2:
            pass_on(j - 2)
    pass_on(parts - 2)
    pass_on(parts - 1)
    for j in range(parts):
        close_first(j)
        hand_out(1, field1, thin if j == 0 else part(j), relay_two, own.at[1])

    gather(1, field1, SECOND_ORDER)
    for j in range(parts):
        drain(core_in.at[0, pl.ds(0, 2), part(j)], ex_send.at[0, j])

    tv = jnp.full((1, T), heat_ref[0], jnp.float32)
    total = 1.0 + tv + tv * tv / 2.0
    coef0 = 1.0 / total
    coef1 = tv / total
    coef2 = (tv * tv / 2.0) / total

    def pair_up(j):
        rows = part(j)
        await_cores(1, j)
        mine = coef2 * (acc[own_tile, rows, :] + core_in[1, hx, rows, :])
        mine += coef0 * own[0, rows, :].astype(jnp.float32) + coef1 * own[1, rows, :].astype(jnp.float32)
        acc[own_tile, rows, :] = mine
        pair_out[0, rows, :] = mine.astype(jnp.bfloat16)
        theirs = coef2 * (acc[other_tile, rows, :] + core_in[1, 1 - hx, rows, :])
        acc[other_tile, rows, :] = theirs
        pair_out[1, rows, :] = theirs.astype(jnp.bfloat16)
        for i in range(2):
            send(pair_out.at[i, rows], pair_in.at[1 - i, rows], pair_send.at[j], pair_recv.at[j], x_near)

    def close_second(j):
        rows = part(j)
        drain(pair_in.at[pl.ds(0, 2), rows], pair_recv.at[j])
        for i, tile in enumerate((own_tile, other_tile)):
            comb[tile, rows, :] = (acc[tile, rows, :] + pair_in[i, rows, :].astype(jnp.float32)).astype(
                jnp.bfloat16
            )
            send(comb.at[tile, rows], comb.at[tile, rows], cb_send, cb_recv, sibling)

    for j in range(parts):
        products(field1, j)
        swap_cores(1, j)
        if j >= 2:
            pair_up(j - 2)
    pair_up(parts - 2)
    pair_up(parts - 1)
    for j in range(parts):
        close_second(j)
    drain(feat, load_sem.at[1])
    drain(weight, load_sem.at[2])
    drain(comb.at[pl.ds(0, 2)], cb_recv)

    partial = jnp.zeros((192, T), jnp.float32)
    for t in range(4):
        partial += lax.dot_general(
            feat[:, t * T : (t + 1) * T], comb[t], (((1,), (1,)), ((), ())),
            preferred_element_type=jnp.float32,
        )
    partial = partial * (1.0 / 256.0)
    for i in range(8):
        piece = partial[i * PIECE : (i + 1) * PIECE]
        gwp[i] = jnp.concatenate([piece[:, :128], piece[:, 128:]], axis=0).astype(jnp.bfloat16)

    for step in range(1, 8):
        place, device = plane_peer(step)
        send(gwp.at[place], g1.at[here], gw_send.at[0], gw_recv.at[0], device)
    g1[here] = gwp[here]

    for t in range(4):
        gf_ref[:, t * T : (t + 1) * T] = jnp.dot(
            weight[...], comb[t], preferred_element_type=jnp.float32
        ).astype(jnp.bfloat16)

    drain(g1.at[pl.ds(0, 7)], gw_recv.at[0])
    s1[...] = functools.reduce(lambda a, b: a + b, [g1[i].astype(jnp.float32) for i in range(8)]).astype(
        jnp.bfloat16
    )
    for step in range(1, 8):
        send(s1, g2.at[z], gw_send.at[1], gw_recv.at[1], z_peer(step)[1])
    g2[z] = s1[...]
    drain(g2.at[pl.ds(0, 7)], gw_recv.at[1])
    s2[...] = functools.reduce(lambda a, b: a + b, [g2[i].astype(jnp.float32) for i in range(8)])
    for step in range(1, 8):
        send(s2, gfin.at[here], gw_send.at[2], gw_recv.at[2], plane_peer(step)[1])
    gfin[here] = s2[...]

    for p, buf in enumerate((field0, field1)):
        @pl.when(one_is_self == 0)
        def _(p=p):
            drain(own.at[p], self_sem.at[p])

        drain(own.at[p], send_sem.at[p, 0])
        drain(buf.at[pl.ds(0, 14), wide], send_sem.at[p, 1])
        drain(buf.at[pl.ds(0, 8), thin], send_sem.at[p, 2])
        drain(buf.at[pl.ds(0, 64), wide], send_sem.at[p, 3])
        drain(buf.at[pl.ds(0, 56), thin], send_sem.at[p, 4])
    for j in range(parts):
        drain(core_in.at[1, pl.ds(0, 2), part(j)], ex_send.at[1, j])
        drain(chip_in.at[part(j)], chip_send.at[j])
        drain(pair_in.at[pl.ds(0, 2), part(j)], pair_send.at[j])
    drain(comb.at[pl.ds(0, 2)], cb_send)

    drain(gfin.at[pl.ds(0, 7)], gw_recv.at[2])
    for i in range(8):
        gw_ref[i * PIECE : (i + 1) * PIECE, :128] = gfin[i, :PIECE, :]
        gw_ref[i * PIECE : (i + 1) * PIECE, 128:] = gfin[i, PIECE:, :]
    for i, ref in enumerate((g1, g2, gfin)):
        drain(ref.at[pl.ds(0, 7)], gw_send.at[i])


def hand_back(gw_in, gf_in, gw_out, gf_out):
    gw_out[...] = gw_in[...]
    gf_out[...] = gf_in[...]


def local(cotangent, features, weight, heat_time, tile_values, tile_row, tile_col, section_offsets):
    vmem = pl.BlockSpec(memory_space=pltpu.VMEM)
    hbm = pl.BlockSpec(memory_space=pltpu.HBM)
    f32, bf16, i32 = jnp.float32, jnp.bfloat16, jnp.int32
    dma = pltpu.SemaphoreType.DMA
    parts = T // CHUNK
    grad_weight, grad_features = pl.pallas_call(
        kernel,
        out_shape=(
            jax.ShapeDtypeStruct((192, T), f32),
            jax.ShapeDtypeStruct((192, 1024), bf16),
        ),
        in_specs=[hbm, hbm, hbm, pl.BlockSpec(memory_space=pltpu.SMEM), hbm, hbm, hbm, hbm],
        out_specs=(vmem, vmem),
        scratch_shapes=[
            pltpu.SMEM((16,), i32), pltpu.SMEM((16,), i32), pltpu.SMEM((17,), i32),
            pltpu.VMEM((2, T, T), bf16),
            pltpu.VMEM((192, 1024), bf16),
            pltpu.VMEM((192, T), bf16),
            pltpu.VMEM((16, T, T), bf16),
            pltpu.VMEM((RELAY + 16, T, T), bf16),
            pltpu.VMEM((RELAY + 16, T, T), bf16),
            pltpu.VMEM((3, T, T), bf16),
            pltpu.VMEM((4, T, T), f32),
            pltpu.VMEM((2, 2, T, T), f32),
            pltpu.VMEM((T, T), bf16),
            pltpu.VMEM((T, T), bf16),
            pltpu.VMEM((2, T, T), bf16),
            pltpu.VMEM((2, T, T), bf16),
            pltpu.VMEM((4, T, T), bf16),
            pltpu.VMEM((8, 2 * PIECE, 128), bf16),
            pltpu.VMEM((8, 2 * PIECE, 128), bf16),
            pltpu.VMEM((2 * PIECE, 128), bf16),
            pltpu.VMEM((8, 2 * PIECE, 128), bf16),
            pltpu.VMEM((2 * PIECE, 128), f32),
            pltpu.VMEM((8, 2 * PIECE, 128), f32),
            dma((3,)), dma((3,)), dma((2,)),
            dma((2,)),
            dma((2, 8, 2)),
            dma((2, 2)),
            dma((2, 17)),
            dma((2, 8, 2)),
            dma((2, 5)),
            dma((2,)),
            dma((2, parts)), dma((2, parts)),
            dma((parts,)), dma((parts,)),
            dma((parts,)), dma((parts,)),
            dma, dma,
            dma((3,)), dma((3,)),
        ],
        compiler_params=pltpu.CompilerParams(
            collective_id=0, has_side_effects=True, vmem_limit_bytes=60 << 20
        ),
        cost_estimate=pl.CostEstimate(flops=4_800_000_000, bytes_accessed=4_000_000, transcendentals=0),
        name="diffuse",
    )(tile_row, tile_col, section_offsets, heat_time, cotangent, features.T, weight, tile_values)
    grad_weight, grad_features = pl.pallas_call(
        hand_back,
        out_shape=(
            jax.ShapeDtypeStruct((192, T), f32),
            jax.ShapeDtypeStruct((192, 1024), bf16),
        ),
        in_specs=[vmem, vmem],
        out_specs=(vmem, vmem),
        name="hand_back",
    )(grad_weight, grad_features)
    return grad_weight, grad_features.T


def solution(mesh):
    in_specs = (
        P("blk", None),
        P("blk", "rep"),
        P("rep", None),
        P(),
        P(("blk", "rep"), None, None),
        P(("blk", "rep")),
        P(("blk", "rep")),
        P(("blk", "rep")),
    )
    out_specs = (P("rep", None), P("blk", "rep"))
    return jax.shard_map(local, mesh=mesh, in_specs=in_specs, out_specs=out_specs, check_vma=False)
```

```python
import functools

import jax
import jax.numpy as jnp
from jax import lax
from jax.experimental import pallas as pl
from jax.experimental.pallas import tpu as pltpu
from jax.sharding import PartitionSpec as P

MESH = pl.DeviceIdType.MESH
T = 256
THIN = 64
CHUNK = THIN
RELAY = 64
PIECE = 24

FIRST_ORDER = " ".join((
    "T00 W00 W01 t00",
    "W10 W41 F00 W11",
    "W40 F01 R00 W20",
    "F10 W51 F40 W21",
    "W50 F41 F11 R11",
    "R40 R10 F51 W30",
    "R41 W61 F20 F21",
    "W31 F50 W60 F30",
    "R20 F61 R51 W70",
    "F31 R21 R50 W71",
    "F60 F70 F71 R31",
    "R61 R30 R60",
))
SECOND_ORDER = " ".join((
    "W01 W00 T00 W41",
    "W10 W11 t00 F01",
    "W51 F00 W40 W20",
    "R00 F41 F10 W61",
    "W30 W21 F40 F20",
    "F51 F11 R40 R10",
    "W50 F30 W71 F61",
    "R11 F21 R41 W70",
    "F50 R50 W31 F71",
    "R20 W60 F70 R51",
    "R21 F31 F60 R30",
    "R61 R60 R31",
))


def xor(a, b):
    return a + b - 2 * a * b


def kernel(
    rows_hbm, cols_hbm, offs_hbm, heat_ref, cot_hbm, feat_hbm, weight_hbm, tiles_hbm,
    gw_ref, gf_ref,
    rows_ref, cols_ref, offs_ref, cot, feat, weight, tiles,
    wide0, thin0, wide1, thin1, own, acc, core_in, chip_out, chip_in, pair_out, pair_in, comb,
    gwp, g1, s1, g2, s2, gfin,
    load_sem, small_sem, cot_sem,
    rt_sem, relay_sem, thin_sem, plane_sem, ring_sem, send_sem, self_sem,
    ex_send, ex_recv, chip_send, chip_recv, pair_send, pair_recv, cb_send, cb_recv, gw_send, gw_recv,
):
    blk = lax.axis_index("blk")
    rep = lax.axis_index("rep")
    z = blk // 8
    y = (blk // 2) % 4
    xh = blk % 2
    xl = rep // 2
    c = rep % 2
    n = xor(c, xh)
    hx = xor(xl, xh)
    own_tile = hx * 2 + c
    other_tile = (1 - hx) * 2 + c

    def dev(xh_, xl_, y_, z_, c_):
        return (z_ * 8 + y_ * 2 + xh_, xl_ * 2 + c_)

    def delta2(xh_, xl_):
        return (1 - xh_) * (3 - xl_) + xh_ * xl_

    relay_one = dev(xh, xl, (y + 1 - xl) % 4, z, 0)
    relay_two = dev(1 - xh, xl, (y + delta2(xh, xl)) % 4, z, 1)
    relay_two_near = dev(1 - xh, 1 - xl, (y + delta2(xh, 1 - xl)) % 4, z, 1)
    one_is_self = xl * (1 - c)

    yr = ((1 - c) * (y - 1 + xl) + c * (y - delta2(1 - xh, xl)) + 4) % 4
    hr = xor(xl, n)
    ey = 2 * hx - 1
    yc = ((1 - c) * (y - ey - 1 + xl) + c * (y - ey - delta2(1 - xh, xl)) + 8) % 4

    z_up = dev(xh, xl, y, (z + 1) % 8, c)
    z_dn = dev(xh, xl, y, (z + 7) % 8, c)
    y_chain = dev(xh, xl, (y + ey + 4) % 4, z, c)
    y_other = dev(xh, xl, (y - ey + 4) % 4, z, c)
    x_near = dev(xh, 1 - xl, y, z, c)
    x_far = dev(1 - xh, 1 - xl, y, z, 1 - c)
    sibling = dev(xh, xl, y, z, 1 - c)
    here = y * 2 + xh

    def plane_peer(step):
        place = (here + step) % 8
        return place, dev(place % 2, xl, place // 2, z, c)

    def z_peer(step):
        zt = (z + step) % 8
        return zt, dev(xh, xl, y, zt, c)

    def load(src, dst, sem):
        pltpu.make_async_copy(src, dst, sem).start()

    for i, tile in enumerate((own_tile, other_tile)):
        load(cot_hbm.at[pl.ds(pl.multiple_of(tile * T, T), T)], cot.at[i], cot_sem.at[i])
    load(rows_hbm, rows_ref, small_sem.at[0])
    load(cols_hbm, cols_ref, small_sem.at[1])
    load(offs_hbm, offs_ref, small_sem.at[2])
    load(tiles_hbm, tiles, load_sem.at[0])
    load(feat_hbm, feat, load_sem.at[1])
    load(weight_hbm, weight, load_sem.at[2])

    barrier = pltpu.get_barrier_semaphore()

    def greet(device):
        pl.semaphore_signal(barrier, inc=1, device_id=device, device_id_type=MESH)

    @pl.when(c == 0)
    def _():
        @pl.when(one_is_self == 0)
        def _():
            greet(dev(xh, xl, yr, z, 0))

        greet(dev(xh, xl, yr, z, 1))

    @pl.when(c == 1)
    def _():
        for core in range(2):
            greet(dev(1 - xh, xl, yr, z, core))
            greet(dev(1 - xh, 1 - xl, yr, z, core))

    for device in (y_chain, y_other, x_near, x_far, sibling):
        greet(device)
    greet(z_up)
    greet(z_dn)

    def send(src, dst, ssem, rsem, device):
        pltpu.make_async_remote_copy(
            src_ref=src, dst_ref=dst, send_sem=ssem, recv_sem=rsem, device_id=device, device_id_type=MESH
        ).start()

    def drain(ref, sem):
        pltpu.make_async_copy(ref, ref, sem).wait()

    def turned(ref):
        return ref[...].astype(jnp.float32).T.astype(jnp.bfloat16)

    drain(cot.at[0], cot_sem.at[0])
    own[0] = turned(cot.at[0])
    drain(cot.at[1], cot_sem.at[1])
    own[2] = turned(cot.at[1])

    pl.semaphore_wait(barrier, 10 - one_is_self)

    parts = T // CHUNK

    def part(j):
        return pl.ds(j * CHUNK, CHUNK)

    follow_of = {1: 2, 2: 3, 3: 7, 4: 5, 5: 6, 6: 7}

    def zp(i):
        return (z + (0, 7, 6, 5, 1, 2, 3, 4)[i]) % 8

    def spot(i, ysrc):
        return (zp(i) * 2 + ysrc // 2) * 4 + hr * 2

    def hand_out(p, thin_buf, wide_buf, j, to_two, two):
        mine = own.at[p, part(j)]
        slot = RELAY + z * 2 + c
        if j == 0:
            place, sem = thin_buf.at[slot], rt_sem.at[p]
        else:
            place, sem = wide_buf.at[slot, part(j - 1)], relay_sem.at[p, 0, c]

        @pl.when(one_is_self == 1)
        def _():
            load(mine, place, sem)

        @pl.when(one_is_self == 0)
        def _():
            send(mine, place, self_sem.at[p], sem, relay_one)

        send(two.at[part(j)], place, send_sem.at[p, 0], sem, to_two)

    def gather(p, thin_buf, wide_buf, order):
        def over_plane(buf, i, tile, count, ssem, chain_sem, rest):
            src = buf.at[pl.ds(RELAY + zp(i) * 2 + tile, count)]
            dst = buf.at[pl.ds(spot(i, yr) + tile, count)]
            send(src, dst, ssem, chain_sem, y_chain)
            send(src, dst, ssem, rest, y_other)
            send(src, dst, ssem, rest, x_near)

            @pl.when(n == 0)
            def _():
                send(src, dst, ssem, rest, x_far)

        def far(buf, i, tile, count, ssem, chain_sem, rest):
            @pl.when(n == 1)
            def _():
                drain(buf.at[pl.ds(0, count)], chain_sem)
                place = buf.at[pl.ds(spot(i, yc) + tile, count)]
                send(place, place, ssem, rest, x_far)

        def along_z(i, tile, up, follow):
            place = wide_buf.at[RELAY + zp(i) * 2 + tile]
            send(place, place, send_sem.at[p, 1], relay_sem.at[p, follow, tile], z_up if up else z_dn)

        def ring(i, block, up, follow):
            place = thin_buf.at[pl.ds(zp(i) * 8 + block * 4, 4)]
            send(place, place, send_sem.at[p, 4], ring_sem.at[p, follow, block], z_up if up else z_dn)

        def thin_task():
            drain(thin_buf.at[pl.ds(0, 2)], rt_sem.at[p])
            over_plane(thin_buf, 0, 0, 2, send_sem.at[p, 2], thin_sem.at[p, n], thin_sem.at[p, 0])

        def thin_far_task():
            far(thin_buf, 0, 0, 2, send_sem.at[p, 2], thin_sem.at[p, 1], thin_sem.at[p, 0])

        def wide_task(i, tile):
            drain(wide_buf.at[0], relay_sem.at[p, i, tile])
            if i == 0:
                along_z(0, tile, True, 1)
                along_z(0, tile, False, 4)
            elif i in (1, 2, 4, 5) or (i, tile) in ((3, 0), (6, 1)):
                along_z(i, tile, i < 4, follow_of[i])
            over_plane(
                wide_buf, i, tile, 1, send_sem.at[p, 3],
                plane_sem.at[p, n * (1 + i * 2 + tile)], plane_sem.at[p, 0],
            )

        def wide_far_task(i, tile):
            far(wide_buf, i, tile, 1, send_sem.at[p, 3], plane_sem.at[p, 1 + i * 2 + tile], plane_sem.at[p, 0])

        def ring_task(i, block):
            if i == 0:
                for cls, count in ((0, 8), (1, 6)):
                    @pl.when(n == cls)
                    def _(count=count):
                        drain(thin_buf.at[pl.ds(0, count)], thin_sem.at[p, 0])

                for b in range(2):
                    ring(0, b, True, 1)
                    ring(0, b, False, 4)
                return
            drain(thin_buf.at[pl.ds(0, 4)], ring_sem.at[p, i, block])
            if i in (1, 2, 4, 5) or (i, block) in ((3, 0), (6, 1)):
                ring(i, block, i < 4, follow_of[i])

        for name in order.split():
            kind, i, piece = name[0], int(name[1]), int(name[2])
            if kind == "T":
                thin_task()
            elif kind == "t":
                thin_far_task()
            elif kind == "W":
                wide_task(i, piece)
            elif kind == "F":
                wide_far_task(i, piece)
            else:
                ring_task(i, piece)
        for cls, count in ((0, 64), (1, 48)):
            @pl.when(n == cls)
            def _(count=count):
                drain(wide_buf.at[pl.ds(0, count)], plane_sem.at[p, 0])

    def last_thin(p, thin_buf):
        for block in range(2):
            drain(thin_buf.at[pl.ds(0, 4)], ring_sem.at[p, 7, block])

    def products(thin_buf, wide_buf, j):
        rows = part(j)
        total = jnp.zeros((4 * CHUNK, T), jnp.float32)
        for k in range(16):
            row = rows_ref[k]
            col = cols_ref[k] % 4
            alive = k < offs_ref[16]
            index = ((row // 16) % 16) * 4 + row % 4
            tile = thin_buf[index] if j == 0 else wide_buf[index, part(j - 1), :]
            picked = [
                jnp.where(jnp.logical_and(col == t, alive), tile, jnp.zeros_like(tile)) for t in range(4)
            ]
            total = total + jnp.dot(
                jnp.concatenate(picked, axis=0), tiles[k], preferred_element_type=jnp.float32
            )
        for t in range(4):
            acc[t, rows, :] = total[t * CHUNK : (t + 1) * CHUNK]

    def swap_cores(p, j):
        rows = part(j)
        for g in range(2):
            send(
                acc.at[g * 2 + 1 - c, rows], core_in.at[p, g, rows],
                ex_send.at[p, j], ex_recv.at[p, j], sibling,
            )

    def await_cores(p, j):
        drain(core_in.at[p, pl.ds(0, 2), part(j)], ex_recv.at[p, j])

    for j in range(parts):
        hand_out(0, thin0, wide0, j, relay_two_near, own.at[2])
    gather(0, thin0, wide0, FIRST_ORDER)
    for i, ref in enumerate((rows_ref, cols_ref, offs_ref)):
        drain(ref, small_sem.at[i])
    drain(tiles, load_sem.at[0])

    def pass_on(j):
        rows = part(j)
        await_cores(0, j)
        chip_out[rows, :] = (acc[other_tile, rows, :] + core_in[0, 1 - hx, rows, :]).astype(jnp.bfloat16)
        send(chip_out.at[rows], chip_in.at[rows], chip_send.at[j], chip_recv.at[j], x_near)

    def close_first(j):
        rows = part(j)
        drain(chip_in.at[rows], chip_recv.at[j])
        own[1, rows, :] = (
            acc[own_tile, rows, :] + core_in[0, hx, rows, :] + chip_in[rows, :].astype(jnp.float32)
        ).astype(jnp.bfloat16)

    for j in range(1, parts):
        products(thin0, wide0, j)
        swap_cores(0, j)
    for j in range(1, parts):
        pass_on(j)
    last_thin(0, thin0)
    products(thin0, wide0, 0)
    swap_cores(0, 0)
    for j in range(1, parts):
        close_first(j)
        hand_out(1, thin1, wide1, j, relay_two, own.at[1])
    pass_on(0)
    close_first(0)
    hand_out(1, thin1, wide1, 0, relay_two, own.at[1])

    gather(1, thin1, wide1, SECOND_ORDER)
    for j in range(parts):
        drain(core_in.at[0, pl.ds(0, 2), part(j)], ex_send.at[0, j])

    tv = jnp.full((1, T), heat_ref[0], jnp.float32)
    total = 1.0 + tv + tv * tv / 2.0
    coef0 = 1.0 / total
    coef1 = tv / total
    coef2 = (tv * tv / 2.0) / total

    def pair_up(j):
        rows = part(j)
        await_cores(1, j)
        mine = coef2 * (acc[own_tile, rows, :] + core_in[1, hx, rows, :])
        mine += coef0 * own[0, rows, :].astype(jnp.float32) + coef1 * own[1, rows, :].astype(jnp.float32)
        acc[own_tile, rows, :] = mine
        pair_out[0, rows, :] = mine.astype(jnp.bfloat16)
        theirs = coef2 * (acc[other_tile, rows, :] + core_in[1, 1 - hx, rows, :])
        acc[other_tile, rows, :] = theirs
        pair_out[1, rows, :] = theirs.astype(jnp.bfloat16)
        for i in range(2):
            send(pair_out.at[i, rows], pair_in.at[1 - i, rows], pair_send.at[j], pair_recv.at[j], x_near)

    def close_second(j):
        rows = part(j)
        drain(pair_in.at[pl.ds(0, 2), rows], pair_recv.at[j])
        for i, tile in enumerate((own_tile, other_tile)):
            comb[tile, rows, :] = (acc[tile, rows, :] + pair_in[i, rows, :].astype(jnp.float32)).astype(
                jnp.bfloat16
            )
            send(comb.at[tile, rows], comb.at[tile, rows], cb_send, cb_recv, sibling)

    for j in range(1, parts):
        products(thin1, wide1, j)
        swap_cores(1, j)
    for j in range(1, parts):
        pair_up(j)
    last_thin(1, thin1)
    products(thin1, wide1, 0)
    swap_cores(1, 0)
    for j in range(1, parts):
        close_second(j)
    pair_up(0)
    close_second(0)
    drain(feat, load_sem.at[1])
    drain(weight, load_sem.at[2])
    drain(comb.at[pl.ds(0, 2)], cb_recv)

    partial = jnp.zeros((192, T), jnp.float32)
    for t in range(4):
        partial += lax.dot_general(
            feat[:, t * T : (t + 1) * T], comb[t], (((1,), (1,)), ((), ())),
            preferred_element_type=jnp.float32,
        )
    partial = partial * (1.0 / 256.0)
    for i in range(8):
        piece = partial[i * PIECE : (i + 1) * PIECE]
        gwp[i] = jnp.concatenate([piece[:, :128], piece[:, 128:]], axis=0).astype(jnp.bfloat16)

    for step in range(1, 8):
        place, device = plane_peer(step)
        send(gwp.at[place], g1.at[here], gw_send.at[0], gw_recv.at[0], device)
    g1[here] = gwp[here]

    for t in range(4):
        gf_ref[:, t * T : (t + 1) * T] = jnp.dot(
            weight[...], comb[t], preferred_element_type=jnp.float32
        ).astype(jnp.bfloat16)

    drain(g1.at[pl.ds(0, 7)], gw_recv.at[0])
    s1[...] = functools.reduce(lambda a, b: a + b, [g1[i].astype(jnp.float32) for i in range(8)]).astype(
        jnp.bfloat16
    )
    for step in range(1, 8):
        send(s1, g2.at[z], gw_send.at[1], gw_recv.at[1], z_peer(step)[1])
    g2[z] = s1[...]
    drain(g2.at[pl.ds(0, 7)], gw_recv.at[1])
    s2[...] = functools.reduce(lambda a, b: a + b, [g2[i].astype(jnp.float32) for i in range(8)])
    for step in range(1, 8):
        send(s2, gfin.at[here], gw_send.at[2], gw_recv.at[2], plane_peer(step)[1])
    gfin[here] = s2[...]

    for p, (thin_buf, wide_buf) in enumerate(((thin0, wide0), (thin1, wide1))):
        @pl.when(one_is_self == 0)
        def _(p=p):
            drain(own.at[p], self_sem.at[p])

        drain(own.at[p], send_sem.at[p, 0])
        drain(wide_buf.at[pl.ds(0, 14)], send_sem.at[p, 1])
        drain(thin_buf.at[pl.ds(0, 8)], send_sem.at[p, 2])
        drain(wide_buf.at[pl.ds(0, 64)], send_sem.at[p, 3])
        drain(thin_buf.at[pl.ds(0, 56)], send_sem.at[p, 4])
    for j in range(parts):
        drain(core_in.at[1, pl.ds(0, 2), part(j)], ex_send.at[1, j])
        drain(chip_in.at[part(j)], chip_send.at[j])
        drain(pair_in.at[pl.ds(0, 2), part(j)], pair_send.at[j])
    drain(comb.at[pl.ds(0, 2)], cb_send)

    drain(gfin.at[pl.ds(0, 7)], gw_recv.at[2])
    for i in range(8):
        gw_ref[i * PIECE : (i + 1) * PIECE, :128] = gfin[i, :PIECE, :]
        gw_ref[i * PIECE : (i + 1) * PIECE, 128:] = gfin[i, PIECE:, :]
    for i, ref in enumerate((g1, g2, gfin)):
        drain(ref.at[pl.ds(0, 7)], gw_send.at[i])


def hand_back(gw_in, gf_in, gw_out, gf_out):
    gw_out[...] = gw_in[...]
    gf_out[...] = gf_in[...]


def local(cotangent, features, weight, heat_time, tile_values, tile_row, tile_col, section_offsets):
    vmem = pl.BlockSpec(memory_space=pltpu.VMEM)
    hbm = pl.BlockSpec(memory_space=pltpu.HBM)
    f32, bf16, i32 = jnp.float32, jnp.bfloat16, jnp.int32
    dma = pltpu.SemaphoreType.DMA
    parts = T // CHUNK
    grad_weight, grad_features = pl.pallas_call(
        kernel,
        out_shape=(
            jax.ShapeDtypeStruct((192, T), f32),
            jax.ShapeDtypeStruct((192, 1024), bf16),
        ),
        in_specs=[hbm, hbm, hbm, pl.BlockSpec(memory_space=pltpu.SMEM), hbm, hbm, hbm, hbm],
        out_specs=(vmem, vmem),
        scratch_shapes=[
            pltpu.SMEM((16,), i32), pltpu.SMEM((16,), i32), pltpu.SMEM((17,), i32),
            pltpu.VMEM((2, T, T), bf16),
            pltpu.VMEM((192, 1024), bf16),
            pltpu.VMEM((192, T), bf16),
            pltpu.VMEM((16, T, T), bf16),
            pltpu.VMEM((RELAY + 16, T - THIN, T), bf16),
            pltpu.VMEM((RELAY + 16, THIN, T), bf16),
            pltpu.VMEM((RELAY + 16, T - THIN, T), bf16),
            pltpu.VMEM((RELAY + 16, THIN, T), bf16),
            pltpu.VMEM((3, T, T), bf16),
            pltpu.VMEM((4, T, T), f32),
            pltpu.VMEM((2, 2, T, T), f32),
            pltpu.VMEM((T, T), bf16),
            pltpu.VMEM((T, T), bf16),
            pltpu.VMEM((2, T, T), bf16),
            pltpu.VMEM((2, T, T), bf16),
            pltpu.VMEM((4, T, T), bf16),
            pltpu.VMEM((8, 2 * PIECE, 128), bf16),
            pltpu.VMEM((8, 2 * PIECE, 128), bf16),
            pltpu.VMEM((2 * PIECE, 128), bf16),
            pltpu.VMEM((8, 2 * PIECE, 128), bf16),
            pltpu.VMEM((2 * PIECE, 128), f32),
            pltpu.VMEM((8, 2 * PIECE, 128), f32),
            dma((3,)), dma((3,)), dma((2,)),
            dma((2,)),
            dma((2, 8, 2)),
            dma((2, 2)),
            dma((2, 17)),
            dma((2, 8, 2)),
            dma((2, 5)),
            dma((2,)),
            dma((2, parts)), dma((2, parts)),
            dma((parts,)), dma((parts,)),
            dma((parts,)), dma((parts,)),
            dma, dma,
            dma((3,)), dma((3,)),
        ],
        compiler_params=pltpu.CompilerParams(
            collective_id=0, has_side_effects=True, vmem_limit_bytes=60 << 20
        ),
        cost_estimate=pl.CostEstimate(flops=4_800_000_000, bytes_accessed=4_000_000, transcendentals=0),
        name="diffuse",
    )(tile_row, tile_col, section_offsets, heat_time, cotangent, features.T, weight, tile_values)
    grad_weight, grad_features = pl.pallas_call(
        hand_back,
        out_shape=(
            jax.ShapeDtypeStruct((192, T), f32),
            jax.ShapeDtypeStruct((192, 1024), bf16),
        ),
        in_specs=[vmem, vmem],
        out_specs=(vmem, vmem),
        name="hand_back",
    )(grad_weight, grad_features)
    return grad_weight, grad_features.T


def solution(mesh):
    in_specs = (
        P("blk", None),
        P("blk", "rep"),
        P("rep", None),
        P(),
        P(("blk", "rep"), None, None),
        P(("blk", "rep")),
        P(("blk", "rep")),
        P(("blk", "rep")),
    )
    out_specs = (P("rep", None), P("blk", "rep"))
    return jax.shard_map(local, mesh=mesh, in_specs=in_specs, out_specs=out_specs, check_vma=False)
```

```python
import functools

import jax
import jax.numpy as jnp
from jax import lax
from jax.experimental import pallas as pl
from jax.experimental.pallas import tpu as pltpu
from jax.sharding import PartitionSpec as P

MESH = pl.DeviceIdType.MESH
T = 256
THIN = 80
BOUNDS = (0, 80, 160, 256)
RELAY = 64
PLANE_STEPS = (3, 5, 1, 7, 4, 2, 6)
Z_STEPS = (4, 3, 5, 2, 6, 1, 7)
PIECE = 24

FIRST_ORDER = " ".join((
    "T00 W01 P01 W00",
    "P00 t00 W41 F01",
    "W11 W10 W40 P41",
    "P10 P11 P40 F00",
    "R00 F41 F40 W20",
    "W50 W51 P51 F11",
    "P50 W21 F10 P20",
    "P21 R41 R10 W30",
    "P30 W61 F21 P61",
    "W60 R40 F20 F51",
    "P60 F50 W31 R11",
    "P31 W71 P71 R20",
    "F30 F61 R51 R50",
    "W70 F60 P70 F31",
    "R21 F71 F70 R60",
    "R61 R30 R31",
))
SECOND_ORDER = " ".join((
    "W01 W00 P01 T00",
    "W11 W41 P41 W40",
    "W10 P10 F01 P00",
    "W51 W21 t00 F10",
    "P21 P40 W50 W20",
    "R00 F41 F00 P20",
    "P51 F21 F40 W30",
    "W61 P30 W60 P60",
    "W31 R10 R41 F20",
    "R40 R11 F51 P61",
    "P11 F30 P31 W70",
    "F60 F61 P70 R51",
    "F11 P50 W71 R21",
    "R50 P71 R20 F31",
    "F70 F50 F71 R31",
    "R60 R61 R30",
))


def xor(a, b):
    return a + b - 2 * a * b


def kernel(
    rows_hbm, cols_hbm, offs_hbm, heat_ref, cot_hbm, feat_hbm, weight_hbm, tiles_hbm,
    gw_ref, gf_ref,
    rows_ref, cols_ref, offs_ref, cot, feat, weight, tiles,
    wide0, thin0, wide1, thin1, own, acc, core_in, chip_out, chip_in, pair_out, pair_in, comb,
    gwp, g1, s1, g2, s2, gfin,
    load_sem, small_sem, cot_sem,
    rt_sem, relay_sem, thin_sem, plane_sem, ring_sem, send_sem, self_sem,
    ex_send, ex_recv, chip_send, chip_recv, pair_send, pair_recv, cb_send, cb_recv, gw_send, gw_recv,
):
    blk = lax.axis_index("blk")
    rep = lax.axis_index("rep")
    z = blk // 8
    y = (blk // 2) % 4
    xh = blk % 2
    xl = rep // 2
    c = rep % 2
    n = xor(c, xh)
    hx = xor(xl, xh)
    own_tile = hx * 2 + c
    other_tile = (1 - hx) * 2 + c

    def dev(xh_, xl_, y_, z_, c_):
        return (z_ * 8 + y_ * 2 + xh_, xl_ * 2 + c_)

    def delta2(xh_, xl_):
        return (1 - xh_) * (3 - xl_) + xh_ * xl_

    relay_one = dev(xh, xl, (y + 1 - xl) % 4, z, 0)
    relay_two = dev(1 - xh, xl, (y + delta2(xh, xl)) % 4, z, 1)
    relay_two_near = dev(1 - xh, 1 - xl, (y + delta2(xh, 1 - xl)) % 4, z, 1)
    one_is_self = xl * (1 - c)

    yr = ((1 - c) * (y - 1 + xl) + c * (y - delta2(1 - xh, xl)) + 4) % 4
    hr = xor(xl, n)
    ey = 2 * hx - 1
    yc = ((1 - c) * (y - ey - 1 + xl) + c * (y - ey - delta2(1 - xh, xl)) + 8) % 4

    z_up = dev(xh, xl, y, (z + 1) % 8, c)
    z_dn = dev(xh, xl, y, (z + 7) % 8, c)
    y_chain = dev(xh, xl, (y + ey + 4) % 4, z, c)
    y_other = dev(xh, xl, (y - ey + 4) % 4, z, c)
    x_near = dev(xh, 1 - xl, y, z, c)
    x_far = dev(1 - xh, 1 - xl, y, z, 1 - c)
    sibling = dev(xh, xl, y, z, 1 - c)
    here = y * 2 + xh

    def plane_peer(step):
        place = (here + step) % 8
        return place, dev(place % 2, xl, place // 2, z, c)

    def z_peer(step):
        zt = (z + step) % 8
        return zt, dev(xh, xl, y, zt, c)

    def load(src, dst, sem):
        pltpu.make_async_copy(src, dst, sem).start()

    for i, tile in enumerate((own_tile, other_tile)):
        load(cot_hbm.at[pl.ds(pl.multiple_of(tile * T, T), T)], cot.at[i], cot_sem.at[i])
    load(rows_hbm, rows_ref, small_sem.at[0])
    load(cols_hbm, cols_ref, small_sem.at[1])
    load(offs_hbm, offs_ref, small_sem.at[2])
    load(tiles_hbm, tiles, load_sem.at[0])
    load(feat_hbm, feat, load_sem.at[1])
    load(weight_hbm, weight, load_sem.at[2])

    barrier = pltpu.get_barrier_semaphore()

    def greet(device):
        pl.semaphore_signal(barrier, inc=1, device_id=device, device_id_type=MESH)

    @pl.when(c == 0)
    def _():
        @pl.when(one_is_self == 0)
        def _():
            greet(dev(xh, xl, yr, z, 0))

        greet(dev(xh, xl, yr, z, 1))

    @pl.when(c == 1)
    def _():
        for core in range(2):
            greet(dev(1 - xh, xl, yr, z, core))
            greet(dev(1 - xh, 1 - xl, yr, z, core))

    for device in (y_chain, y_other, x_near, x_far, sibling):
        greet(device)
    greet(z_up)
    greet(z_dn)

    def send(src, dst, ssem, rsem, device):
        pltpu.make_async_remote_copy(
            src_ref=src, dst_ref=dst, send_sem=ssem, recv_sem=rsem, device_id=device, device_id_type=MESH
        ).start()

    def drain(ref, sem):
        pltpu.make_async_copy(ref, ref, sem).wait()

    def turned(ref):
        return ref[...].astype(jnp.float32).T.astype(jnp.bfloat16)

    drain(cot.at[0], cot_sem.at[0])
    own[0] = turned(cot.at[0])
    drain(cot.at[1], cot_sem.at[1])
    own[2] = turned(cot.at[1])

    pl.semaphore_wait(barrier, 10 - one_is_self)

    parts = len(BOUNDS) - 1

    def part(j):
        return pl.ds(BOUNDS[j], BOUNDS[j + 1] - BOUNDS[j])

    def wide_part(j):
        return pl.ds(BOUNDS[j] - THIN, BOUNDS[j + 1] - BOUNDS[j])

    follow_of = {1: 2, 2: 3, 3: 7, 4: 5, 5: 6, 6: 7}

    def zp(i):
        return (z + (0, 7, 6, 5, 1, 2, 3, 4)[i]) % 8

    def spot(i, ysrc):
        return (zp(i) * 2 + ysrc // 2) * 4 + hr * 2

    def hand_out(p, thin_buf, wide_buf, j, to_two, two):
        mine = own.at[p, part(j)]
        slot = RELAY + z * 2 + c
        if j == 0:
            place, sem = thin_buf.at[slot], rt_sem.at[p]
        else:
            place, sem = wide_buf.at[slot, wide_part(j)], relay_sem.at[p, 0, c]

        @pl.when(one_is_self == 1)
        def _():
            load(mine, place, sem)

        @pl.when(one_is_self == 0)
        def _():
            send(mine, place, self_sem.at[p], sem, relay_one)

        send(two.at[part(j)], place, send_sem.at[p, 0], sem, to_two)

    def gather(p, thin_buf, wide_buf, order):
        def over_plane(buf, i, tile, count, ssem, chain_sem, rest):
            src = buf.at[pl.ds(RELAY + zp(i) * 2 + tile, count)]
            dst = buf.at[pl.ds(spot(i, yr) + tile, count)]
            send(src, dst, ssem, chain_sem, y_chain)
            send(src, dst, ssem, rest, y_other)
            send(src, dst, ssem, rest, x_near)

            @pl.when(n == 0)
            def _():
                send(src, dst, ssem, rest, x_far)

        def far(buf, i, tile, count, ssem, chain_sem, rest):
            @pl.when(n == 1)
            def _():
                drain(buf.at[pl.ds(0, count)], chain_sem)
                place = buf.at[pl.ds(spot(i, yc) + tile, count)]
                send(place, place, ssem, rest, x_far)

        def along_z(i, tile, up, follow):
            place = wide_buf.at[RELAY + zp(i) * 2 + tile]
            send(place, place, send_sem.at[p, 1], relay_sem.at[p, follow, tile], z_up if up else z_dn)

        def ring(i, block, up, follow):
            place = thin_buf.at[pl.ds(zp(i) * 8 + block * 4, 4)]
            send(place, place, send_sem.at[p, 4], ring_sem.at[p, follow, block], z_up if up else z_dn)

        def thin_task():
            drain(thin_buf.at[pl.ds(0, 2)], rt_sem.at[p])
            over_plane(thin_buf, 0, 0, 2, send_sem.at[p, 2], thin_sem.at[p, n], thin_sem.at[p, 0])

        def thin_far_task():
            far(thin_buf, 0, 0, 2, send_sem.at[p, 2], thin_sem.at[p, 1], thin_sem.at[p, 0])

        def wide_task(i, tile):
            drain(wide_buf.at[0], relay_sem.at[p, i, tile])
            if i == 0:
                along_z(0, tile, True, 1)
                along_z(0, tile, False, 4)
            elif i in (1, 2, 4, 5) or (i, tile) in ((3, 0), (6, 1)):
                along_z(i, tile, i < 4, follow_of[i])

        def wide_plane_task(i, tile):
            over_plane(
                wide_buf, i, tile, 1, send_sem.at[p, 3],
                plane_sem.at[p, n * (1 + i * 2 + tile)], plane_sem.at[p, 0],
            )

        def wide_far_task(i, tile):
            far(wide_buf, i, tile, 1, send_sem.at[p, 3], plane_sem.at[p, 1 + i * 2 + tile], plane_sem.at[p, 0])

        def ring_task(i, block):
            if i == 0:
                for cls, count in ((0, 8), (1, 6)):
                    @pl.when(n == cls)
                    def _(count=count):
                        drain(thin_buf.at[pl.ds(0, count)], thin_sem.at[p, 0])

                for b in range(2):
                    ring(0, b, True, 1)
                    ring(0, b, False, 4)
                return
            drain(thin_buf.at[pl.ds(0, 4)], ring_sem.at[p, i, block])
            if i in (1, 2, 4, 5) or (i, block) in ((3, 0), (6, 1)):
                ring(i, block, i < 4, follow_of[i])

        for name in order.split():
            kind, i, piece = name[0], int(name[1]), int(name[2])
            if kind == "T":
                thin_task()
            elif kind == "t":
                thin_far_task()
            elif kind == "W":
                wide_task(i, piece)
            elif kind == "P":
                wide_plane_task(i, piece)
            elif kind == "F":
                wide_far_task(i, piece)
            else:
                ring_task(i, piece)
        for cls, count in ((0, 64), (1, 48)):
            @pl.when(n == cls)
            def _(count=count):
                drain(wide_buf.at[pl.ds(0, count)], plane_sem.at[p, 0])

    def last_thin(p, thin_buf):
        for block in range(2):
            drain(thin_buf.at[pl.ds(0, 4)], ring_sem.at[p, 7, block])

    def products(thin_buf, wide_buf, j):
        rows = part(j)
        size = BOUNDS[j + 1] - BOUNDS[j]
        total = jnp.zeros((4 * size, T), jnp.float32)
        for k in range(16):
            row = rows_ref[k]
            col = cols_ref[k] % 4
            alive = k < offs_ref[16]
            index = ((row // 16) % 16) * 4 + row % 4
            tile = thin_buf[index] if j == 0 else wide_buf[index, wide_part(j), :]
            picked = [
                jnp.where(jnp.logical_and(col == t, alive), tile, jnp.zeros_like(tile)) for t in range(4)
            ]
            total = total + jnp.dot(
                jnp.concatenate(picked, axis=0), tiles[k], preferred_element_type=jnp.float32
            )
        for t in range(4):
            acc[t, rows, :] = total[t * size : (t + 1) * size]

    def swap_cores(p, j):
        rows = part(j)
        for g in range(2):
            send(
                acc.at[g * 2 + 1 - c, rows], core_in.at[p, g, rows],
                ex_send.at[p, j], ex_recv.at[p, j], sibling,
            )

    def await_cores(p, j):
        drain(core_in.at[p, pl.ds(0, 2), part(j)], ex_recv.at[p, j])

    for j in range(parts):
        hand_out(0, thin0, wide0, j, relay_two_near, own.at[2])
    gather(0, thin0, wide0, FIRST_ORDER)
    for i, ref in enumerate((rows_ref, cols_ref, offs_ref)):
        drain(ref, small_sem.at[i])
    drain(tiles, load_sem.at[0])

    def pass_on(j):
        rows = part(j)
        await_cores(0, j)
        chip_out[rows, :] = (acc[other_tile, rows, :] + core_in[0, 1 - hx, rows, :]).astype(jnp.bfloat16)
        send(chip_out.at[rows], chip_in.at[rows], chip_send.at[j], chip_recv.at[j], x_near)

    def close_first(j):
        rows = part(j)
        drain(chip_in.at[rows], chip_recv.at[j])
        own[1, rows, :] = (
            acc[own_tile, rows, :] + core_in[0, hx, rows, :] + chip_in[rows, :].astype(jnp.float32)
        ).astype(jnp.bfloat16)

    for j in range(1, parts):
        products(thin0, wide0, j)
        swap_cores(0, j)
    for j in range(1, parts):
        pass_on(j)
    last_thin(0, thin0)
    products(thin0, wide0, 0)
    swap_cores(0, 0)
    for j in range(1, parts):
        close_first(j)
        hand_out(1, thin1, wide1, j, relay_two, own.at[1])
    pass_on(0)
    close_first(0)
    hand_out(1, thin1, wide1, 0, relay_two, own.at[1])

    gather(1, thin1, wide1, SECOND_ORDER)
    for j in range(parts):
        drain(core_in.at[0, pl.ds(0, 2), part(j)], ex_send.at[0, j])

    tv = jnp.full((1, T), heat_ref[0], jnp.float32)
    total = 1.0 + tv + tv * tv / 2.0
    coef0 = 1.0 / total
    coef1 = tv / total
    coef2 = (tv * tv / 2.0) / total

    def pair_up(j):
        rows = part(j)
        await_cores(1, j)
        mine = coef2 * (acc[own_tile, rows, :] + core_in[1, hx, rows, :])
        mine += coef0 * own[0, rows, :].astype(jnp.float32) + coef1 * own[1, rows, :].astype(jnp.float32)
        acc[own_tile, rows, :] = mine
        pair_out[0, rows, :] = mine.astype(jnp.bfloat16)
        theirs = coef2 * (acc[other_tile, rows, :] + core_in[1, 1 - hx, rows, :])
        acc[other_tile, rows, :] = theirs
        pair_out[1, rows, :] = theirs.astype(jnp.bfloat16)
        for i in range(2):
            send(pair_out.at[i, rows], pair_in.at[1 - i, rows], pair_send.at[j], pair_recv.at[j], x_near)

    def close_second(j):
        rows = part(j)
        drain(pair_in.at[pl.ds(0, 2), rows], pair_recv.at[j])
        for i, tile in enumerate((own_tile, other_tile)):
            comb[tile, rows, :] = (acc[tile, rows, :] + pair_in[i, rows, :].astype(jnp.float32)).astype(
                jnp.bfloat16
            )
            send(comb.at[tile, rows], comb.at[tile, rows], cb_send, cb_recv, sibling)

    for j in range(1, parts):
        products(thin1, wide1, j)
        swap_cores(1, j)
    for j in range(1, parts):
        pair_up(j)
    last_thin(1, thin1)
    products(thin1, wide1, 0)
    swap_cores(1, 0)
    for j in range(1, parts):
        close_second(j)
    pair_up(0)
    close_second(0)
    drain(feat, load_sem.at[1])
    drain(weight, load_sem.at[2])
    drain(comb.at[pl.ds(0, 2)], cb_recv)

    partial = jnp.zeros((192, T), jnp.float32)
    for t in range(4):
        partial += lax.dot_general(
            feat[:, t * T : (t + 1) * T], comb[t], (((1,), (1,)), ((), ())),
            preferred_element_type=jnp.float32,
        )
    partial = partial * (1.0 / 256.0)
    for i in range(8):
        piece = partial[i * PIECE : (i + 1) * PIECE]
        gwp[i] = jnp.concatenate([piece[:, :128], piece[:, 128:]], axis=0).astype(jnp.bfloat16)

    for step in PLANE_STEPS:
        place, device = plane_peer(step)
        send(gwp.at[place], g1.at[here], gw_send.at[0], gw_recv.at[0], device)
    g1[here] = gwp[here]

    for t in range(4):
        gf_ref[:, t * T : (t + 1) * T] = jnp.dot(
            weight[...], comb[t], preferred_element_type=jnp.float32
        ).astype(jnp.bfloat16)

    drain(g1.at[pl.ds(0, 7)], gw_recv.at[0])
    s1[...] = functools.reduce(lambda a, b: a + b, [g1[i].astype(jnp.float32) for i in range(8)]).astype(
        jnp.bfloat16
    )
    for step in Z_STEPS:
        send(s1, g2.at[z], gw_send.at[1], gw_recv.at[1], z_peer(step)[1])
    g2[z] = s1[...]
    drain(g2.at[pl.ds(0, 7)], gw_recv.at[1])
    s2[...] = functools.reduce(lambda a, b: a + b, [g2[i].astype(jnp.float32) for i in range(8)])
    for step in PLANE_STEPS:
        send(s2, gfin.at[here], gw_send.at[2], gw_recv.at[2], plane_peer(step)[1])
    gfin[here] = s2[...]

    for p, (thin_buf, wide_buf) in enumerate(((thin0, wide0), (thin1, wide1))):
        @pl.when(one_is_self == 0)
        def _(p=p):
            drain(own.at[p], self_sem.at[p])

        drain(own.at[p], send_sem.at[p, 0])
        drain(wide_buf.at[pl.ds(0, 14)], send_sem.at[p, 1])
        drain(thin_buf.at[pl.ds(0, 8)], send_sem.at[p, 2])
        drain(wide_buf.at[pl.ds(0, 64)], send_sem.at[p, 3])
        drain(thin_buf.at[pl.ds(0, 56)], send_sem.at[p, 4])
    for j in range(parts):
        drain(core_in.at[1, pl.ds(0, 2), part(j)], ex_send.at[1, j])
        drain(chip_in.at[part(j)], chip_send.at[j])
        drain(pair_in.at[pl.ds(0, 2), part(j)], pair_send.at[j])
    drain(comb.at[pl.ds(0, 2)], cb_send)

    drain(gfin.at[pl.ds(0, 7)], gw_recv.at[2])
    for i in range(8):
        gw_ref[i * PIECE : (i + 1) * PIECE, :128] = gfin[i, :PIECE, :]
        gw_ref[i * PIECE : (i + 1) * PIECE, 128:] = gfin[i, PIECE:, :]
    for i, ref in enumerate((g1, g2, gfin)):
        drain(ref.at[pl.ds(0, 7)], gw_send.at[i])


def hand_back(gw_in, gf_in, gw_out, gf_out):
    gw_out[...] = gw_in[...]
    gf_out[...] = gf_in[...]


def local(cotangent, features, weight, heat_time, tile_values, tile_row, tile_col, section_offsets):
    vmem = pl.BlockSpec(memory_space=pltpu.VMEM)
    hbm = pl.BlockSpec(memory_space=pltpu.HBM)
    f32, bf16, i32 = jnp.float32, jnp.bfloat16, jnp.int32
    dma = pltpu.SemaphoreType.DMA
    parts = len(BOUNDS) - 1
    grad_weight, grad_features = pl.pallas_call(
        kernel,
        out_shape=(
            jax.ShapeDtypeStruct((192, T), f32),
            jax.ShapeDtypeStruct((192, 1024), bf16),
        ),
        in_specs=[hbm, hbm, hbm, pl.BlockSpec(memory_space=pltpu.SMEM), hbm, hbm, hbm, hbm],
        out_specs=(vmem, vmem),
        scratch_shapes=[
            pltpu.SMEM((16,), i32), pltpu.SMEM((16,), i32), pltpu.SMEM((17,), i32),
            pltpu.VMEM((2, T, T), bf16),
            pltpu.VMEM((192, 1024), bf16),
            pltpu.VMEM((192, T), bf16),
            pltpu.VMEM((16, T, T), bf16),
            pltpu.VMEM((RELAY + 16, T - THIN, T), bf16),
            pltpu.VMEM((RELAY + 16, THIN, T), bf16),
            pltpu.VMEM((RELAY + 16, T - THIN, T), bf16),
            pltpu.VMEM((RELAY + 16, THIN, T), bf16),
            pltpu.VMEM((3, T, T), bf16),
            pltpu.VMEM((4, T, T), f32),
            pltpu.VMEM((2, 2, T, T), f32),
            pltpu.VMEM((T, T), bf16),
            pltpu.VMEM((T, T), bf16),
            pltpu.VMEM((2, T, T), bf16),
            pltpu.VMEM((2, T, T), bf16),
            pltpu.VMEM((4, T, T), bf16),
            pltpu.VMEM((8, 2 * PIECE, 128), bf16),
            pltpu.VMEM((8, 2 * PIECE, 128), bf16),
            pltpu.VMEM((2 * PIECE, 128), bf16),
            pltpu.VMEM((8, 2 * PIECE, 128), bf16),
            pltpu.VMEM((2 * PIECE, 128), f32),
            pltpu.VMEM((8, 2 * PIECE, 128), f32),
            dma((3,)), dma((3,)), dma((2,)),
            dma((2,)),
            dma((2, 8, 2)),
            dma((2, 2)),
            dma((2, 17)),
            dma((2, 8, 2)),
            dma((2, 5)),
            dma((2,)),
            dma((2, parts)), dma((2, parts)),
            dma((parts,)), dma((parts,)),
            dma((parts,)), dma((parts,)),
            dma, dma,
            dma((3,)), dma((3,)),
        ],
        compiler_params=pltpu.CompilerParams(
            collective_id=0, has_side_effects=True, vmem_limit_bytes=60 << 20
        ),
        cost_estimate=pl.CostEstimate(flops=4_800_000_000, bytes_accessed=4_000_000, transcendentals=0),
        name="diffuse",
    )(tile_row, tile_col, section_offsets, heat_time, cotangent, features.T, weight, tile_values)
    grad_weight, grad_features = pl.pallas_call(
        hand_back,
        out_shape=(
            jax.ShapeDtypeStruct((192, T), f32),
            jax.ShapeDtypeStruct((192, 1024), bf16),
        ),
        in_specs=[vmem, vmem],
        out_specs=(vmem, vmem),
        name="hand_back",
    )(grad_weight, grad_features)
    return grad_weight, grad_features.T


def solution(mesh):
    in_specs = (
        P("blk", None),
        P("blk", "rep"),
        P("rep", None),
        P(),
        P(("blk", "rep"), None, None),
        P(("blk", "rep")),
        P(("blk", "rep")),
        P(("blk", "rep")),
    )
    out_specs = (P("rep", None), P("blk", "rep"))
    return jax.shard_map(local, mesh=mesh, in_specs=in_specs, out_specs=out_specs, check_vma=False)
```

```python
import functools

import jax
import jax.numpy as jnp
from jax import lax
from jax.experimental import pallas as pl
from jax.experimental.pallas import tpu as pltpu
from jax.sharding import PartitionSpec as P

MESH = pl.DeviceIdType.MESH
T = 256
THIN = 80
BOUNDS = (0, 80, 160, 256)
RELAY = 64
PLANE_STEPS = (3, 5, 1, 7, 4, 2, 6)
Z_STEPS = (4, 3, 5, 2, 6, 1, 7)
PIECE = 24

FIRST_ORDER = " ".join((
    "T00 W01 P01 W00",
    "P00 t00 W41 F01",
    "W11 W10 W40 P41",
    "P10 P11 P40 F00",
    "R00 F41 F40 W20",
    "W50 W51 P51 F11",
    "P50 W21 F10 P20",
    "P21 R41 R10 W30",
    "P30 W61 F21 P61",
    "W60 R40 F20 F51",
    "P60 F50 W31 R11",
    "P31 W71 P71 R20",
    "F30 F61 R51 R50",
    "W70 F60 P70 F31",
    "R21 F71 F70 R60",
    "R61 R30 R31",
))
SECOND_ORDER = " ".join((
    "W01 W00 P01 T00",
    "W11 W41 P41 W40",
    "W10 P10 F01 P00",
    "W51 W21 t00 F10",
    "P21 P40 W50 W20",
    "R00 F41 F00 P20",
    "P51 F21 F40 W30",
    "W61 P30 W60 P60",
    "W31 R10 R41 F20",
    "R40 R11 F51 P61",
    "P11 F30 P31 W70",
    "F60 F61 P70 R51",
    "F11 P50 W71 R21",
    "R50 P71 R20 F31",
    "F70 F50 F71 R31",
    "R60 R61 R30",
))


def xor(a, b):
    return a + b - 2 * a * b


def kernel(
    rows_hbm, cols_hbm, offs_hbm, heat_ref, cot_hbm, feat_hbm, weight_hbm, tiles_hbm,
    gw_ref, gf_ref,
    rows_ref, cols_ref, offs_ref, sorted_ref, ends_ref, sums, cot, feat, weight, tiles,
    wide0, thin0, wide1, thin1, own, acc, core_in, chip_out, chip_in, pair_out, pair_in, comb,
    gwp, g1, s1, g2, s2, gfin,
    load_sem, small_sem, cot_sem,
    rt_sem, relay_sem, thin_sem, plane_sem, ring_sem, send_sem, self_sem,
    ex_send, ex_recv, chip_send, chip_recv, pair_send, pair_recv, cb_send, cb_recv, gw_send, gw_recv,
):
    blk = lax.axis_index("blk")
    rep = lax.axis_index("rep")
    z = blk // 8
    y = (blk // 2) % 4
    xh = blk % 2
    xl = rep // 2
    c = rep % 2
    n = xor(c, xh)
    hx = xor(xl, xh)
    own_tile = hx * 2 + c
    other_tile = (1 - hx) * 2 + c

    def dev(xh_, xl_, y_, z_, c_):
        return (z_ * 8 + y_ * 2 + xh_, xl_ * 2 + c_)

    def delta2(xh_, xl_):
        return (1 - xh_) * (3 - xl_) + xh_ * xl_

    relay_one = dev(xh, xl, (y + 1 - xl) % 4, z, 0)
    relay_two = dev(1 - xh, xl, (y + delta2(xh, xl)) % 4, z, 1)
    relay_two_near = dev(1 - xh, 1 - xl, (y + delta2(xh, 1 - xl)) % 4, z, 1)
    one_is_self = xl * (1 - c)

    yr = ((1 - c) * (y - 1 + xl) + c * (y - delta2(1 - xh, xl)) + 4) % 4
    hr = xor(xl, n)
    ey = 2 * hx - 1
    yc = ((1 - c) * (y - ey - 1 + xl) + c * (y - ey - delta2(1 - xh, xl)) + 8) % 4

    z_up = dev(xh, xl, y, (z + 1) % 8, c)
    z_dn = dev(xh, xl, y, (z + 7) % 8, c)
    y_chain = dev(xh, xl, (y + ey + 4) % 4, z, c)
    y_other = dev(xh, xl, (y - ey + 4) % 4, z, c)
    x_near = dev(xh, 1 - xl, y, z, c)
    x_far = dev(1 - xh, 1 - xl, y, z, 1 - c)
    sibling = dev(xh, xl, y, z, 1 - c)
    here = y * 2 + xh

    def plane_peer(step):
        place = (here + step) % 8
        return place, dev(place % 2, xl, place // 2, z, c)

    def z_peer(step):
        zt = (z + step) % 8
        return zt, dev(xh, xl, y, zt, c)

    def load(src, dst, sem):
        pltpu.make_async_copy(src, dst, sem).start()

    for i, tile in enumerate((own_tile, other_tile)):
        load(cot_hbm.at[pl.ds(pl.multiple_of(tile * T, T), T)], cot.at[i], cot_sem.at[i])
    load(rows_hbm, rows_ref, small_sem.at[0])
    load(cols_hbm, cols_ref, small_sem.at[1])
    load(offs_hbm, offs_ref, small_sem.at[2])
    load(tiles_hbm, tiles, load_sem.at[0])
    load(feat_hbm, feat, load_sem.at[1])
    load(weight_hbm, weight, load_sem.at[2])

    barrier = pltpu.get_barrier_semaphore()

    def greet(device):
        pl.semaphore_signal(barrier, inc=1, device_id=device, device_id_type=MESH)

    @pl.when(c == 0)
    def _():
        @pl.when(one_is_self == 0)
        def _():
            greet(dev(xh, xl, yr, z, 0))

        greet(dev(xh, xl, yr, z, 1))

    @pl.when(c == 1)
    def _():
        for core in range(2):
            greet(dev(1 - xh, xl, yr, z, core))
            greet(dev(1 - xh, 1 - xl, yr, z, core))

    for device in (y_chain, y_other, x_near, x_far, sibling):
        greet(device)
    greet(z_up)
    greet(z_dn)

    def send(src, dst, ssem, rsem, device):
        pltpu.make_async_remote_copy(
            src_ref=src, dst_ref=dst, send_sem=ssem, recv_sem=rsem, device_id=device, device_id_type=MESH
        ).start()

    def drain(ref, sem):
        pltpu.make_async_copy(ref, ref, sem).wait()

    def turned(ref):
        return ref[...].astype(jnp.float32).T.astype(jnp.bfloat16)

    drain(cot.at[0], cot_sem.at[0])
    own[0] = turned(cot.at[0])
    drain(cot.at[1], cot_sem.at[1])
    own[2] = turned(cot.at[1])

    pl.semaphore_wait(barrier, 10 - one_is_self)

    parts = len(BOUNDS) - 1

    def part(j):
        return pl.ds(BOUNDS[j], BOUNDS[j + 1] - BOUNDS[j])

    def wide_part(j):
        return pl.ds(BOUNDS[j] - THIN, BOUNDS[j + 1] - BOUNDS[j])

    follow_of = {1: 2, 2: 3, 3: 7, 4: 5, 5: 6, 6: 7}

    def zp(i):
        return (z + (0, 7, 6, 5, 1, 2, 3, 4)[i]) % 8

    def spot(i, ysrc):
        return (zp(i) * 2 + ysrc // 2) * 4 + hr * 2

    def hand_out(p, thin_buf, wide_buf, j, to_two, two):
        mine = own.at[p, part(j)]
        slot = RELAY + z * 2 + c
        if j == 0:
            place, sem = thin_buf.at[slot], rt_sem.at[p]
        else:
            place, sem = wide_buf.at[slot, wide_part(j)], relay_sem.at[p, 0, c]

        @pl.when(one_is_self == 1)
        def _():
            load(mine, place, sem)

        @pl.when(one_is_self == 0)
        def _():
            send(mine, place, self_sem.at[p], sem, relay_one)

        send(two.at[part(j)], place, send_sem.at[p, 0], sem, to_two)

    def gather(p, thin_buf, wide_buf, order):
        def over_plane(buf, i, tile, count, ssem, chain_sem, rest):
            src = buf.at[pl.ds(RELAY + zp(i) * 2 + tile, count)]
            dst = buf.at[pl.ds(spot(i, yr) + tile, count)]
            send(src, dst, ssem, chain_sem, y_chain)
            send(src, dst, ssem, rest, y_other)
            send(src, dst, ssem, rest, x_near)

            @pl.when(n == 0)
            def _():
                send(src, dst, ssem, rest, x_far)

        def far(buf, i, tile, count, ssem, chain_sem, rest):
            @pl.when(n == 1)
            def _():
                drain(buf.at[pl.ds(0, count)], chain_sem)
                place = buf.at[pl.ds(spot(i, yc) + tile, count)]
                send(place, place, ssem, rest, x_far)

        def along_z(i, tile, up, follow):
            place = wide_buf.at[RELAY + zp(i) * 2 + tile]
            send(place, place, send_sem.at[p, 1], relay_sem.at[p, follow, tile], z_up if up else z_dn)

        def ring(i, block, up, follow):
            place = thin_buf.at[pl.ds(zp(i) * 8 + block * 4, 4)]
            send(place, place, send_sem.at[p, 4], ring_sem.at[p, follow, block], z_up if up else z_dn)

        def thin_task():
            drain(thin_buf.at[pl.ds(0, 2)], rt_sem.at[p])
            over_plane(thin_buf, 0, 0, 2, send_sem.at[p, 2], thin_sem.at[p, n], thin_sem.at[p, 0])

        def thin_far_task():
            far(thin_buf, 0, 0, 2, send_sem.at[p, 2], thin_sem.at[p, 1], thin_sem.at[p, 0])

        def wide_task(i, tile):
            drain(wide_buf.at[0], relay_sem.at[p, i, tile])
            if i == 0:
                along_z(0, tile, True, 1)
                along_z(0, tile, False, 4)
            elif i in (1, 2, 4, 5) or (i, tile) in ((3, 0), (6, 1)):
                along_z(i, tile, i < 4, follow_of[i])

        def wide_plane_task(i, tile):
            over_plane(
                wide_buf, i, tile, 1, send_sem.at[p, 3],
                plane_sem.at[p, n * (1 + i * 2 + tile)], plane_sem.at[p, 0],
            )

        def wide_far_task(i, tile):
            far(wide_buf, i, tile, 1, send_sem.at[p, 3], plane_sem.at[p, 1 + i * 2 + tile], plane_sem.at[p, 0])

        def ring_task(i, block):
            if i == 0:
                for cls, count in ((0, 8), (1, 6)):
                    @pl.when(n == cls)
                    def _(count=count):
                        drain(thin_buf.at[pl.ds(0, count)], thin_sem.at[p, 0])

                for b in range(2):
                    ring(0, b, True, 1)
                    ring(0, b, False, 4)
                return
            drain(thin_buf.at[pl.ds(0, 4)], ring_sem.at[p, i, block])
            if i in (1, 2, 4, 5) or (i, block) in ((3, 0), (6, 1)):
                ring(i, block, i < 4, follow_of[i])

        for name in order.split():
            kind, i, piece = name[0], int(name[1]), int(name[2])
            if kind == "T":
                thin_task()
            elif kind == "t":
                thin_far_task()
            elif kind == "W":
                wide_task(i, piece)
            elif kind == "P":
                wide_plane_task(i, piece)
            elif kind == "F":
                wide_far_task(i, piece)
            else:
                ring_task(i, piece)
        for cls, count in ((0, 64), (1, 48)):
            @pl.when(n == cls)
            def _(count=count):
                drain(wide_buf.at[pl.ds(0, count)], plane_sem.at[p, 0])

    def last_thin(p, thin_buf):
        for block in range(2):
            drain(thin_buf.at[pl.ds(0, 4)], ring_sem.at[p, 7, block])

    def sort_slots():
        keys = [jnp.where(k < offs_ref[16], cols_ref[k] % 4, 4) for k in range(16)]
        ranks = []
        for k in range(16):
            rank = jnp.int32(0)
            for q in range(16):
                if q != k:
                    ahead = keys[q] <= keys[k] if q < k else keys[q] < keys[k]
                    rank = rank + jnp.where(ahead, 1, 0)
            ranks.append(rank)
        for place in range(16):
            slot = jnp.int32(0)
            for k in range(16):
                slot = slot + jnp.where(ranks[k] == place, k, 0)
            sorted_ref[place] = slot
        for t in range(4):
            below = jnp.int32(0)
            for k in range(16):
                below = below + jnp.where(keys[k] <= t, 1, 0)
            ends_ref[t] = below

    def products(thin_buf, wide_buf, j):
        rows = part(j)
        size = BOUNDS[j + 1] - BOUNDS[j]
        total = jnp.zeros((size, T), jnp.float32)
        sums[0, :size, :] = total
        for k in range(16):
            slot = sorted_ref[k] % 16
            row = rows_ref[slot]
            index = ((row // 16) % 16) * 4 + row % 4
            tile = thin_buf[index] if j == 0 else wide_buf[index, wide_part(j), :]
            total = total + jnp.dot(tile, tiles[slot], preferred_element_type=jnp.float32)
            sums[k + 1, :size, :] = total
        for t in range(4):
            upto = sums[ends_ref[t] % 17, :size, :]
            if t > 0:
                upto = upto - sums[ends_ref[t - 1] % 17, :size, :]
            acc[t, rows, :] = upto

    def swap_cores(p, j):
        rows = part(j)
        for g in range(2):
            send(
                acc.at[g * 2 + 1 - c, rows], core_in.at[p, g, rows],
                ex_send.at[p, j], ex_recv.at[p, j], sibling,
            )

    def await_cores(p, j):
        drain(core_in.at[p, pl.ds(0, 2), part(j)], ex_recv.at[p, j])

    for j in range(parts):
        hand_out(0, thin0, wide0, j, relay_two_near, own.at[2])
    for i, ref in enumerate((rows_ref, cols_ref, offs_ref)):
        drain(ref, small_sem.at[i])
    sort_slots()
    gather(0, thin0, wide0, FIRST_ORDER)
    drain(tiles, load_sem.at[0])

    def pass_on(j):
        rows = part(j)
        await_cores(0, j)
        chip_out[rows, :] = (acc[other_tile, rows, :] + core_in[0, 1 - hx, rows, :]).astype(jnp.bfloat16)
        send(chip_out.at[rows], chip_in.at[rows], chip_send.at[j], chip_recv.at[j], x_near)

    def close_first(j):
        rows = part(j)
        drain(chip_in.at[rows], chip_recv.at[j])
        own[1, rows, :] = (
            acc[own_tile, rows, :] + core_in[0, hx, rows, :] + chip_in[rows, :].astype(jnp.float32)
        ).astype(jnp.bfloat16)

    for j in range(1, parts):
        products(thin0, wide0, j)
        swap_cores(0, j)
    for j in range(1, parts):
        pass_on(j)
    last_thin(0, thin0)
    products(thin0, wide0, 0)
    swap_cores(0, 0)
    for j in range(1, parts):
        close_first(j)
        hand_out(1, thin1, wide1, j, relay_two, own.at[1])
    pass_on(0)
    close_first(0)
    hand_out(1, thin1, wide1, 0, relay_two, own.at[1])

    gather(1, thin1, wide1, SECOND_ORDER)
    for j in range(parts):
        drain(core_in.at[0, pl.ds(0, 2), part(j)], ex_send.at[0, j])

    tv = jnp.full((1, T), heat_ref[0], jnp.float32)
    total = 1.0 + tv + tv * tv / 2.0
    coef0 = 1.0 / total
    coef1 = tv / total
    coef2 = (tv * tv / 2.0) / total

    def pair_up(j):
        rows = part(j)
        await_cores(1, j)
        mine = coef2 * (acc[own_tile, rows, :] + core_in[1, hx, rows, :])
        mine += coef0 * own[0, rows, :].astype(jnp.float32) + coef1 * own[1, rows, :].astype(jnp.float32)
        acc[own_tile, rows, :] = mine
        pair_out[0, rows, :] = mine.astype(jnp.bfloat16)
        theirs = coef2 * (acc[other_tile, rows, :] + core_in[1, 1 - hx, rows, :])
        acc[other_tile, rows, :] = theirs
        pair_out[1, rows, :] = theirs.astype(jnp.bfloat16)
        for i in range(2):
            send(pair_out.at[i, rows], pair_in.at[1 - i, rows], pair_send.at[j], pair_recv.at[j], x_near)

    def close_second(j):
        rows = part(j)
        drain(pair_in.at[pl.ds(0, 2), rows], pair_recv.at[j])
        for i, tile in enumerate((own_tile, other_tile)):
            comb[tile, rows, :] = (acc[tile, rows, :] + pair_in[i, rows, :].astype(jnp.float32)).astype(
                jnp.bfloat16
            )
            send(comb.at[tile, rows], comb.at[tile, rows], cb_send, cb_recv, sibling)

    for j in range(1, parts):
        products(thin1, wide1, j)
        swap_cores(1, j)
    for j in range(1, parts):
        pair_up(j)
    last_thin(1, thin1)
    products(thin1, wide1, 0)
    swap_cores(1, 0)
    for j in range(1, parts):
        close_second(j)
    pair_up(0)
    close_second(0)
    drain(feat, load_sem.at[1])
    drain(weight, load_sem.at[2])
    drain(comb.at[pl.ds(0, 2)], cb_recv)

    partial = jnp.zeros((192, T), jnp.float32)
    for t in range(4):
        partial += lax.dot_general(
            feat[:, t * T : (t + 1) * T], comb[t], (((1,), (1,)), ((), ())),
            preferred_element_type=jnp.float32,
        )
    partial = partial * (1.0 / 256.0)
    for i in range(8):
        piece = partial[i * PIECE : (i + 1) * PIECE]
        gwp[i] = jnp.concatenate([piece[:, :128], piece[:, 128:]], axis=0).astype(jnp.bfloat16)

    for step in PLANE_STEPS:
        place, device = plane_peer(step)
        send(gwp.at[place], g1.at[here], gw_send.at[0], gw_recv.at[0], device)
    g1[here] = gwp[here]

    for t in range(4):
        gf_ref[:, t * T : (t + 1) * T] = jnp.dot(
            weight[...], comb[t], preferred_element_type=jnp.float32
        ).astype(jnp.bfloat16)

    drain(g1.at[pl.ds(0, 7)], gw_recv.at[0])
    s1[...] = functools.reduce(lambda a, b: a + b, [g1[i].astype(jnp.float32) for i in range(8)]).astype(
        jnp.bfloat16
    )
    for step in Z_STEPS:
        send(s1, g2.at[z], gw_send.at[1], gw_recv.at[1], z_peer(step)[1])
    g2[z] = s1[...]
    drain(g2.at[pl.ds(0, 7)], gw_recv.at[1])
    s2[...] = functools.reduce(lambda a, b: a + b, [g2[i].astype(jnp.float32) for i in range(8)])
    for step in PLANE_STEPS:
        send(s2, gfin.at[here], gw_send.at[2], gw_recv.at[2], plane_peer(step)[1])
    gfin[here] = s2[...]

    for p, (thin_buf, wide_buf) in enumerate(((thin0, wide0), (thin1, wide1))):
        @pl.when(one_is_self == 0)
        def _(p=p):
            drain(own.at[p], self_sem.at[p])

        drain(own.at[p], send_sem.at[p, 0])
        drain(wide_buf.at[pl.ds(0, 14)], send_sem.at[p, 1])
        drain(thin_buf.at[pl.ds(0, 8)], send_sem.at[p, 2])
        drain(wide_buf.at[pl.ds(0, 64)], send_sem.at[p, 3])
        drain(thin_buf.at[pl.ds(0, 56)], send_sem.at[p, 4])
    for j in range(parts):
        drain(core_in.at[1, pl.ds(0, 2), part(j)], ex_send.at[1, j])
        drain(chip_in.at[part(j)], chip_send.at[j])
        drain(pair_in.at[pl.ds(0, 2), part(j)], pair_send.at[j])
    drain(comb.at[pl.ds(0, 2)], cb_send)

    drain(gfin.at[pl.ds(0, 7)], gw_recv.at[2])
    for i in range(8):
        gw_ref[i * PIECE : (i + 1) * PIECE, :128] = gfin[i, :PIECE, :]
        gw_ref[i * PIECE : (i + 1) * PIECE, 128:] = gfin[i, PIECE:, :]
    for i, ref in enumerate((g1, g2, gfin)):
        drain(ref.at[pl.ds(0, 7)], gw_send.at[i])


def hand_back(gw_in, gf_in, gw_out, gf_out):
    gw_out[...] = gw_in[...]
    gf_out[...] = gf_in[...]


def local(cotangent, features, weight, heat_time, tile_values, tile_row, tile_col, section_offsets):
    vmem = pl.BlockSpec(memory_space=pltpu.VMEM)
    hbm = pl.BlockSpec(memory_space=pltpu.HBM)
    f32, bf16, i32 = jnp.float32, jnp.bfloat16, jnp.int32
    dma = pltpu.SemaphoreType.DMA
    parts = len(BOUNDS) - 1
    grad_weight, grad_features = pl.pallas_call(
        kernel,
        out_shape=(
            jax.ShapeDtypeStruct((192, T), f32),
            jax.ShapeDtypeStruct((192, 1024), bf16),
        ),
        in_specs=[hbm, hbm, hbm, pl.BlockSpec(memory_space=pltpu.SMEM), hbm, hbm, hbm, hbm],
        out_specs=(vmem, vmem),
        scratch_shapes=[
            pltpu.SMEM((16,), i32), pltpu.SMEM((16,), i32), pltpu.SMEM((17,), i32),
            pltpu.SMEM((16,), i32), pltpu.SMEM((4,), i32),
            pltpu.VMEM((17, max(b - a for a, b in zip(BOUNDS, BOUNDS[1:])), T), f32),
            pltpu.VMEM((2, T, T), bf16),
            pltpu.VMEM((192, 1024), bf16),
            pltpu.VMEM((192, T), bf16),
            pltpu.VMEM((16, T, T), bf16),
            pltpu.VMEM((RELAY + 16, T - THIN, T), bf16),
            pltpu.VMEM((RELAY + 16, THIN, T), bf16),
            pltpu.VMEM((RELAY + 16, T - THIN, T), bf16),
            pltpu.VMEM((RELAY + 16, THIN, T), bf16),
            pltpu.VMEM((3, T, T), bf16),
            pltpu.VMEM((4, T, T), f32),
            pltpu.VMEM((2, 2, T, T), f32),
            pltpu.VMEM((T, T), bf16),
            pltpu.VMEM((T, T), bf16),
            pltpu.VMEM((2, T, T), bf16),
            pltpu.VMEM((2, T, T), bf16),
            pltpu.VMEM((4, T, T), bf16),
            pltpu.VMEM((8, 2 * PIECE, 128), bf16),
            pltpu.VMEM((8, 2 * PIECE, 128), bf16),
            pltpu.VMEM((2 * PIECE, 128), bf16),
            pltpu.VMEM((8, 2 * PIECE, 128), bf16),
            pltpu.VMEM((2 * PIECE, 128), f32),
            pltpu.VMEM((8, 2 * PIECE, 128), f32),
            dma((3,)), dma((3,)), dma((2,)),
            dma((2,)),
            dma((2, 8, 2)),
            dma((2, 2)),
            dma((2, 17)),
            dma((2, 8, 2)),
            dma((2, 5)),
            dma((2,)),
            dma((2, parts)), dma((2, parts)),
            dma((parts,)), dma((parts,)),
            dma((parts,)), dma((parts,)),
            dma, dma,
            dma((3,)), dma((3,)),
        ],
        compiler_params=pltpu.CompilerParams(
            collective_id=0, has_side_effects=True, vmem_limit_bytes=60 << 20
        ),
        cost_estimate=pl.CostEstimate(flops=4_800_000_000, bytes_accessed=4_000_000, transcendentals=0),
        name="diffuse",
    )(tile_row, tile_col, section_offsets, heat_time, cotangent, features.T, weight, tile_values)
    grad_weight, grad_features = pl.pallas_call(
        hand_back,
        out_shape=(
            jax.ShapeDtypeStruct((192, T), f32),
            jax.ShapeDtypeStruct((192, 1024), bf16),
        ),
        in_specs=[vmem, vmem],
        out_specs=(vmem, vmem),
        name="hand_back",
    )(grad_weight, grad_features)
    return grad_weight, grad_features.T


def solution(mesh):
    in_specs = (
        P("blk", None),
        P("blk", "rep"),
        P("rep", None),
        P(),
        P(("blk", "rep"), None, None),
        P(("blk", "rep")),
        P(("blk", "rep")),
        P(("blk", "rep")),
    )
    out_specs = (P("rep", None), P("blk", "rep"))
    return jax.shard_map(local, mesh=mesh, in_specs=in_specs, out_specs=out_specs, check_vma=False)
```

```python
import functools

import jax
import jax.numpy as jnp
from jax import lax
from jax.experimental import pallas as pl
from jax.experimental.pallas import tpu as pltpu
from jax.sharding import PartitionSpec as P

MESH = pl.DeviceIdType.MESH
T = 256
THIN = 80
BOUNDS = (0, 80, 160, 256)
RELAY = 64
PLANE_STEPS = (3, 5, 1, 7, 4, 2, 6)
Z_STEPS = (4, 3, 5, 2, 6, 1, 7)
PIECE = 24

FIRST_ORDER = " ".join((
    "T00 W01 P01 W00",
    "P00 t00 W41 F01",
    "W11 W10 W40 P41",
    "P10 P11 P40 F00",
    "R00 F41 F40 W20",
    "W50 W51 P51 F11",
    "P50 W21 F10 P20",
    "P21 R41 R10 W30",
    "P30 W61 F21 P61",
    "W60 R40 F20 F51",
    "P60 F50 W31 R11",
    "P31 W71 P71 R20",
    "F30 F61 R51 R50",
    "W70 F60 P70 F31",
    "R21 F71 F70 R60",
    "R61 R30 R31",
))
SECOND_ORDER = " ".join((
    "W01 W00 P01 T00",
    "W11 W41 P41 W40",
    "W10 P10 F01 P00",
    "W51 W21 t00 F10",
    "P21 P40 W50 W20",
    "R00 F41 F00 P20",
    "P51 F21 F40 W30",
    "W61 P30 W60 P60",
    "W31 R10 R41 F20",
    "R40 R11 F51 P61",
    "P11 F30 P31 W70",
    "F60 F61 P70 R51",
    "F11 P50 W71 R21",
    "R50 P71 R20 F31",
    "F70 F50 F71 R31",
    "R60 R61 R30",
))


def xor(a, b):
    return a + b - 2 * a * b


def kernel(
    rows_hbm, cols_hbm, offs_hbm, heat_ref, cot_hbm, feat_hbm, weight_hbm, tiles_hbm,
    gw_ref, gf_ref,
    rows_ref, cols_ref, offs_ref, sorted_ref, ends_ref, sums, cot, feat, weight, tiles,
    wide0, thin0, wide1, thin1, own, acc, core_in, chip_out, chip_in, pair_out, pair_in, comb,
    gwp, g1, s1, g2, s2, gfin,
    load_sem, small_sem, cot_sem,
    rt_sem, relay_sem, thin_sem, plane_sem, ring_sem, send_sem, self_sem,
    ex_send, ex_recv, chip_send, chip_recv, pair_send, pair_recv, cb_send, cb_recv, gw_send, gw_recv,
):
    blk = lax.axis_index("blk")
    rep = lax.axis_index("rep")
    z = blk // 8
    y = (blk // 2) % 4
    xh = blk % 2
    xl = rep // 2
    c = rep % 2
    n = xor(c, xh)
    hx = xor(xl, xh)
    own_tile = hx * 2 + c
    other_tile = (1 - hx) * 2 + c

    def dev(xh_, xl_, y_, z_, c_):
        return (z_ * 8 + y_ * 2 + xh_, xl_ * 2 + c_)

    def delta2(xh_, xl_):
        return (1 - xh_) * (3 - xl_) + xh_ * xl_

    relay_one = dev(xh, xl, (y + 1 - xl) % 4, z, 0)
    relay_two = dev(1 - xh, xl, (y + delta2(xh, xl)) % 4, z, 1)
    relay_two_near = dev(1 - xh, 1 - xl, (y + delta2(xh, 1 - xl)) % 4, z, 1)
    one_is_self = xl * (1 - c)

    yr = ((1 - c) * (y - 1 + xl) + c * (y - delta2(1 - xh, xl)) + 4) % 4
    hr = xor(xl, n)
    ey = 2 * hx - 1
    yc = ((1 - c) * (y - ey - 1 + xl) + c * (y - ey - delta2(1 - xh, xl)) + 8) % 4

    z_up = dev(xh, xl, y, (z + 1) % 8, c)
    z_dn = dev(xh, xl, y, (z + 7) % 8, c)
    y_chain = dev(xh, xl, (y + ey + 4) % 4, z, c)
    y_other = dev(xh, xl, (y - ey + 4) % 4, z, c)
    x_near = dev(xh, 1 - xl, y, z, c)
    x_far = dev(1 - xh, 1 - xl, y, z, 1 - c)
    sibling = dev(xh, xl, y, z, 1 - c)
    here = y * 2 + xh

    def plane_peer(step):
        place = (here + step) % 8
        return place, dev(place % 2, xl, place // 2, z, c)

    def z_peer(step):
        zt = (z + step) % 8
        return zt, dev(xh, xl, y, zt, c)

    def load(src, dst, sem):
        pltpu.make_async_copy(src, dst, sem).start()

    for i, tile in enumerate((own_tile, other_tile)):
        load(cot_hbm.at[pl.ds(pl.multiple_of(tile * T, T), T)], cot.at[i], cot_sem.at[i])
    load(rows_hbm, rows_ref, small_sem.at[0])
    load(cols_hbm, cols_ref, small_sem.at[1])
    load(offs_hbm, offs_ref, small_sem.at[2])

    barrier = pltpu.get_barrier_semaphore()

    def greet(device):
        pl.semaphore_signal(barrier, inc=1, device_id=device, device_id_type=MESH)

    @pl.when(c == 0)
    def _():
        @pl.when(one_is_self == 0)
        def _():
            greet(dev(xh, xl, yr, z, 0))

        greet(dev(xh, xl, yr, z, 1))

    @pl.when(c == 1)
    def _():
        for core in range(2):
            greet(dev(1 - xh, xl, yr, z, core))
            greet(dev(1 - xh, 1 - xl, yr, z, core))

    for device in (y_chain, y_other, x_near, x_far, sibling):
        greet(device)
    greet(z_up)
    greet(z_dn)

    def send(src, dst, ssem, rsem, device):
        pltpu.make_async_remote_copy(
            src_ref=src, dst_ref=dst, send_sem=ssem, recv_sem=rsem, device_id=device, device_id_type=MESH
        ).start()

    def drain(ref, sem):
        pltpu.make_async_copy(ref, ref, sem).wait()

    def turned(ref):
        return ref[...].astype(jnp.float32).T.astype(jnp.bfloat16)

    drain(cot.at[0], cot_sem.at[0])
    own[0] = turned(cot.at[0])
    drain(cot.at[1], cot_sem.at[1])
    own[2] = turned(cot.at[1])

    pl.semaphore_wait(barrier, 10 - one_is_self)

    parts = len(BOUNDS) - 1

    def part(j):
        return pl.ds(BOUNDS[j], BOUNDS[j + 1] - BOUNDS[j])

    def wide_part(j):
        return pl.ds(BOUNDS[j] - THIN, BOUNDS[j + 1] - BOUNDS[j])

    follow_of = {1: 2, 2: 3, 3: 7, 4: 5, 5: 6, 6: 7}

    def zp(i):
        return (z + (0, 7, 6, 5, 1, 2, 3, 4)[i]) % 8

    def spot(i, ysrc):
        return (zp(i) * 2 + ysrc // 2) * 4 + hr * 2

    def hand_out(p, thin_buf, wide_buf, j, to_two, two):
        mine = own.at[p, part(j)]
        slot = RELAY + z * 2 + c
        if j == 0:
            place, sem = thin_buf.at[slot], rt_sem.at[p]
        else:
            place, sem = wide_buf.at[slot, wide_part(j)], relay_sem.at[p, 0, c]

        @pl.when(one_is_self == 1)
        def _():
            load(mine, place, sem)

        @pl.when(one_is_self == 0)
        def _():
            send(mine, place, self_sem.at[p], sem, relay_one)

        send(two.at[part(j)], place, send_sem.at[p, 0], sem, to_two)

    def gather(p, thin_buf, wide_buf, order):
        def over_plane(buf, i, tile, count, ssem, chain_sem, rest):
            src = buf.at[pl.ds(RELAY + zp(i) * 2 + tile, count)]
            dst = buf.at[pl.ds(spot(i, yr) + tile, count)]
            send(src, dst, ssem, chain_sem, y_chain)
            send(src, dst, ssem, rest, y_other)
            send(src, dst, ssem, rest, x_near)

            @pl.when(n == 0)
            def _():
                send(src, dst, ssem, rest, x_far)

        def far(buf, i, tile, count, ssem, chain_sem, rest):
            @pl.when(n == 1)
            def _():
                drain(buf.at[pl.ds(0, count)], chain_sem)
                place = buf.at[pl.ds(spot(i, yc) + tile, count)]
                send(place, place, ssem, rest, x_far)

        def along_z(i, tile, up, follow):
            place = wide_buf.at[RELAY + zp(i) * 2 + tile]
            send(place, place, send_sem.at[p, 1], relay_sem.at[p, follow, tile], z_up if up else z_dn)

        def ring(i, block, up, follow):
            place = thin_buf.at[pl.ds(zp(i) * 8 + block * 4, 4)]
            send(place, place, send_sem.at[p, 4], ring_sem.at[p, follow, block], z_up if up else z_dn)

        def thin_task():
            drain(thin_buf.at[pl.ds(0, 2)], rt_sem.at[p])
            over_plane(thin_buf, 0, 0, 2, send_sem.at[p, 2], thin_sem.at[p, n], thin_sem.at[p, 0])

        def thin_far_task():
            far(thin_buf, 0, 0, 2, send_sem.at[p, 2], thin_sem.at[p, 1], thin_sem.at[p, 0])

        def wide_task(i, tile):
            drain(wide_buf.at[0], relay_sem.at[p, i, tile])
            if i == 0:
                along_z(0, tile, True, 1)
                along_z(0, tile, False, 4)
            elif i in (1, 2, 4, 5) or (i, tile) in ((3, 0), (6, 1)):
                along_z(i, tile, i < 4, follow_of[i])

        def wide_plane_task(i, tile):
            over_plane(
                wide_buf, i, tile, 1, send_sem.at[p, 3],
                plane_sem.at[p, n * (1 + i * 2 + tile)], plane_sem.at[p, 0],
            )

        def wide_far_task(i, tile):
            far(wide_buf, i, tile, 1, send_sem.at[p, 3], plane_sem.at[p, 1 + i * 2 + tile], plane_sem.at[p, 0])

        def ring_task(i, block):
            if i == 0:
                for cls, count in ((0, 8), (1, 6)):
                    @pl.when(n == cls)
                    def _(count=count):
                        drain(thin_buf.at[pl.ds(0, count)], thin_sem.at[p, 0])

                for b in range(2):
                    ring(0, b, True, 1)
                    ring(0, b, False, 4)
                return
            drain(thin_buf.at[pl.ds(0, 4)], ring_sem.at[p, i, block])
            if i in (1, 2, 4, 5) or (i, block) in ((3, 0), (6, 1)):
                ring(i, block, i < 4, follow_of[i])

        for name in order.split():
            kind, i, piece = name[0], int(name[1]), int(name[2])
            if kind == "T":
                thin_task()
            elif kind == "t":
                thin_far_task()
            elif kind == "W":
                wide_task(i, piece)
            elif kind == "P":
                wide_plane_task(i, piece)
            elif kind == "F":
                wide_far_task(i, piece)
            else:
                ring_task(i, piece)
        for cls, count in ((0, 64), (1, 48)):
            @pl.when(n == cls)
            def _(count=count):
                drain(wide_buf.at[pl.ds(0, count)], plane_sem.at[p, 0])

    def last_thin(p, thin_buf):
        for block in range(2):
            drain(thin_buf.at[pl.ds(0, 4)], ring_sem.at[p, 7, block])

    def sort_slots():
        keys = [jnp.where(k < offs_ref[16], cols_ref[k] % 4, 4) for k in range(16)]
        ranks = []
        for k in range(16):
            rank = jnp.int32(0)
            for q in range(16):
                if q != k:
                    ahead = keys[q] <= keys[k] if q < k else keys[q] < keys[k]
                    rank = rank + jnp.where(ahead, 1, 0)
            ranks.append(rank)
        for place in range(16):
            slot = jnp.int32(0)
            for k in range(16):
                slot = slot + jnp.where(ranks[k] == place, k, 0)
            sorted_ref[place] = slot
        for t in range(4):
            below = jnp.int32(0)
            for k in range(16):
                below = below + jnp.where(keys[k] <= t, 1, 0)
            ends_ref[t] = below

    def products(thin_buf, wide_buf, j):
        rows = part(j)
        size = BOUNDS[j + 1] - BOUNDS[j]
        total = jnp.zeros((size, T), jnp.float32)
        sums[0, :size, :] = total
        for k in range(16):
            slot = sorted_ref[k] % 16
            row = rows_ref[slot]
            index = ((row // 16) % 16) * 4 + row % 4
            tile = thin_buf[index] if j == 0 else wide_buf[index, wide_part(j), :]
            total = total + jnp.dot(tile, tiles[slot], preferred_element_type=jnp.float32)
            sums[k + 1, :size, :] = total
        for t in range(4):
            upto = sums[ends_ref[t] % 17, :size, :]
            if t > 0:
                upto = upto - sums[ends_ref[t - 1] % 17, :size, :]
            acc[t, rows, :] = upto

    def swap_cores(p, j):
        rows = part(j)
        for g in range(2):
            send(
                acc.at[g * 2 + 1 - c, rows], core_in.at[p, g, rows],
                ex_send.at[p, j], ex_recv.at[p, j], sibling,
            )

    def await_cores(p, j):
        drain(core_in.at[p, pl.ds(0, 2), part(j)], ex_recv.at[p, j])

    for j in range(parts):
        hand_out(0, thin0, wide0, j, relay_two_near, own.at[2])
    load(tiles_hbm, tiles, load_sem.at[0])
    load(feat_hbm, feat, load_sem.at[1])
    load(weight_hbm, weight, load_sem.at[2])
    for i, ref in enumerate((rows_ref, cols_ref, offs_ref)):
        drain(ref, small_sem.at[i])
    sort_slots()
    gather(0, thin0, wide0, FIRST_ORDER)
    drain(tiles, load_sem.at[0])

    def pass_on(j):
        rows = part(j)
        await_cores(0, j)
        chip_out[rows, :] = (acc[other_tile, rows, :] + core_in[0, 1 - hx, rows, :]).astype(jnp.bfloat16)
        send(chip_out.at[rows], chip_in.at[rows], chip_send.at[j], chip_recv.at[j], x_near)

    def close_first(j):
        rows = part(j)
        drain(chip_in.at[rows], chip_recv.at[j])
        own[1, rows, :] = (
            acc[own_tile, rows, :] + core_in[0, hx, rows, :] + chip_in[rows, :].astype(jnp.float32)
        ).astype(jnp.bfloat16)

    for j in range(1, parts):
        products(thin0, wide0, j)
        swap_cores(0, j)
    for j in range(1, parts):
        pass_on(j)
    last_thin(0, thin0)
    products(thin0, wide0, 0)
    swap_cores(0, 0)
    close_first(1)
    hand_out(1, thin1, wide1, 1, relay_two, own.at[1])
    pass_on(0)
    for j in range(2, parts):
        close_first(j)
        hand_out(1, thin1, wide1, j, relay_two, own.at[1])
    close_first(0)
    hand_out(1, thin1, wide1, 0, relay_two, own.at[1])

    gather(1, thin1, wide1, SECOND_ORDER)
    for j in range(parts):
        drain(core_in.at[0, pl.ds(0, 2), part(j)], ex_send.at[0, j])

    tv = jnp.full((1, T), heat_ref[0], jnp.float32)
    total = 1.0 + tv + tv * tv / 2.0
    coef0 = 1.0 / total
    coef1 = tv / total
    coef2 = (tv * tv / 2.0) / total

    def pair_up(j):
        rows = part(j)
        await_cores(1, j)
        mine = coef2 * (acc[own_tile, rows, :] + core_in[1, hx, rows, :])
        mine += coef0 * own[0, rows, :].astype(jnp.float32) + coef1 * own[1, rows, :].astype(jnp.float32)
        acc[own_tile, rows, :] = mine
        pair_out[0, rows, :] = mine.astype(jnp.bfloat16)
        theirs = coef2 * (acc[other_tile, rows, :] + core_in[1, 1 - hx, rows, :])
        acc[other_tile, rows, :] = theirs
        pair_out[1, rows, :] = theirs.astype(jnp.bfloat16)
        for i in range(2):
            send(pair_out.at[i, rows], pair_in.at[1 - i, rows], pair_send.at[j], pair_recv.at[j], x_near)

    def close_second(j):
        rows = part(j)
        drain(pair_in.at[pl.ds(0, 2), rows], pair_recv.at[j])
        for i, tile in enumerate((own_tile, other_tile)):
            comb[tile, rows, :] = (acc[tile, rows, :] + pair_in[i, rows, :].astype(jnp.float32)).astype(
                jnp.bfloat16
            )
            send(comb.at[tile, rows], comb.at[tile, rows], cb_send, cb_recv, sibling)

    for j in range(1, parts):
        products(thin1, wide1, j)
        swap_cores(1, j)
    for j in range(1, parts):
        pair_up(j)
    last_thin(1, thin1)
    products(thin1, wide1, 0)
    swap_cores(1, 0)
    pair_up(0)
    for j in range(1, parts):
        close_second(j)
    close_second(0)
    drain(feat, load_sem.at[1])
    drain(weight, load_sem.at[2])
    drain(comb.at[pl.ds(0, 2)], cb_recv)

    partial = jnp.zeros((192, T), jnp.float32)
    for t in range(4):
        partial += lax.dot_general(
            feat[:, t * T : (t + 1) * T], comb[t], (((1,), (1,)), ((), ())),
            preferred_element_type=jnp.float32,
        )
    partial = partial * (1.0 / 256.0)
    for i in range(8):
        piece = partial[i * PIECE : (i + 1) * PIECE]
        gwp[i] = jnp.concatenate([piece[:, :128], piece[:, 128:]], axis=0).astype(jnp.bfloat16)

    for step in PLANE_STEPS:
        place, device = plane_peer(step)
        send(gwp.at[place], g1.at[here], gw_send.at[0], gw_recv.at[0], device)
    g1[here] = gwp[here]

    for t in range(4):
        gf_ref[:, t * T : (t + 1) * T] = jnp.dot(
            weight[...], comb[t], preferred_element_type=jnp.float32
        ).astype(jnp.bfloat16)

    drain(g1.at[pl.ds(0, 7)], gw_recv.at[0])
    s1[...] = functools.reduce(lambda a, b: a + b, [g1[i].astype(jnp.float32) for i in range(8)]).astype(
        jnp.bfloat16
    )
    for step in Z_STEPS:
        send(s1, g2.at[z], gw_send.at[1], gw_recv.at[1], z_peer(step)[1])
    g2[z] = s1[...]
    drain(g2.at[pl.ds(0, 7)], gw_recv.at[1])
    s2[...] = functools.reduce(lambda a, b: a + b, [g2[i].astype(jnp.float32) for i in range(8)])
    for step in PLANE_STEPS:
        send(s2, gfin.at[here], gw_send.at[2], gw_recv.at[2], plane_peer(step)[1])
    gfin[here] = s2[...]

    for p, (thin_buf, wide_buf) in enumerate(((thin0, wide0), (thin1, wide1))):
        @pl.when(one_is_self == 0)
        def _(p=p):
            drain(own.at[p], self_sem.at[p])

        drain(own.at[p], send_sem.at[p, 0])
        drain(wide_buf.at[pl.ds(0, 14)], send_sem.at[p, 1])
        drain(thin_buf.at[pl.ds(0, 8)], send_sem.at[p, 2])
        drain(wide_buf.at[pl.ds(0, 64)], send_sem.at[p, 3])
        drain(thin_buf.at[pl.ds(0, 56)], send_sem.at[p, 4])
    for j in range(parts):
        drain(core_in.at[1, pl.ds(0, 2), part(j)], ex_send.at[1, j])
        drain(chip_in.at[part(j)], chip_send.at[j])
        drain(pair_in.at[pl.ds(0, 2), part(j)], pair_send.at[j])
    drain(comb.at[pl.ds(0, 2)], cb_send)

    drain(gfin.at[pl.ds(0, 7)], gw_recv.at[2])
    for i in range(8):
        gw_ref[i * PIECE : (i + 1) * PIECE, :128] = gfin[i, :PIECE, :]
        gw_ref[i * PIECE : (i + 1) * PIECE, 128:] = gfin[i, PIECE:, :]
    for i, ref in enumerate((g1, g2, gfin)):
        drain(ref.at[pl.ds(0, 7)], gw_send.at[i])


def hand_back(gw_in, gf_in, gw_out, gf_out):
    gw_out[...] = gw_in[...]
    gf_out[...] = gf_in[...]


def local(cotangent, features, weight, heat_time, tile_values, tile_row, tile_col, section_offsets):
    vmem = pl.BlockSpec(memory_space=pltpu.VMEM)
    hbm = pl.BlockSpec(memory_space=pltpu.HBM)
    f32, bf16, i32 = jnp.float32, jnp.bfloat16, jnp.int32
    dma = pltpu.SemaphoreType.DMA
    parts = len(BOUNDS) - 1
    grad_weight, grad_features = pl.pallas_call(
        kernel,
        out_shape=(
            jax.ShapeDtypeStruct((192, T), f32),
            jax.ShapeDtypeStruct((192, 1024), bf16),
        ),
        in_specs=[hbm, hbm, hbm, pl.BlockSpec(memory_space=pltpu.SMEM), hbm, hbm, hbm, hbm],
        out_specs=(vmem, vmem),
        scratch_shapes=[
            pltpu.SMEM((16,), i32), pltpu.SMEM((16,), i32), pltpu.SMEM((17,), i32),
            pltpu.SMEM((16,), i32), pltpu.SMEM((4,), i32),
            pltpu.VMEM((17, max(b - a for a, b in zip(BOUNDS, BOUNDS[1:])), T), f32),
            pltpu.VMEM((2, T, T), bf16),
            pltpu.VMEM((192, 1024), bf16),
            pltpu.VMEM((192, T), bf16),
            pltpu.VMEM((16, T, T), bf16),
            pltpu.VMEM((RELAY + 16, T - THIN, T), bf16),
            pltpu.VMEM((RELAY + 16, THIN, T), bf16),
            pltpu.VMEM((RELAY + 16, T - THIN, T), bf16),
            pltpu.VMEM((RELAY + 16, THIN, T), bf16),
            pltpu.VMEM((3, T, T), bf16),
            pltpu.VMEM((4, T, T), f32),
            pltpu.VMEM((2, 2, T, T), f32),
            pltpu.VMEM((T, T), bf16),
            pltpu.VMEM((T, T), bf16),
            pltpu.VMEM((2, T, T), bf16),
            pltpu.VMEM((2, T, T), bf16),
            pltpu.VMEM((4, T, T), bf16),
            pltpu.VMEM((8, 2 * PIECE, 128), bf16),
            pltpu.VMEM((8, 2 * PIECE, 128), bf16),
            pltpu.VMEM((2 * PIECE, 128), bf16),
            pltpu.VMEM((8, 2 * PIECE, 128), bf16),
            pltpu.VMEM((2 * PIECE, 128), f32),
            pltpu.VMEM((8, 2 * PIECE, 128), f32),
            dma((3,)), dma((3,)), dma((2,)),
            dma((2,)),
            dma((2, 8, 2)),
            dma((2, 2)),
            dma((2, 17)),
            dma((2, 8, 2)),
            dma((2, 5)),
            dma((2,)),
            dma((2, parts)), dma((2, parts)),
            dma((parts,)), dma((parts,)),
            dma((parts,)), dma((parts,)),
            dma, dma,
            dma((3,)), dma((3,)),
        ],
        compiler_params=pltpu.CompilerParams(
            collective_id=0, has_side_effects=True, vmem_limit_bytes=60 << 20
        ),
        cost_estimate=pl.CostEstimate(flops=4_800_000_000, bytes_accessed=4_000_000, transcendentals=0),
        name="diffuse",
    )(tile_row, tile_col, section_offsets, heat_time, cotangent, features.T, weight, tile_values)
    grad_weight, grad_features = pl.pallas_call(
        hand_back,
        out_shape=(
            jax.ShapeDtypeStruct((192, T), f32),
            jax.ShapeDtypeStruct((192, 1024), bf16),
        ),
        in_specs=[vmem, vmem],
        out_specs=(vmem, vmem),
        name="hand_back",
    )(grad_weight, grad_features)
    return grad_weight, grad_features.T


def solution(mesh):
    in_specs = (
        P("blk", None),
        P("blk", "rep"),
        P("rep", None),
        P(),
        P(("blk", "rep"), None, None),
        P(("blk", "rep")),
        P(("blk", "rep")),
        P(("blk", "rep")),
    )
    out_specs = (P("rep", None), P("blk", "rep"))
    return jax.shard_map(local, mesh=mesh, in_specs=in_specs, out_specs=out_specs, check_vma=False)
```

```python
import functools

import jax
import jax.numpy as jnp
from jax import lax
from jax.experimental import pallas as pl
from jax.experimental.pallas import tpu as pltpu
from jax.sharding import PartitionSpec as P

MESH = pl.DeviceIdType.MESH
T = 256
THIN = 80
BOUNDS = (0, 80, 192, 256)
RELAY = 64
PLANE_STEPS = (3, 5, 1, 7, 4, 2, 6)
Z_STEPS = (4, 3, 5, 2, 6, 1, 7)
PIECE = 24

FIRST_ORDER = " ".join((
    "T00 W01 P01 W00",
    "P00 t00 W41 F01",
    "W11 W10 W40 P41",
    "P10 P11 P40 F00",
    "R00 F41 F40 W20",
    "W50 W51 P51 F11",
    "P50 W21 F10 P20",
    "P21 R41 R10 W30",
    "P30 W61 F21 P61",
    "W60 R40 F20 F51",
    "P60 F50 W31 R11",
    "P31 W71 P71 R20",
    "F30 F61 R51 R50",
    "W70 F60 P70 F31",
    "R21 F71 F70 R60",
    "R61 R30 R31",
))
SECOND_ORDER = " ".join((
    "W01 W00 P01 T00",
    "W11 W41 P41 W40",
    "W10 P10 F01 P00",
    "W51 W21 t00 F10",
    "P21 P40 W50 W20",
    "R00 F41 F00 P20",
    "P51 F21 F40 W30",
    "W61 P30 W60 P60",
    "W31 R10 R41 F20",
    "R40 R11 F51 P61",
    "P11 F30 P31 W70",
    "F60 F61 P70 R51",
    "F11 P50 W71 R21",
    "R50 P71 R20 F31",
    "F70 F50 F71 R31",
    "R60 R61 R30",
))


def xor(a, b):
    return a + b - 2 * a * b


def kernel(
    rows_hbm, cols_hbm, offs_hbm, heat_ref, cot_hbm, feat_hbm, weight_hbm, tiles_hbm,
    gw_ref, gf_ref,
    rows_ref, cols_ref, offs_ref, sorted_ref, ends_ref, sums, cot, feat, weight, tiles,
    wide0, thin0, wide1, thin1, own, acc, core_in, chip_out, chip_in, pair_out, pair_in, comb,
    gwp, g1, s1, g2, s2, gfin,
    load_sem, small_sem, cot_sem,
    rt_sem, relay_sem, thin_sem, plane_sem, ring_sem, send_sem, self_sem,
    ex_send, ex_recv, chip_send, chip_recv, pair_send, pair_recv, cb_send, cb_recv, gw_send, gw_recv,
):
    blk = lax.axis_index("blk")
    rep = lax.axis_index("rep")
    z = blk // 8
    y = (blk // 2) % 4
    xh = blk % 2
    xl = rep // 2
    c = rep % 2
    n = xor(c, xh)
    hx = xor(xl, xh)
    own_tile = hx * 2 + c
    other_tile = (1 - hx) * 2 + c

    def dev(xh_, xl_, y_, z_, c_):
        return (z_ * 8 + y_ * 2 + xh_, xl_ * 2 + c_)

    def delta2(xh_, xl_):
        return (1 - xh_) * (3 - xl_) + xh_ * xl_

    relay_one = dev(xh, xl, (y + 1 - xl) % 4, z, 0)
    relay_two = dev(1 - xh, xl, (y + delta2(xh, xl)) % 4, z, 1)
    relay_two_near = dev(1 - xh, 1 - xl, (y + delta2(xh, 1 - xl)) % 4, z, 1)
    one_is_self = xl * (1 - c)

    yr = ((1 - c) * (y - 1 + xl) + c * (y - delta2(1 - xh, xl)) + 4) % 4
    hr = xor(xl, n)
    ey = 2 * hx - 1
    yc = ((1 - c) * (y - ey - 1 + xl) + c * (y - ey - delta2(1 - xh, xl)) + 8) % 4

    z_up = dev(xh, xl, y, (z + 1) % 8, c)
    z_dn = dev(xh, xl, y, (z + 7) % 8, c)
    y_chain = dev(xh, xl, (y + ey + 4) % 4, z, c)
    y_other = dev(xh, xl, (y - ey + 4) % 4, z, c)
    x_near = dev(xh, 1 - xl, y, z, c)
    x_far = dev(1 - xh, 1 - xl, y, z, 1 - c)
    sibling = dev(xh, xl, y, z, 1 - c)
    here = y * 2 + xh

    def plane_peer(step):
        place = (here + step) % 8
        return place, dev(place % 2, xl, place // 2, z, c)

    def z_peer(step):
        zt = (z + step) % 8
        return zt, dev(xh, xl, y, zt, c)

    def load(src, dst, sem):
        pltpu.make_async_copy(src, dst, sem).start()

    for i, tile in enumerate((own_tile, other_tile)):
        load(cot_hbm.at[pl.ds(pl.multiple_of(tile * T, T), T)], cot.at[i], cot_sem.at[i])
    load(rows_hbm, rows_ref, small_sem.at[0])
    load(cols_hbm, cols_ref, small_sem.at[1])
    load(offs_hbm, offs_ref, small_sem.at[2])

    barrier = pltpu.get_barrier_semaphore()

    def greet(device):
        pl.semaphore_signal(barrier, inc=1, device_id=device, device_id_type=MESH)

    @pl.when(c == 0)
    def _():
        @pl.when(one_is_self == 0)
        def _():
            greet(dev(xh, xl, yr, z, 0))

        greet(dev(xh, xl, yr, z, 1))

    @pl.when(c == 1)
    def _():
        for core in range(2):
            greet(dev(1 - xh, xl, yr, z, core))
            greet(dev(1 - xh, 1 - xl, yr, z, core))

    for device in (y_chain, y_other, x_near, x_far, sibling):
        greet(device)
    greet(z_up)
    greet(z_dn)

    def send(src, dst, ssem, rsem, device):
        pltpu.make_async_remote_copy(
            src_ref=src, dst_ref=dst, send_sem=ssem, recv_sem=rsem, device_id=device, device_id_type=MESH
        ).start()

    def drain(ref, sem):
        pltpu.make_async_copy(ref, ref, sem).wait()

    def turned(ref):
        return ref[...].astype(jnp.float32).T.astype(jnp.bfloat16)

    drain(cot.at[0], cot_sem.at[0])
    own[0] = turned(cot.at[0])
    drain(cot.at[1], cot_sem.at[1])
    own[2] = turned(cot.at[1])

    pl.semaphore_wait(barrier, 10 - one_is_self)

    parts = len(BOUNDS) - 1

    def part(j):
        return pl.ds(BOUNDS[j], BOUNDS[j + 1] - BOUNDS[j])

    def wide_part(j):
        return pl.ds(BOUNDS[j] - THIN, BOUNDS[j + 1] - BOUNDS[j])

    follow_of = {1: 2, 2: 3, 3: 7, 4: 5, 5: 6, 6: 7}

    def zp(i):
        return (z + (0, 7, 6, 5, 1, 2, 3, 4)[i]) % 8

    def spot(i, ysrc):
        return (zp(i) * 2 + ysrc // 2) * 4 + hr * 2

    def hand_out(p, thin_buf, wide_buf, j, to_two, two):
        mine = own.at[p, part(j)]
        slot = RELAY + z * 2 + c
        if j == 0:
            place, sem = thin_buf.at[slot], rt_sem.at[p]
        else:
            place, sem = wide_buf.at[slot, wide_part(j)], relay_sem.at[p, 0, c]

        @pl.when(one_is_self == 1)
        def _():
            load(mine, place, sem)

        @pl.when(one_is_self == 0)
        def _():
            send(mine, place, self_sem.at[p], sem, relay_one)

        send(two.at[part(j)], place, send_sem.at[p, 0], sem, to_two)

    def gather(p, thin_buf, wide_buf, order):
        def over_plane(buf, i, tile, count, ssem, chain_sem, rest):
            src = buf.at[pl.ds(RELAY + zp(i) * 2 + tile, count)]
            dst = buf.at[pl.ds(spot(i, yr) + tile, count)]
            send(src, dst, ssem, chain_sem, y_chain)
            send(src, dst, ssem, rest, y_other)
            send(src, dst, ssem, rest, x_near)

            @pl.when(n == 0)
            def _():
                send(src, dst, ssem, rest, x_far)

        def far(buf, i, tile, count, ssem, chain_sem, rest):
            @pl.when(n == 1)
            def _():
                drain(buf.at[pl.ds(0, count)], chain_sem)
                place = buf.at[pl.ds(spot(i, yc) + tile, count)]
                send(place, place, ssem, rest, x_far)

        def along_z(i, tile, up, follow):
            place = wide_buf.at[RELAY + zp(i) * 2 + tile]
            send(place, place, send_sem.at[p, 1], relay_sem.at[p, follow, tile], z_up if up else z_dn)

        def ring(i, block, up, follow):
            place = thin_buf.at[pl.ds(zp(i) * 8 + block * 4, 4)]
            send(place, place, send_sem.at[p, 4], ring_sem.at[p, follow, block], z_up if up else z_dn)

        def thin_task():
            drain(thin_buf.at[pl.ds(0, 2)], rt_sem.at[p])
            over_plane(thin_buf, 0, 0, 2, send_sem.at[p, 2], thin_sem.at[p, n], thin_sem.at[p, 0])

        def thin_far_task():
            far(thin_buf, 0, 0, 2, send_sem.at[p, 2], thin_sem.at[p, 1], thin_sem.at[p, 0])

        def wide_task(i, tile):
            drain(wide_buf.at[0], relay_sem.at[p, i, tile])
            if i == 0:
                along_z(0, tile, True, 1)
                along_z(0, tile, False, 4)
            elif i in (1, 2, 4, 5) or (i, tile) in ((3, 0), (6, 1)):
                along_z(i, tile, i < 4, follow_of[i])

        def wide_plane_task(i, tile):
            over_plane(
                wide_buf, i, tile, 1, send_sem.at[p, 3],
                plane_sem.at[p, n * (1 + i * 2 + tile)], plane_sem.at[p, 0],
            )

        def wide_far_task(i, tile):
            far(wide_buf, i, tile, 1, send_sem.at[p, 3], plane_sem.at[p, 1 + i * 2 + tile], plane_sem.at[p, 0])

        def ring_task(i, block):
            if i == 0:
                for cls, count in ((0, 8), (1, 6)):
                    @pl.when(n == cls)
                    def _(count=count):
                        drain(thin_buf.at[pl.ds(0, count)], thin_sem.at[p, 0])

                for b in range(2):
                    ring(0, b, True, 1)
                    ring(0, b, False, 4)
                return
            drain(thin_buf.at[pl.ds(0, 4)], ring_sem.at[p, i, block])
            if i in (1, 2, 4, 5) or (i, block) in ((3, 0), (6, 1)):
                ring(i, block, i < 4, follow_of[i])

        for name in order.split():
            kind, i, piece = name[0], int(name[1]), int(name[2])
            if kind == "T":
                thin_task()
            elif kind == "t":
                thin_far_task()
            elif kind == "W":
                wide_task(i, piece)
            elif kind == "P":
                wide_plane_task(i, piece)
            elif kind == "F":
                wide_far_task(i, piece)
            else:
                ring_task(i, piece)
        for cls, count in ((0, 64), (1, 48)):
            @pl.when(n == cls)
            def _(count=count):
                drain(wide_buf.at[pl.ds(0, count)], plane_sem.at[p, 0])

    def last_thin(p, thin_buf):
        for block in range(2):
            drain(thin_buf.at[pl.ds(0, 4)], ring_sem.at[p, 7, block])

    def sort_slots():
        keys = [jnp.where(k < offs_ref[16], cols_ref[k] % 4, 4) for k in range(16)]
        ranks = []
        for k in range(16):
            rank = jnp.int32(0)
            for q in range(16):
                if q != k:
                    ahead = keys[q] <= keys[k] if q < k else keys[q] < keys[k]
                    rank = rank + jnp.where(ahead, 1, 0)
            ranks.append(rank)
        for place in range(16):
            slot = jnp.int32(0)
            for k in range(16):
                slot = slot + jnp.where(ranks[k] == place, k, 0)
            sorted_ref[place] = slot
        for t in range(4):
            below = jnp.int32(0)
            for k in range(16):
                below = below + jnp.where(keys[k] <= t, 1, 0)
            ends_ref[t] = below

    def products(thin_buf, wide_buf, j):
        rows = part(j)
        size = BOUNDS[j + 1] - BOUNDS[j]
        total = jnp.zeros((size, T), jnp.float32)
        sums[0, :size, :] = total
        for k in range(16):
            slot = sorted_ref[k] % 16
            row = rows_ref[slot]
            index = ((row // 16) % 16) * 4 + row % 4
            tile = thin_buf[index] if j == 0 else wide_buf[index, wide_part(j), :]
            total = total + jnp.dot(tile, tiles[slot], preferred_element_type=jnp.float32)
            sums[k + 1, :size, :] = total
        for t in range(4):
            upto = sums[ends_ref[t] % 17, :size, :]
            if t > 0:
                upto = upto - sums[ends_ref[t - 1] % 17, :size, :]
            acc[t, rows, :] = upto

    def swap_cores(p, j):
        rows = part(j)
        for g in range(2):
            send(
                acc.at[g * 2 + 1 - c, rows], core_in.at[p, g, rows],
                ex_send.at[p, j], ex_recv.at[p, j], sibling,
            )

    def await_cores(p, j):
        drain(core_in.at[p, pl.ds(0, 2), part(j)], ex_recv.at[p, j])

    for j in range(parts):
        hand_out(0, thin0, wide0, j, relay_two_near, own.at[2])
    load(tiles_hbm, tiles, load_sem.at[0])
    load(feat_hbm, feat, load_sem.at[1])
    load(weight_hbm, weight, load_sem.at[2])
    for i, ref in enumerate((rows_ref, cols_ref, offs_ref)):
        drain(ref, small_sem.at[i])
    sort_slots()
    gather(0, thin0, wide0, FIRST_ORDER)
    drain(tiles, load_sem.at[0])

    def pass_on(j):
        rows = part(j)
        await_cores(0, j)
        chip_out[rows, :] = (acc[other_tile, rows, :] + core_in[0, 1 - hx, rows, :]).astype(jnp.bfloat16)
        send(chip_out.at[rows], chip_in.at[rows], chip_send.at[j], chip_recv.at[j], x_near)

    def close_first(j):
        rows = part(j)
        drain(chip_in.at[rows], chip_recv.at[j])
        own[1, rows, :] = (
            acc[own_tile, rows, :] + core_in[0, hx, rows, :] + chip_in[rows, :].astype(jnp.float32)
        ).astype(jnp.bfloat16)

    for j in range(1, parts):
        products(thin0, wide0, j)
        swap_cores(0, j)
    for j in range(1, parts):
        pass_on(j)
    last_thin(0, thin0)
    products(thin0, wide0, 0)
    swap_cores(0, 0)
    close_first(1)
    hand_out(1, thin1, wide1, 1, relay_two, own.at[1])
    pass_on(0)
    for j in range(2, parts):
        close_first(j)
        hand_out(1, thin1, wide1, j, relay_two, own.at[1])
    close_first(0)
    hand_out(1, thin1, wide1, 0, relay_two, own.at[1])

    gather(1, thin1, wide1, SECOND_ORDER)
    for j in range(parts):
        drain(core_in.at[0, pl.ds(0, 2), part(j)], ex_send.at[0, j])

    tv = jnp.full((1, T), heat_ref[0], jnp.float32)
    total = 1.0 + tv + tv * tv / 2.0
    coef0 = 1.0 / total
    coef1 = tv / total
    coef2 = (tv * tv / 2.0) / total

    def pair_up(j):
        rows = part(j)
        await_cores(1, j)
        mine = coef2 * (acc[own_tile, rows, :] + core_in[1, hx, rows, :])
        mine += coef0 * own[0, rows, :].astype(jnp.float32) + coef1 * own[1, rows, :].astype(jnp.float32)
        acc[own_tile, rows, :] = mine
        pair_out[0, rows, :] = mine.astype(jnp.bfloat16)
        theirs = coef2 * (acc[other_tile, rows, :] + core_in[1, 1 - hx, rows, :])
        acc[other_tile, rows, :] = theirs
        pair_out[1, rows, :] = theirs.astype(jnp.bfloat16)
        for i in range(2):
            send(pair_out.at[i, rows], pair_in.at[1 - i, rows], pair_send.at[j], pair_recv.at[j], x_near)

    def close_second(j):
        rows = part(j)
        drain(pair_in.at[pl.ds(0, 2), rows], pair_recv.at[j])
        for i, tile in enumerate((own_tile, other_tile)):
            comb[tile, rows, :] = (acc[tile, rows, :] + pair_in[i, rows, :].astype(jnp.float32)).astype(
                jnp.bfloat16
            )
            send(comb.at[tile, rows], comb.at[tile, rows], cb_send, cb_recv, sibling)

    for j in range(1, parts):
        products(thin1, wide1, j)
        swap_cores(1, j)
    for j in range(1, parts):
        pair_up(j)
    last_thin(1, thin1)
    products(thin1, wide1, 0)
    swap_cores(1, 0)
    pair_up(0)
    for j in range(1, parts):
        close_second(j)
    close_second(0)
    drain(feat, load_sem.at[1])
    drain(weight, load_sem.at[2])
    drain(comb.at[pl.ds(0, 2)], cb_recv)

    partial = jnp.zeros((192, T), jnp.float32)
    for t in range(4):
        partial += lax.dot_general(
            feat[:, t * T : (t + 1) * T], comb[t], (((1,), (1,)), ((), ())),
            preferred_element_type=jnp.float32,
        )
    partial = partial * (1.0 / 256.0)
    for i in range(8):
        piece = partial[i * PIECE : (i + 1) * PIECE]
        gwp[i] = jnp.concatenate([piece[:, :128], piece[:, 128:]], axis=0).astype(jnp.bfloat16)

    for step in PLANE_STEPS:
        place, device = plane_peer(step)
        send(gwp.at[place], g1.at[here], gw_send.at[0], gw_recv.at[0], device)
    g1[here] = gwp[here]

    for t in range(4):
        gf_ref[:, t * T : (t + 1) * T] = jnp.dot(
            weight[...], comb[t], preferred_element_type=jnp.float32
        ).astype(jnp.bfloat16)

    drain(g1.at[pl.ds(0, 7)], gw_recv.at[0])
    s1[...] = functools.reduce(lambda a, b: a + b, [g1[i].astype(jnp.float32) for i in range(8)]).astype(
        jnp.bfloat16
    )
    for step in Z_STEPS:
        send(s1, g2.at[z], gw_send.at[1], gw_recv.at[1], z_peer(step)[1])
    g2[z] = s1[...]
    drain(g2.at[pl.ds(0, 7)], gw_recv.at[1])
    s2[...] = functools.reduce(lambda a, b: a + b, [g2[i].astype(jnp.float32) for i in range(8)])
    for step in PLANE_STEPS:
        send(s2, gfin.at[here], gw_send.at[2], gw_recv.at[2], plane_peer(step)[1])
    gfin[here] = s2[...]

    for p, (thin_buf, wide_buf) in enumerate(((thin0, wide0), (thin1, wide1))):
        @pl.when(one_is_self == 0)
        def _(p=p):
            drain(own.at[p], self_sem.at[p])

        drain(own.at[p], send_sem.at[p, 0])
        drain(wide_buf.at[pl.ds(0, 14)], send_sem.at[p, 1])
        drain(thin_buf.at[pl.ds(0, 8)], send_sem.at[p, 2])
        drain(wide_buf.at[pl.ds(0, 64)], send_sem.at[p, 3])
        drain(thin_buf.at[pl.ds(0, 56)], send_sem.at[p, 4])
    for j in range(parts):
        drain(core_in.at[1, pl.ds(0, 2), part(j)], ex_send.at[1, j])
        drain(chip_in.at[part(j)], chip_send.at[j])
        drain(pair_in.at[pl.ds(0, 2), part(j)], pair_send.at[j])
    drain(comb.at[pl.ds(0, 2)], cb_send)

    drain(gfin.at[pl.ds(0, 7)], gw_recv.at[2])
    for i in range(8):
        gw_ref[i * PIECE : (i + 1) * PIECE, :128] = gfin[i, :PIECE, :]
        gw_ref[i * PIECE : (i + 1) * PIECE, 128:] = gfin[i, PIECE:, :]
    for i, ref in enumerate((g1, g2, gfin)):
        drain(ref.at[pl.ds(0, 7)], gw_send.at[i])


def hand_back(gw_in, gf_in, gw_out, gf_out):
    gw_out[...] = gw_in[...]
    gf_out[...] = gf_in[...]


def local(cotangent, features, weight, heat_time, tile_values, tile_row, tile_col, section_offsets):
    vmem = pl.BlockSpec(memory_space=pltpu.VMEM)
    hbm = pl.BlockSpec(memory_space=pltpu.HBM)
    f32, bf16, i32 = jnp.float32, jnp.bfloat16, jnp.int32
    dma = pltpu.SemaphoreType.DMA
    parts = len(BOUNDS) - 1
    grad_weight, grad_features = pl.pallas_call(
        kernel,
        out_shape=(
            jax.ShapeDtypeStruct((192, T), f32),
            jax.ShapeDtypeStruct((192, 1024), bf16),
        ),
        in_specs=[hbm, hbm, hbm, pl.BlockSpec(memory_space=pltpu.SMEM), hbm, hbm, hbm, hbm],
        out_specs=(vmem, vmem),
        scratch_shapes=[
            pltpu.SMEM((16,), i32), pltpu.SMEM((16,), i32), pltpu.SMEM((17,), i32),
            pltpu.SMEM((16,), i32), pltpu.SMEM((4,), i32),
            pltpu.VMEM((17, max(b - a for a, b in zip(BOUNDS, BOUNDS[1:])), T), f32),
            pltpu.VMEM((2, T, T), bf16),
            pltpu.VMEM((192, 1024), bf16),
            pltpu.VMEM((192, T), bf16),
            pltpu.VMEM((16, T, T), bf16),
            pltpu.VMEM((RELAY + 16, T - THIN, T), bf16),
            pltpu.VMEM((RELAY + 16, THIN, T), bf16),
            pltpu.VMEM((RELAY + 16, T - THIN, T), bf16),
            pltpu.VMEM((RELAY + 16, THIN, T), bf16),
            pltpu.VMEM((3, T, T), bf16),
            pltpu.VMEM((4, T, T), f32),
            pltpu.VMEM((2, 2, T, T), f32),
            pltpu.VMEM((T, T), bf16),
            pltpu.VMEM((T, T), bf16),
            pltpu.VMEM((2, T, T), bf16),
            pltpu.VMEM((2, T, T), bf16),
            pltpu.VMEM((4, T, T), bf16),
            pltpu.VMEM((8, 2 * PIECE, 128), bf16),
            pltpu.VMEM((8, 2 * PIECE, 128), bf16),
            pltpu.VMEM((2 * PIECE, 128), bf16),
            pltpu.VMEM((8, 2 * PIECE, 128), bf16),
            pltpu.VMEM((2 * PIECE, 128), f32),
            pltpu.VMEM((8, 2 * PIECE, 128), f32),
            dma((3,)), dma((3,)), dma((2,)),
            dma((2,)),
            dma((2, 8, 2)),
            dma((2, 2)),
            dma((2, 17)),
            dma((2, 8, 2)),
            dma((2, 5)),
            dma((2,)),
            dma((2, parts)), dma((2, parts)),
            dma((parts,)), dma((parts,)),
            dma((parts,)), dma((parts,)),
            dma, dma,
            dma((3,)), dma((3,)),
        ],
        compiler_params=pltpu.CompilerParams(
            collective_id=0, has_side_effects=True, vmem_limit_bytes=60 << 20
        ),
        cost_estimate=pl.CostEstimate(flops=4_800_000_000, bytes_accessed=4_000_000, transcendentals=0),
        name="diffuse",
    )(tile_row, tile_col, section_offsets, heat_time, cotangent, features.T, weight, tile_values)
    grad_weight, grad_features = pl.pallas_call(
        hand_back,
        out_shape=(
            jax.ShapeDtypeStruct((192, T), f32),
            jax.ShapeDtypeStruct((192, 1024), bf16),
        ),
        in_specs=[vmem, vmem],
        out_specs=(vmem, vmem),
        name="hand_back",
    )(grad_weight, grad_features)
    return grad_weight, grad_features.T


def solution(mesh):
    in_specs = (
        P("blk", None),
        P("blk", "rep"),
        P("rep", None),
        P(),
        P(("blk", "rep"), None, None),
        P(("blk", "rep")),
        P(("blk", "rep")),
        P(("blk", "rep")),
    )
    out_specs = (P("rep", None), P("blk", "rep"))
    return jax.shard_map(local, mesh=mesh, in_specs=in_specs, out_specs=out_specs, check_vma=False)
```
